32 devices in a mesh: dp: 8 (over z, x), row: 4 (over y, core).
Axes of the slice: x: 2, y: 2, z: 4, core: 2. Of those that a mesh axis runs over, the one named last changes fastest.
Arguments:
- patches: bfloat16 [2, 8, 48, 96, 384], P(None, 'dp', 'row'), may hold values from -6 to 6
- unpadded_patch_size: int32 [2, 8, 2], P(None, 'dp'), may hold values from 37 to 96, as said below
- patch_expert_index: int32 [2, 8, 48, 96, 1], P(None, 'dp', 'row'), may hold values from 0 to 15
- cotangent: bfloat16 [2, 8, 24, 48, 768], P(None, 'dp', 'row'), may hold values from -6 to 6
- query_key_value_weight: bfloat16 [384, 1152], P('dp'), may hold values from -0.3125 to 0.3125
- query_projection_bias: float32 [384], replicated, may hold values from -3 to 3
- value_projection_bias: float32 [384], replicated, may hold values from -3 to 3
- log_cosine_scale: float32 [12], replicated, may hold values from 1.6 to 3
- bias_network_first_weight: float32 [2, 512], replicated, may hold values from -4 to 4
- bias_network_first_bias: float32 [512], replicated, may hold values from -3 to 3
- bias_network_second_weight: float32 [512, 12], replicated, may hold values from -0.125 to 0.125
- output_projection_weight: bfloat16 [384, 384], P('dp'), may hold values from -0.3125 to 0.3125
- output_projection_bias: float32 [384], replicated, may hold values from -3 to 3
- attention_norm_gain: float32 [384], replicated, may hold values from 0.5 to 1.5
- attention_norm_bias: float32 [384], replicated, may hold values from -3 to 3
- routing_weight: bfloat16 [384, 16], P('dp'), may hold values from -0.15625 to 0.15625
- expert_first_weight: bfloat16 [16, 384, 1536], P('dp'), may hold values from -0.3125 to 0.3125
- expert_first_bias: float32 [16, 1536], P('dp'), may hold values from -0.625 to 0.625
- expert_second_weight: bfloat16 [16, 1536, 384], P('dp'), may hold values from -0.15625 to 0.15625
- expert_second_bias: float32 [16, 384], P('dp'), may hold values from -0.625 to 0.625
- expert_norm_gain: float32 [384], replicated, may hold values from 0.5 to 1.5
- expert_norm_bias: float32 [384], replicated, may hold values from -3 to 3
- patch_merging_weight: bfloat16 [1536, 768], P('dp'), may hold values from -0.15625 to 0.15625
- merging_norm_gain: float32 [768], replicated, may hold values from 0.5 to 1.5
- merging_norm_bias: float32 [768], replicated, may hold values from -3 to 3
Outputs:
- merged_out: bfloat16 [2, 8, 24, 48, 768], P(None, 'dp', 'row')
- patches_grad: bfloat16 [2, 8, 48, 96, 384], P(None, 'dp', 'row')
- qkv_weight_grad: float32 [384, 1152], P('dp')
- query_bias_grad: float32 [384], replicated
- value_bias_grad: float32 [384], replicated
- logit_scale_grad: float32 [12], replicated
- cpb_first_grad: float32 [2, 512], replicated
- cpb_first_bias_grad: float32 [512], replicated
- cpb_second_grad: float32 [512, 12], replicated
- proj_weight_grad: float32 [384, 384], P('dp')
- proj_bias_grad: float32 [384], replicated
- attn_gain_grad: float32 [384], replicated
- attn_shift_grad: float32 [384], replicated
- router_weight_grad: float32 [384, 16], P('dp')
- expert_in_grad: float32 [16, 384, 1536], P('dp')
- expert_in_bias_grad: float32 [16, 1536], P('dp')
- expert_out_grad: float32 [16, 1536, 384], P('dp')
- expert_out_bias_grad: float32 [16, 384], P('dp')
- moe_gain_grad: float32 [384], replicated
- moe_shift_grad: float32 [384], replicated
- merge_weight_grad: float32 [1536, 768], P('dp')
- merge_gain_grad: float32 [768], replicated
- merge_shift_grad: float32 [768], replicated
The draws below stay inside these ranges and needn't reach their ends.
Inputs may be any that keep to these rules, and one draw needn't show every extreme that they name: `unpadded_patch_size`: valid rows lie within the last 12 rows of 48, valid columns within the last 12 columns of 96; the first image of each micro-batch is whole.
All inputs are finite; a program needn't handle non-finite values.
Results may differ from the reference program's by a relative error of at most 0.028.
Values may be sent and summed in bfloat16 or wider, within the bound.
No kernel may reach another device: no remote copies, remote signals or barrier semaphores. Data moves between devices by JAX's collectives and lax.ppermute only.
A program may use at most 320 MiB of HBM per device.

```python
from functools import partial
import jax
import jax.numpy as jnp
from jax import lax

DIM = 384
HEAD_COUNT = 12
HEAD_DIM = 32
FF = 1536
BIAS_NET_UNITS = 512
WINDOW_SIDE = 12
MICRO = 2
WINX = 8
EXPERTS = 16
IMAGES = 8
HEIGHT = 48
WIDTH = 96
TOK_MB = 1152
CAP = 90
N_ROW = 4


def draw_unpadded_patch_size(key, part):
    key = jax.random.fold_in(key, 11)
    row_limit = jax.random.randint(jax.random.fold_in(key, 1), (MICRO, IMAGES), HEIGHT - WINDOW_SIDE + 1, HEIGHT + 1)
    col_limit = jax.random.randint(jax.random.fold_in(key, 2), (MICRO, IMAGES), WIDTH - WINDOW_SIDE + 1, WIDTH + 1)
    whole = (jnp.arange(IMAGES) == 0)[None, :]
    row_limit = jnp.where(whole, HEIGHT, row_limit)
    col_limit = jnp.where(whole, WIDTH, col_limit)
    return jnp.stack([row_limit, col_limit], -1).astype(jnp.int32)


def block_levels(stream_key, shape, pieces, low, top_value):
    def one(dim, parts):
        heights = jax.random.uniform(jax.random.fold_in(jax.random.fold_in(stream_key, 6), dim), (parts,), jnp.float32, low / len(pieces), top_value / len(pieces))
        return jnp.repeat(jnp.exp(heights), shape[dim] // parts).reshape((-1,) + (1,) * (len(shape) - dim - 1))

    level = one(*pieces[0])
    for cut in pieces[1:]:
        level = level * one(*cut)
    return level


def choose_distinct(key, rows, count, top, lift):
    sequence = jax.random.permutation(jax.random.fold_in(key, 1), count)
    favour = sequence
    for power in range(3):
        favour = favour * favour // count
    favour = favour * lift // count
    chance = jax.random.randint(jax.random.fold_in(key, 2), (rows, count), 0, 4096) + favour
    sure = jax.random.permutation(jax.random.fold_in(key, 3), rows)[jnp.arange(count) % rows]
    chance = jnp.where(jnp.arange(rows)[:, None] == sure[None, :], 1 << 14, chance)
    score = chance * count + jnp.arange(count)
    return lax.top_k(score.astype(jnp.int32), top)[1].astype(jnp.int32)


def normal_values(rng, dims, scale, reach, pieces=(), kind=jnp.bfloat16):
    loudness = block_levels(rng, dims, pieces, -0.22, 0.18) if pieces else 1.0
    array = jax.random.normal(rng, dims, jnp.float32) * scale * loudness
    return jnp.minimum(jnp.maximum(array, -reach), reach).astype(kind)


def setup_inputs(seed: int = 0) -> dict:
    key_list = jax.random.split(jax.random.key(seed), 26)
    return {
        "patches": normal_values(key_list[0], (MICRO, IMAGES, HEIGHT, WIDTH, DIM), 1.0, 6.0, ((1, 8), (2, 4))),
        "unpadded_patch_size": draw_unpadded_patch_size(jax.random.fold_in(key_list[25], 71), 0),
        "patch_expert_index": choose_distinct(key_list[2], MICRO * IMAGES * HEIGHT * WIDTH, EXPERTS, 1, 1024).reshape((MICRO, IMAGES, HEIGHT, WIDTH, 1)),
        "cotangent": normal_values(key_list[3], (MICRO, IMAGES, HEIGHT // 2, WIDTH // 2, 2 * DIM), 1.0, 6.0, ((1, 8), (2, 4))),
        "query_key_value_weight": normal_values(key_list[4], (DIM, 3 * DIM), DIM ** -0.5, 0.3125, ((0, 8),)),
        "query_projection_bias": normal_values(key_list[5], (DIM,), 0.5, 3.0, (), jnp.float32),
        "value_projection_bias": normal_values(key_list[6], (DIM,), 0.5, 3.0, (), jnp.float32),
        "log_cosine_scale": jnp.clip(jax.random.uniform(key_list[7], (HEAD_COUNT,), jnp.float32, 1.6, 3.0), 1.6, 3.0),
        "bias_network_first_weight": normal_values(key_list[8], (2, BIAS_NET_UNITS), 2 ** -0.5, 4.0, (), jnp.float32),
        "bias_network_first_bias": normal_values(key_list[9], (BIAS_NET_UNITS,), 0.5, 3.0, (), jnp.float32),
        "bias_network_second_weight": normal_values(key_list[10], (BIAS_NET_UNITS, HEAD_COUNT), (4 * BIAS_NET_UNITS) ** -0.5, 0.125, (), jnp.float32),
        "output_projection_weight": normal_values(key_list[11], (DIM, DIM), DIM ** -0.5, 0.3125, ((0, 8),)),
        "output_projection_bias": normal_values(key_list[12], (DIM,), 0.5, 3.0, (), jnp.float32),
        "attention_norm_gain": jnp.clip(1.0 + 0.1 * jax.random.normal(key_list[13], (DIM,), jnp.float32), 0.5, 1.5),
        "attention_norm_bias": normal_values(key_list[14], (DIM,), 0.5, 3.0, (), jnp.float32),
        "routing_weight": normal_values(key_list[15], (DIM, EXPERTS), (4 * DIM) ** -0.5, 0.15625, ((0, 8),)),
        "expert_first_weight": normal_values(key_list[16], (EXPERTS, DIM, FF), DIM ** -0.5, 0.3125, ((0, 8),)),
        "expert_first_bias": normal_values(key_list[17], (EXPERTS, FF), 0.1, 0.625, ((0, 8),), jnp.float32),
        "expert_second_weight": normal_values(key_list[18], (EXPERTS, FF, DIM), FF ** -0.5, 0.15625, ((0, 8),)),
        "expert_second_bias": normal_values(key_list[19], (EXPERTS, DIM), 0.1, 0.625, ((0, 8),), jnp.float32),
        "expert_norm_gain": jnp.clip(1.0 + 0.1 * jax.random.normal(key_list[20], (DIM,), jnp.float32), 0.5, 1.5),
        "expert_norm_bias": normal_values(key_list[21], (DIM,), 0.5, 3.0, (), jnp.float32),
        "patch_merging_weight": normal_values(key_list[22], (4 * DIM, 2 * DIM), (4 * DIM) ** -0.5, 0.15625, ((0, 8),)),
        "merging_norm_gain": jnp.clip(1.0 + 0.1 * jax.random.normal(key_list[23], (2 * DIM,), jnp.float32), 0.5, 1.5),
        "merging_norm_bias": normal_values(key_list[24], (2 * DIM,), 0.5, 3.0, (), jnp.float32),
    }


PRECISION_HIGH = lax.Precision.HIGHEST
EPS_NORM = 1e-05
EPS_UNIT = 1e-06
MASK_FILL = -100.0

@jax.custom_vjp
def low(v):
    return lax.optimization_barrier(v.astype(jnp.bfloat16)).astype(jnp.float32)

@jax.custom_vjp
def low_back(v):
    return v

def low_keep(v):
    return (low(v), None)

def low_pass(kept, grad):
    return (grad,)

def back_keep(v):
    return (v, None)

def back_low(kept, grad):
    return (low(grad),)
low.defvjp(low_keep, low_pass)
low_back.defvjp(back_keep, back_low)

def layer_norm(values, gain_vec, shift_vec):
    centred = values - lax.optimization_barrier(jnp.mean(values, -1, keepdims=True))
    spread = lax.optimization_barrier(jnp.mean(centred * centred, -1, keepdims=True))
    return centred * lax.rsqrt(spread + EPS_NORM) * gain_vec + shift_vec

def exact_error_gelu(values):
    return jax.nn.gelu(values, approximate=False)

def relative_position_bias(bias_network_first_weight, bias_network_first_bias, bias_network_second_weight):
    span_axis = (jnp.arange(2 * WINDOW_SIDE - 1, dtype=jnp.float32) - (WINDOW_SIDE - 1)) * (8.0 / (WINDOW_SIDE - 1))
    span_axis = jnp.sign(span_axis) * jnp.log2(jnp.abs(span_axis) + 1.0) / 3.0
    grid_rows = jnp.broadcast_to(span_axis[:, None], (2 * WINDOW_SIDE - 1, 2 * WINDOW_SIDE - 1))
    relative_coordinates = jnp.stack([grid_rows, grid_rows.T], -1)
    hidden_activation = exact_error_gelu(jnp.einsum('plr,rt->plt', relative_coordinates, bias_network_first_weight, precision=PRECISION_HIGH) + bias_network_first_bias)
    bias_network_table = 16.0 * jax.nn.sigmoid(jnp.einsum('qvw,wk->qvk', hidden_activation, bias_network_second_weight, precision=PRECISION_HIGH))
    offsets = jnp.arange(WINDOW_SIDE)[:, None] - jnp.arange(WINDOW_SIDE)[None, :] + (WINDOW_SIDE - 1)
    select_rows = (offsets[:, :, None] == jnp.arange(2 * WINDOW_SIDE - 1)[None, None, :]).astype(jnp.float32)
    expert_combine = jnp.einsum('fqy,uzs,ysr->rfuqz', select_rows, select_rows, bias_network_table, precision=PRECISION_HIGH)
    return expert_combine.reshape(bias_network_table.shape[-1], WINDOW_SIDE * WINDOW_SIDE, WINDOW_SIDE * WINDOW_SIDE)

def window_mask(row_start, total_rows, total_cols, valid_rows, valid_cols):
    half_win = WINDOW_SIDE // 2
    rows_at = row_start + jnp.arange(WINDOW_SIDE)
    cols_at = jnp.arange(total_cols)
    row_zone = (rows_at >= total_rows - WINDOW_SIDE).astype(jnp.int32) + (rows_at >= total_rows - half_win).astype(jnp.int32)
    col_zone = (cols_at >= total_cols - WINDOW_SIDE).astype(jnp.int32) + (cols_at >= total_cols - half_win).astype(jnp.int32)
    zone_ids = 3 * row_zone[:, None] + col_zone[None, :]
    inside = ((rows_at + half_win) % total_rows < valid_rows)[:, None] & ((cols_at + half_win) % total_cols < valid_cols)[None, :]
    win_count = total_cols // WINDOW_SIDE
    zone_ids = zone_ids.reshape(WINDOW_SIDE, win_count, WINDOW_SIDE).transpose(1, 0, 2).reshape(win_count, WINDOW_SIDE * WINDOW_SIDE)
    inside = inside.reshape(WINDOW_SIDE, win_count, WINDOW_SIDE).transpose(1, 0, 2).reshape(win_count, WINDOW_SIDE * WINDOW_SIDE)
    return jnp.where(zone_ids[:, :, None] != zone_ids[:, None, :], MASK_FILL, 0.0) + jnp.where(inside[:, None, :], 0.0, MASK_FILL)

def directions(query_raw, key_raw, log_cosine_scale):
    query_unit = query_raw * lax.rsqrt(lax.optimization_barrier(jnp.sum(query_raw * query_raw, -1, keepdims=True)) + EPS_UNIT)
    key_unit = key_raw * lax.rsqrt(lax.optimization_barrier(jnp.sum(key_raw * key_raw, -1, keepdims=True)) + EPS_UNIT)
    return (query_unit * jnp.exp(log_cosine_scale)[:, None], key_unit)

def route_tables(token_experts, experts, capacity):
    selected_expert = (token_experts[:, None] == jnp.arange(experts)[None, :]).astype(jnp.float32)
    slot_index = lax.optimization_barrier(jnp.sum(selected_expert * (jnp.cumsum(selected_expert, 0) - 1.0), -1))
    slot_hit = (slot_index[:, None] == jnp.arange(capacity)[None, :].astype(jnp.float32)).astype(jnp.float32)
    return (selected_expert, (selected_expert[:, :, None] * slot_hit[:, None, :]).reshape(token_experts.shape[0], experts * capacity))

def image_masks(valid_pair):
    stacked = jnp.stack([window_mask(WINDOW_SIDE * band, HEIGHT, WIDTH, valid_pair[0], valid_pair[1]) for band in range(N_ROW)])
    return stacked.reshape(N_ROW * WINX, WINDOW_SIDE * WINDOW_SIDE, WINDOW_SIDE * WINDOW_SIDE)

def attend(windows, window_masks, query_key_value_weight, query_projection_bias, value_projection_bias, log_cosine_scale, relative_bias_table):
    win_count = windows.shape[0]
    qkv_rows = low_back(jnp.einsum('npc,cf->npf', windows, query_key_value_weight, precision=PRECISION_HIGH))
    query_raw = (qkv_rows[..., :DIM] + query_projection_bias).reshape(win_count, WINDOW_SIDE * WINDOW_SIDE, HEAD_COUNT, HEAD_DIM)
    key_raw = qkv_rows[..., DIM:2 * DIM].reshape(win_count, WINDOW_SIDE * WINDOW_SIDE, HEAD_COUNT, HEAD_DIM)
    value_raw = (qkv_rows[..., 2 * DIM:] + value_projection_bias).reshape(win_count, WINDOW_SIDE * WINDOW_SIDE, HEAD_COUNT, HEAD_DIM)
    query_unit, key_unit = directions(query_raw, key_raw, log_cosine_scale)
    scores = low_back(jnp.einsum('nphd,nqhd->nhpq', low(query_unit), low(key_unit), precision=PRECISION_HIGH))
    scores = scores + relative_bias_table + window_masks[:, None]
    row_peak = lax.optimization_barrier(jnp.max(scores, -1, keepdims=True))
    exp_scores = jnp.exp(scores - row_peak)
    attn_probs = exp_scores / lax.optimization_barrier(jnp.sum(exp_scores, -1, keepdims=True))
    mixed = jnp.einsum('nhpq,nqhd->nphd', low(attn_probs), low(value_raw), precision=PRECISION_HIGH)
    return low_back(low(mixed)).reshape(win_count, WINDOW_SIDE * WINDOW_SIDE, DIM)

def expert_apply(operands):
    rows, weight_in, bias_in, weight_out, bias_out = operands
    hidden_pre = low_back(jnp.dot(rows, weight_in, precision=PRECISION_HIGH)) + bias_in
    hidden_low = low(exact_error_gelu(hidden_pre))
    return low_back(low(jnp.dot(hidden_low, weight_out, precision=PRECISION_HIGH) + bias_out))

def forward_block(patches, query_key_value_weight, query_projection_bias, value_projection_bias, log_cosine_scale, bias_network_first_weight, bias_network_first_bias, bias_network_second_weight, output_projection_weight, output_projection_bias, attention_norm_gain, attention_norm_bias, routing_weight, expert_first_weight, expert_first_bias, expert_second_weight, expert_second_bias, expert_norm_gain, expert_norm_bias, patch_merging_weight, merging_norm_gain, merging_norm_bias, every_window_mask, selected_expert, expert_dispatch):
    relative_bias_table = relative_position_bias(bias_network_first_weight, bias_network_first_bias, bias_network_second_weight)
    half_win = WINDOW_SIDE // 2
    shifted = jnp.roll(patches, (-half_win, -half_win), (1, 2))
    windows = shifted.reshape(IMAGES, N_ROW, WINDOW_SIDE, WINX, WINDOW_SIDE, DIM).transpose(0, 1, 3, 2, 4, 5)
    windows = windows.reshape(IMAGES, N_ROW * WINX, WINDOW_SIDE * WINDOW_SIDE, DIM)

    def per_image(pair):
        return attend(pair[0], pair[1], query_key_value_weight, query_projection_bias, value_projection_bias, log_cosine_scale, relative_bias_table)
    attn_out = lax.map(jax.checkpoint(per_image), (windows, every_window_mask))
    attn_rows = attn_out.reshape(IMAGES, N_ROW, WINX, WINDOW_SIDE, WINDOW_SIDE, DIM).transpose(0, 1, 3, 2, 4, 5)
    attn_rows = jnp.roll(attn_rows.reshape(IMAGES, HEIGHT, WIDTH, DIM), (half_win, half_win), (1, 2))
    projected = low_back(jnp.einsum('ihwc,cd->ihwd', attn_rows, output_projection_weight, precision=PRECISION_HIGH)) + output_projection_bias
    resid_one = patches + layer_norm(projected, attention_norm_gain, attention_norm_bias)
    resid_low = low(resid_one).reshape(IMAGES, N_ROW, TOK_MB, DIM)
    logits = low_back(jnp.einsum('isnc,ce->isne', resid_low, routing_weight, precision=PRECISION_HIGH))
    logit_peak = lax.optimization_barrier(jnp.max(logits, -1, keepdims=True))
    logit_exp = jnp.exp(logits - logit_peak)
    router_probs = logit_exp / lax.optimization_barrier(jnp.sum(logit_exp, -1, keepdims=True))
    gate_value = lax.optimization_barrier(jnp.sum(router_probs * selected_expert, -1))
    sent = low_back(jnp.einsum('isnk,isnc->iskc', expert_dispatch, resid_low, precision=PRECISION_HIGH))
    buffers = sent.reshape(IMAGES, N_ROW, EXPERTS, CAP, DIM).transpose(2, 0, 1, 3, 4).reshape(EXPERTS, IMAGES * N_ROW * CAP, DIM)
    results = lax.map(jax.checkpoint(expert_apply), (buffers, expert_first_weight, expert_first_bias, expert_second_weight, expert_second_bias))
    returned = results.reshape(EXPERTS, IMAGES, N_ROW, CAP, DIM).transpose(1, 2, 0, 3, 4).reshape(IMAGES, N_ROW, EXPERTS * CAP, DIM)
    picked = jnp.einsum('isnk,iskc->isnc', expert_dispatch, returned, precision=PRECISION_HIGH)
    moe_branch = layer_norm(gate_value[..., None] * picked, expert_norm_gain, expert_norm_bias)
    resid_two = resid_one + moe_branch.reshape(IMAGES, HEIGHT, WIDTH, DIM)
    merged = resid_two.reshape(IMAGES, HEIGHT // 2, 2, WIDTH // 2, 2, DIM).transpose(0, 1, 3, 4, 2, 5)
    merged = low(merged.reshape(IMAGES, HEIGHT // 2, WIDTH // 2, 4 * DIM))
    reduced = low_back(jnp.einsum('ihwk,kd->ihwd', merged, patch_merging_weight, precision=PRECISION_HIGH))
    return layer_norm(reduced, merging_norm_gain, merging_norm_bias)

def reference(patches, unpadded_patch_size, patch_expert_index, cotangent, query_key_value_weight, query_projection_bias, value_projection_bias, log_cosine_scale, bias_network_first_weight, bias_network_first_bias, bias_network_second_weight, output_projection_weight, output_projection_bias, attention_norm_gain, attention_norm_bias, routing_weight, expert_first_weight, expert_first_bias, expert_second_weight, expert_second_bias, expert_norm_gain, expert_norm_bias, patch_merging_weight, merging_norm_gain, merging_norm_bias):
    weight_arrays = tuple((single_entry.astype(jnp.float32) for single_entry in (query_key_value_weight, query_projection_bias, value_projection_bias, log_cosine_scale, bias_network_first_weight, bias_network_first_bias, bias_network_second_weight, output_projection_weight, output_projection_bias, attention_norm_gain, attention_norm_bias, routing_weight, expert_first_weight, expert_first_bias, expert_second_weight, expert_second_bias, expert_norm_gain, expert_norm_bias, patch_merging_weight, merging_norm_gain, merging_norm_bias)))
    outputs = []
    input_grads = []
    totals = None
    for micro_step in range(MICRO):
        every_window_mask = jax.vmap(image_masks)(unpadded_patch_size[micro_step])
        token_rows = patch_expert_index[micro_step, :, :, :, 0].reshape(IMAGES * N_ROW, TOK_MB)
        selected_expert, expert_dispatch = jax.vmap(partial(route_tables, experts=EXPERTS, capacity=CAP))(token_rows)
        selected_expert = selected_expert.reshape(IMAGES, N_ROW, TOK_MB, EXPERTS)
        expert_dispatch = expert_dispatch.reshape(IMAGES, N_ROW, TOK_MB, EXPERTS * CAP)

        def closed(inputs, *params):
            return forward_block(inputs, *params, every_window_mask, selected_expert, expert_dispatch)
        result, pull = jax.vjp(closed, patches[micro_step].astype(jnp.float32), *weight_arrays)
        grads = pull(cotangent[micro_step].astype(jnp.float32))
        outputs.append(result.astype(jnp.bfloat16))
        input_grads.append(grads[0].astype(jnp.bfloat16))
        totals = grads[1:] if totals is None else tuple((first + second for first, second in zip(totals, grads[1:])))
    g_qkv, g_qbias, g_vbias, g_scale, g_first, g_first_bias, g_second, g_proj, g_proj_bias, g_again, g_ashift, g_router, g_ein, g_ein_bias, g_eout, g_eout_bias, g_mgain, g_mshift, g_merge, g_rgain, g_rshift = totals
    return (jnp.stack(outputs), jnp.stack(input_grads), g_qkv, g_qbias, g_vbias, g_scale, g_first, g_first_bias, g_second, g_proj, g_proj_bias, g_again, g_ashift, g_router, g_ein, g_ein_bias, g_eout, g_eout_bias, g_mgain, g_mshift, g_merge, g_rgain, g_rshift)
```

```python
import functools

import jax
import jax.numpy as jnp
from jax import lax
from jax.experimental import pallas as pl
from jax.experimental.pallas import tpu as pltpu
from jax.sharding import PartitionSpec as P

HEAD_COUNT = 12
HEAD_DIM = 32
WINDOW_SIDE = 12
LANES = 128
TILE_HEADS = LANES // HEAD_DIM


PRECISION_HIGH = lax.Precision.HIGHEST
EPS_NORM = 1e-05
EPS_UNIT = 1e-06
MASK_FILL = -100.0
BF = jnp.bfloat16
FL = jnp.float32
VMEM_BYTES = 52 * 2**20


def passed_along(array, axis, by):
    count = lax.axis_size(axis)
    return lax.ppermute(array, axis, [(i, (i + by) % count) for i in range(count)])


def exact_error_gelu(values):
    return jax.nn.gelu(values, approximate=False)


def span_offsets():
    return jnp.arange(WINDOW_SIDE)[:, None] - jnp.arange(WINDOW_SIDE)[None, :] + (WINDOW_SIDE - 1)


def span_select():
    spans = jnp.arange(2 * WINDOW_SIDE - 1)
    return (span_offsets()[:, :, None] == spans[None, None, :]).astype(FL)


def position_table(
    bias_network_first_weight, bias_network_first_bias, bias_network_second_weight
):
    span_axis = (jnp.arange(2 * WINDOW_SIDE - 1, dtype=FL) - (WINDOW_SIDE - 1)) * (
        8.0 / (WINDOW_SIDE - 1)
    )
    span_axis = jnp.sign(span_axis) * jnp.log2(jnp.abs(span_axis) + 1.0) / 3.0
    grid_rows = jnp.broadcast_to(span_axis[:, None], (2 * WINDOW_SIDE - 1, 2 * WINDOW_SIDE - 1))
    relative_coordinates = jnp.stack([grid_rows, grid_rows.T], -1)
    hidden_activation = exact_error_gelu(
        jnp.einsum(
            "plr,rt->plt", relative_coordinates, bias_network_first_weight, precision=PRECISION_HIGH
        )
        + bias_network_first_bias
    )
    return 16.0 * jax.nn.sigmoid(
        jnp.einsum(
            "qvw,wk->qvk", hidden_activation, bias_network_second_weight, precision=PRECISION_HIGH
        )
    )


def spread_table(table):
    select = span_select()
    spread = jnp.einsum("fqy,uzs,ysr->rqzfu", select, select, table, precision=PRECISION_HIGH)
    return spread.reshape(table.shape[-1], WINDOW_SIDE * WINDOW_SIDE, WINDOW_SIDE * WINDOW_SIDE)


def gather_table(grad):
    side = WINDOW_SIDE
    spans = 2 * side - 1
    select = span_select()
    columns = jnp.einsum("jkb,ic->kijcb", select, jnp.eye(side, dtype=FL)).reshape(
        side, side * side, side * spans
    )
    part = lax.dot_general(
        grad.reshape(HEAD_COUNT * side, side * side * side),
        columns.reshape(side * side * side, side * spans),
        (((1,), (0,)), ((), ())),
        precision=PRECISION_HIGH,
    )
    part = part.reshape(HEAD_COUNT, side, side, spans)
    return jnp.einsum("hqpb,pqa->abh", part, select, precision=PRECISION_HIGH)


def window_mask(row_start, total_rows, total_cols, valid_rows, valid_cols):
    half_win = WINDOW_SIDE // 2
    rows_at = row_start + jnp.arange(WINDOW_SIDE)
    cols_at = jnp.arange(total_cols)
    row_zone = (rows_at >= total_rows - WINDOW_SIDE).astype(jnp.int32) + (
        rows_at >= total_rows - half_win
    ).astype(jnp.int32)
    col_zone = (cols_at >= total_cols - WINDOW_SIDE).astype(jnp.int32) + (
        cols_at >= total_cols - half_win
    ).astype(jnp.int32)
    zone_ids = 3 * row_zone[:, None] + col_zone[None, :]
    inside = ((rows_at + half_win) % total_rows < valid_rows)[:, None] & (
        (cols_at + half_win) % total_cols < valid_cols
    )[None, :]
    win_count = total_cols // WINDOW_SIDE
    zone_ids = (
        zone_ids.reshape(WINDOW_SIDE, win_count, WINDOW_SIDE)
        .transpose(1, 0, 2)
        .reshape(win_count, WINDOW_SIDE * WINDOW_SIDE)
    )
    inside = (
        inside.reshape(WINDOW_SIDE, win_count, WINDOW_SIDE)
        .transpose(1, 0, 2)
        .reshape(win_count, WINDOW_SIDE * WINDOW_SIDE)
    )
    mask = jnp.where(zone_ids[:, :, None] != zone_ids[:, None, :], MASK_FILL, 0.0) + jnp.where(
        inside[:, None, :], 0.0, MASK_FILL
    )
    return mask - jnp.max(mask, -1, keepdims=True)


def mm(left, right):
    return jnp.dot(left, right, preferred_element_type=FL)


def mm_nt(left, right):
    return lax.dot_general(left, right, (((1,), (1,)), ((), ())), preferred_element_type=FL)


def mm_tn(left, right):
    return lax.dot_general(left, right, (((0,), (0,)), ((), ())), preferred_element_type=FL)


def call_kernel(body, name, outs, args, scratch=(), flops=10**9):
    moved = sum(a.size * a.dtype.itemsize for a in args)
    vmem = pl.BlockSpec(memory_space=pltpu.VMEM)
    return pl.pallas_call(
        body,
        name=name,
        out_shape=[jax.ShapeDtypeStruct(s, d) for s, d in outs],
        in_specs=[vmem] * len(args),
        out_specs=[vmem] * len(outs),
        scratch_shapes=[pltpu.VMEM(s, d) for s, d in scratch],
        compiler_params=pltpu.CompilerParams(vmem_limit_bytes=VMEM_BYTES),
        cost_estimate=pl.CostEstimate(flops=flops, bytes_accessed=moved, transcendentals=0),
    )(*args)


def rows_at(start, size):
    return pl.ds(pl.multiple_of(start, 16), size)


def head_sums(values, block_ones):
    high = values.astype(BF)
    rest = (values - high.astype(FL)).astype(BF)
    return mm(jnp.concatenate([high, rest], 1), block_ones)


def tiles_of(channels):
    return [slice(LANES * t, LANES * (t + 1)) for t in range(channels // LANES)]


def to_windows(sources, grid_ref, win_ref, band_cols, channels):
    half_win = WINDOW_SIDE // 2
    pitch = band_cols + 8
    win_area = WINDOW_SIDE * WINDOW_SIDE
    for i in range(WINDOW_SIDE):
        value = sources(i).astype(FL)
        for t, lanes in enumerate(tiles_of(channels)):
            grid_ref[t, i * pitch : i * pitch + band_cols, :] = value[:, lanes]
            grid_ref[t, i * pitch + band_cols : (i + 1) * pitch, :] = value[0:8, lanes]
    for t in range(channels // LANES):
        for n in range(band_cols // WINDOW_SIDE):
            for i in range(WINDOW_SIDE):
                at = i * pitch + n * WINDOW_SIDE + half_win
                to = n * win_area + i * WINDOW_SIDE
                win_ref[t, to : to + WINDOW_SIDE, :] = grid_ref[t, at : at + WINDOW_SIDE, :]


def from_windows(put, grid_ref, win_ref, band_cols, channels):
    half_win = WINDOW_SIDE // 2
    pitch = band_cols + 8
    win_area = WINDOW_SIDE * WINDOW_SIDE
    for t in range(channels // LANES):
        for n in range(band_cols // WINDOW_SIDE):
            for i in range(WINDOW_SIDE):
                to = i * pitch + n * WINDOW_SIDE + half_win
                at = n * win_area + i * WINDOW_SIDE
                grid_ref[t, to : to + WINDOW_SIDE, :] = win_ref[t, at : at + WINDOW_SIDE, :]
        for i in range(WINDOW_SIDE):
            grid_ref[t, i * pitch : i * pitch + half_win, :] = grid_ref[
                t, i * pitch + band_cols : i * pitch + band_cols + half_win, :
            ]
    for i in range(WINDOW_SIDE):
        put(
            i,
            jnp.concatenate(
                [
                    grid_ref[t, i * pitch : i * pitch + band_cols, :]
                    for t in range(channels // LANES)
                ],
                1,
            ),
        )


def attend_forward_body(
    band_ref,
    below_ref,
    weight_ref,
    qbias_ref,
    vbias_ref,
    scale_ref,
    bias_ref,
    mask_ref,
    heads_ref,
    block_ref,
    own_ref,
    send_ref,
    win_ref,
    qkv_ref,
    inv_ref,
    grid_scr,
    win_scr,
    *,
    band_cols,
    channels,
):
    tokens = band_ref.shape[0]
    half = tokens // 2
    win_area = WINDOW_SIDE * WINDOW_SIDE
    tiles = tiles_of(channels)

    def source(i):
        if i < WINDOW_SIDE // 2:
            return band_ref[half + i * band_cols : half + (i + 1) * band_cols, :]
        at = (i - WINDOW_SIDE // 2) * band_cols
        return below_ref[at : at + band_cols, :]

    to_windows(source, grid_scr, win_scr, band_cols, channels)
    block_ones = block_ref[...]
    chunk = 2 * win_area

    def project(c, carry):
        rows = rows_at(c * chunk, chunk)
        low = jnp.concatenate([win_scr[t, rows, :] for t in range(len(tiles))], 1).astype(BF)
        win_ref[rows, :] = low
        qkv = mm(low, weight_ref[...])
        for lanes in tiles:
            key_lanes = slice(channels + lanes.start, channels + lanes.stop)
            value_lanes = slice(2 * channels + lanes.start, 2 * channels + lanes.stop)
            query = qkv[:, lanes] + qbias_ref[:, lanes]
            inverse = (
                lax.rsqrt(head_sums(query * query, block_ones) + EPS_UNIT) * scale_ref[:, lanes]
            )
            inv_ref[rows, lanes] = inverse
            qkv_ref[rows, lanes] = (query * inverse).astype(BF)
            key = qkv[:, key_lanes]
            inverse = lax.rsqrt(head_sums(key * key, block_ones) + EPS_UNIT)
            inv_ref[rows, key_lanes] = inverse
            qkv_ref[rows, key_lanes] = (key * inverse).astype(BF)
            qkv_ref[rows, value_lanes] = (qkv[:, value_lanes] + vbias_ref[:, lanes]).astype(BF)
        return carry

    lax.fori_loop(0, tokens // chunk, project, 0)
    lane = lax.broadcasted_iota(jnp.int32, (win_area, LANES), 1)
    in_head = [(lane // HEAD_DIM) == k for k in range(TILE_HEADS)]

    def attend(n, carry):
        rows = rows_at(n * win_area, win_area)
        for t, lanes in enumerate(tiles):
            query = qkv_ref[rows, lanes]
            key = qkv_ref[rows, channels + lanes.start : channels + lanes.stop]
            value = qkv_ref[rows, 2 * channels + lanes.start : 2 * channels + lanes.stop]
            total = None
            for k in range(TILE_HEADS):
                head = t * TILE_HEADS + k
                mine = heads_ref[k]
                scores = mm_nt(query * mine, key)
                powers = jnp.exp(scores + bias_ref[head] + mask_ref[n])
                mixed = mm(powers.astype(BF), value * mine + (1 - mine))
                after = in_head[(k + 1) % TILE_HEADS]
                if total is None:
                    weighted, total = mixed, mixed
                else:
                    weighted = jnp.where(in_head[k], mixed, weighted)
                    total = jnp.where(after, mixed, total)
            total = pltpu.roll(total, LANES - HEAD_DIM, 1)
            win_scr[t, rows, :] = weighted / total
        return carry

    lax.fori_loop(0, tokens // win_area, attend, 0)

    def put(i, value):
        if i < WINDOW_SIDE // 2:
            own_ref[i * band_cols : (i + 1) * band_cols, :] = value.astype(BF)
        else:
            at = (i - WINDOW_SIDE // 2) * band_cols
            send_ref[at : at + band_cols, :] = value.astype(BF)

    from_windows(put, grid_scr, win_scr, band_cols, channels)


def attend_backward_body(
    own_ref,
    lifted_ref,
    weight_ref,
    scale_ref,
    bias_ref,
    mask_ref,
    heads_ref,
    block_ref,
    win_ref,
    qkv_ref,
    inv_ref,
    dx_own_ref,
    dx_send_ref,
    dweight_ref,
    dbias_ref,
    small_ref,
    grid_scr,
    win_scr,
    dqkv_scr,
    *,
    band_cols,
    channels,
):
    half = own_ref.shape[0]
    tokens = 2 * half
    win_area = WINDOW_SIDE * WINDOW_SIDE
    tiles = tiles_of(channels)

    def source(i):
        ref = own_ref if i < WINDOW_SIDE // 2 else lifted_ref
        at = (i % (WINDOW_SIDE // 2)) * band_cols
        return ref[at : at + band_cols, :]

    to_windows(source, grid_scr, win_scr, band_cols, channels)
    block_ones = block_ref[...]
    dbias_ref[...] = jnp.zeros_like(dbias_ref)
    small_ref[...] = jnp.zeros_like(small_ref)

    def attend(n, carry):
        rows = rows_at(n * win_area, win_area)
        for t, lanes in enumerate(tiles):
            key_lanes = slice(channels + lanes.start, channels + lanes.stop)
            value_lanes = slice(2 * channels + lanes.start, 2 * channels + lanes.stop)
            query = qkv_ref[rows, lanes]
            key = qkv_ref[rows, key_lanes]
            value = qkv_ref[rows, value_lanes]
            back_low = win_scr[t, rows, :].astype(BF)
            dquery = dkey = dvalue = None
            for k in range(TILE_HEADS):
                head = t * TILE_HEADS + k
                mine = heads_ref[k]
                query_mine = query * mine
                back_mine = back_low * mine
                scores = mm_nt(key, query_mine)
                powers = jnp.exp(scores + bias_ref[head] + mask_ref[n])
                probs = powers * (1.0 / jnp.sum(powers, 0, keepdims=True))
                weighted = probs * mm_nt(value, back_mine)
                dscores = weighted - probs * jnp.sum(weighted, 0, keepdims=True)
                dbias_ref[head] += dscores
                dlow = dscores.astype(BF)
                dv = mm(probs.astype(BF), back_mine)
                dk = mm(dlow, query_mine)
                dq = mm_tn(dlow, key * mine)
                if dquery is None:
                    dquery, dkey, dvalue = dq, dk, dv
                else:
                    dquery, dkey, dvalue = dquery + dq, dkey + dk, dvalue + dv
            scale = scale_ref[:, lanes]
            unit = query.astype(FL)
            along = head_sums(unit * dquery, block_ones)
            dq_raw = inv_ref[rows, lanes] * (dquery - unit * along / (scale * scale))
            unit = key.astype(FL)
            dk_raw = inv_ref[rows, key_lanes] * (
                dkey - unit * head_sums(unit * dkey, block_ones)
            )
            dqkv_scr[rows, lanes] = dq_raw.astype(BF)
            dqkv_scr[rows, key_lanes] = dk_raw.astype(BF)
            dqkv_scr[rows, value_lanes] = dvalue.astype(BF)
            small_ref[0:1, lanes] += jnp.sum(dq_raw, 0, keepdims=True)
            small_ref[1:2, lanes] += jnp.sum(dvalue, 0, keepdims=True)
            small_ref[2:3, lanes] += jnp.sum(along, 0, keepdims=True)
        return carry

    lax.fori_loop(0, tokens // win_area, attend, 0)
    chunk = 2 * win_area

    def project(c, carry):
        rows = rows_at(c * chunk, chunk)
        back = mm_nt(dqkv_scr[rows, :], weight_ref[...])
        for t, lanes in enumerate(tiles):
            win_scr[t, rows, :] = back[:, lanes]
        return carry

    lax.fori_loop(0, tokens // chunk, project, 0)
    for part in range(3):
        lanes = slice(part * channels, (part + 1) * channels)
        dweight_ref[:, lanes] = mm_tn(win_ref[...], dqkv_scr[:, lanes])

    def put(i, value):
        if i < WINDOW_SIDE // 2:
            dx_own_ref[i * band_cols : (i + 1) * band_cols, :] = value
        else:
            at = (i - WINDOW_SIDE // 2) * band_cols
            dx_send_ref[at : at + band_cols, :] = value.astype(BF)

    from_windows(put, grid_scr, win_scr, band_cols, channels)


def lane_mean(values):
    return jnp.sum(values, -1, keepdims=True) * (1.0 / values.shape[-1])


def normalised(values):
    centred = values - lane_mean(values)
    inverse = lax.rsqrt(lane_mean(centred * centred) + EPS_NORM)
    return centred * inverse, inverse


def normalised_back(back, gain, unit, inverse):
    back = back * gain
    return inverse * (back - lane_mean(back) - unit * lane_mean(back * unit))


CHUNK = 144
PACK = 256


def pack_rows(dest_row_ref, rows_ref, out_ref):
    tokens = rows_ref.shape[0]

    def step(c, carry):
        place = lax.broadcasted_iota(jnp.int32, (PACK, tokens), 0) + c * PACK
        chosen = jnp.where(place == dest_row_ref[...], 1.0, 0.0).astype(BF)
        out_ref[rows_at(c * PACK, PACK), :] = mm(chosen, rows_ref[...]).astype(BF)
        return carry

    lax.fori_loop(0, out_ref.shape[0] // PACK, step, 0)


def unpack_rows(dest_col, buffer_ref):
    place = lax.broadcasted_iota(jnp.int32, (dest_col.shape[0], buffer_ref.shape[0]), 1)
    chosen = jnp.where(place == dest_col, 1.0, 0.0).astype(BF)
    return mm(chosen, buffer_ref[...])


def route_body(
    arrived_ref,
    own_ref,
    band_ref,
    weight_ref,
    small_ref,
    router_ref,
    expert_ref,
    dest_row_ref,
    resid_ref,
    unit_ref,
    aux_ref,
    low_ref,
    sent_ref,
    *,
    experts,
):
    half = arrived_ref.shape[0]
    lane = lax.broadcasted_iota(jnp.int32, (CHUNK, LANES), 1)
    for part, ref in enumerate((arrived_ref, own_ref)):

        def step(c, carry, part=part, ref=ref):
            rows = rows_at(part * half + c * CHUNK, CHUNK)
            projected = mm(ref[rows_at(c * CHUNK, CHUNK), :], weight_ref[...]) + small_ref[0:1, :]
            unit, inverse = normalised(projected)
            unit_ref[rows, :] = unit.astype(BF)
            resid = band_ref[rows, :].astype(FL) + unit * small_ref[1:2, :] + small_ref[2:3, :]
            resid_ref[rows, :] = resid
            low = resid.astype(BF)
            low_ref[rows, :] = low
            logits = jnp.where(lane < experts, mm(low, router_ref[...]), -1e30)
            powers = jnp.exp(logits - jnp.max(logits, -1, keepdims=True))
            probs = powers / jnp.sum(powers, -1, keepdims=True)
            gate = jnp.sum(
                jnp.where(lane == expert_ref[rows, :], probs, 0.0), -1, keepdims=True
            )
            aux_ref[rows, :] = jnp.where(
                lane == LANES - 1, gate, jnp.where(lane == LANES - 2, inverse, probs)
            )
            return carry

        lax.fori_loop(0, half // CHUNK, step, 0)
    pack_rows(dest_row_ref, low_ref, sent_ref)


def merge_body(
    returned_ref,
    dest_col_ref,
    dest_row_ref,
    expert_ref,
    aux_ref,
    resid_ref,
    small_ref,
    weight_ref,
    wide_ref,
    cotangent_ref,
    final_ref,
    merged_ref,
    dreduced_ref,
    dresid_ref,
    dlogits_ref,
    sent_ref,
    sums_ref,
    unit_scr,
    picked_scr,
    inverse_scr,
    token_scr,
    back_scr,
    *,
    experts,
    band_cols,
):
    tokens, channels = resid_ref.shape
    tiles = tiles_of(channels)
    lane = lax.broadcasted_iota(jnp.int32, (CHUNK, LANES), 1)

    def combine(c, carry):
        rows = rows_at(c * CHUNK, CHUNK)
        picked = unpack_rows(dest_col_ref[rows, :], returned_ref)
        picked_scr[rows, :] = picked
        gate = aux_ref[rows, :][:, LANES - 1 : LANES]
        unit, inverse = normalised(gate * picked)
        unit_scr[rows, :] = unit
        inverse_scr[rows, :] = jnp.broadcast_to(inverse, (CHUNK, LANES))
        resid = resid_ref[rows, :] + unit * small_ref[0:1, :] + small_ref[1:2, :]
        for t, lanes in enumerate(tiles):
            token_scr[t, rows, :] = resid[:, lanes]
        return carry

    lax.fori_loop(0, tokens // CHUNK, combine, 0)
    pairs = band_cols // 2
    for i in range(WINDOW_SIDE // 2):
        for k in range(4):
            start = (2 * i + k % 2) * band_cols + k // 2
            for t in range(len(tiles)):
                at = k * channels + t * LANES
                merged_ref[i * pairs : (i + 1) * pairs, at : at + LANES] = token_scr[
                    t, pl.ds(start, pairs, stride=2), :
                ].astype(BF)
    unit, inverse = normalised(mm(merged_ref[...], weight_ref[...]))
    final_ref[...] = (unit * wide_ref[0:1, :] + wide_ref[1:2, :]).astype(BF)
    back = cotangent_ref[...].astype(FL)
    sums_ref[...] = jnp.zeros_like(sums_ref)
    sums_ref[0:1, :] = jnp.sum(back * unit, 0, keepdims=True)
    sums_ref[1:2, :] = jnp.sum(back, 0, keepdims=True)
    dreduced = normalised_back(back, wide_ref[0:1, :], unit, inverse).astype(BF)
    dreduced_ref[...] = dreduced
    for k in range(4):
        part = mm_nt(dreduced, weight_ref[k * channels : (k + 1) * channels, :])
        for i in range(WINDOW_SIDE // 2):
            start = (2 * i + k % 2) * band_cols + k // 2
            for t, lanes in enumerate(tiles):
                token_scr[t, pl.ds(start, pairs, stride=2), :] = part[
                    i * pairs : (i + 1) * pairs, lanes
                ]

    def spread(c, carry):
        rows = rows_at(c * CHUNK, CHUNK)
        back = jnp.concatenate([token_scr[t, rows, :] for t in range(len(tiles))], 1)
        dresid_ref[rows, :] = back
        unit = unit_scr[rows, :]
        sums_ref[2:3, 0:channels] += jnp.sum(back * unit, 0, keepdims=True)
        sums_ref[3:4, 0:channels] += jnp.sum(back, 0, keepdims=True)
        back = normalised_back(back, small_ref[0:1, :], unit, inverse_scr[rows, :][:, 0:1])
        aux = aux_ref[rows, :]
        gate = aux[:, LANES - 1 : LANES]
        dgate = jnp.sum(back * picked_scr[rows, :], -1, keepdims=True)
        back_scr[rows, :] = (back * gate).astype(BF)
        probs = jnp.where(lane < experts, aux, 0.0)
        chosen = jnp.where(lane == expert_ref[rows, :], 1.0, 0.0)
        dlogits_ref[rows, :] = (probs * (chosen - gate) * dgate).astype(BF)
        return carry

    lax.fori_loop(0, tokens // CHUNK, spread, 0)
    pack_rows(dest_row_ref, back_scr, sent_ref)


def settle_body(
    sent_ref,
    dest_col_ref,
    dresid_ref,
    dlogits_ref,
    router_ref,
    unit_ref,
    aux_ref,
    small_ref,
    weight_ref,
    done_ref,
    low_ref,
    rows_ref,
    sums_ref,
):
    tokens, channels = dresid_ref.shape
    sums_ref[...] = jnp.zeros_like(sums_ref)

    def step(c, carry):
        rows = rows_at(c * CHUNK, CHUNK)
        back = dresid_ref[rows, :] + unpack_rows(dest_col_ref[rows, :], sent_ref)
        back = back + mm_nt(dlogits_ref[rows, :], router_ref[...])
        done_ref[rows, :] = back
        unit = unit_ref[rows, :].astype(FL)
        sums_ref[1:2, :] += jnp.sum(back * unit, 0, keepdims=True)
        sums_ref[2:3, :] += jnp.sum(back, 0, keepdims=True)
        inverse = aux_ref[rows, :][:, LANES - 2 : LANES - 1]
        back = normalised_back(back, small_ref[1:2, :], unit, inverse)
        sums_ref[0:1, :] += jnp.sum(back, 0, keepdims=True)
        low = back.astype(BF)
        low_ref[rows, :] = low
        rows_ref[rows, :] = mm_nt(low, weight_ref[...]).astype(BF)
        return carry

    lax.fori_loop(0, tokens // CHUNK, step, 0)


def dense_body(*refs):
    (*ins, proj_ref, router_ref) = refs
    arrived, own, low, resid, dlogits = (ins[i::5] for i in range(5))
    half = arrived[0].shape[0]
    proj = router = None
    for a, o, b, r, d in zip(arrived, own, low, resid, dlogits):
        now = mm_tn(a[...], b[0:half, :]) + mm_tn(o[...], b[half:, :])
        then = mm_tn(r[...], d[...])
        proj = now if proj is None else proj + now
        router = then if router is None else router + then
    proj_ref[...] = proj.astype(BF)
    router_ref[...] = router.astype(BF)


def merge_weight_body(*refs):
    (*ins, out_ref) = refs
    total = None
    for left, right in zip(ins[0::2], ins[1::2]):
        now = mm_tn(left[...], right[...])
        total = now if total is None else total + now
    out_ref[...] = total.astype(BF)


def merge_weight_grad(merged, dreduced, channels):
    args, specs = [], []
    for left, right in zip(merged, dreduced):
        args += [left, right]
        specs += [
            pl.BlockSpec((left.shape[0], channels), lambda k: (0, k)),
            pl.BlockSpec(right.shape, lambda k: (0, 0)),
        ]
    return pl.pallas_call(
        merge_weight_body,
        name="merge_weight_grad",
        grid=(4,),
        out_shape=jax.ShapeDtypeStruct((merged[0].shape[1], dreduced[0].shape[1]), BF),
        in_specs=specs,
        out_specs=pl.BlockSpec((channels, dreduced[0].shape[1]), lambda k: (k, 0)),
        compiler_params=pltpu.CompilerParams(vmem_limit_bytes=VMEM_BYTES),
    )(*args)


FF_CHUNK = 512


def expert_forward_body(
    rows_ref, win_ref, bin_ref, wout_ref, bout_ref, result_ref, hidden_ref, slope_ref, pre_scr, sum_scr
):
    step = pl.program_id(1)
    sources, slots, channels = rows_ref.shape
    rows = rows_ref[...].reshape(sources * slots, channels)
    pre_scr[...] = mm(rows, win_ref[0]) + bin_ref[0]
    block = 64

    def activate(c, carry):
        at = rows_at(c * block, block)
        pre = pre_scr[at, :]
        cdf = 0.5 * (1.0 + lax.erf(pre * 0.7071067811865476))
        hidden_ref[0, at, :] = (pre * cdf).astype(BF)
        slope_ref[0, at, :] = (
            cdf + pre * (0.3989422804014327 * jnp.exp(-0.5 * pre * pre))
        ).astype(BF)
        return carry

    lax.fori_loop(0, sources * slots // block, activate, 0)

    now = mm(hidden_ref[0], wout_ref[0])

    @pl.when(step == 0)
    def _():
        sum_scr[...] = now + bout_ref[0]

    @pl.when(step > 0)
    def _():
        sum_scr[...] += now

    @pl.when(step == pl.num_programs(1) - 1)
    def _():
        result_ref[...] = sum_scr[...].astype(BF).reshape(sources, slots, channels)


def expert_forward(rows, first_weight, first_bias, second_weight, second_bias, local):
    sources, both, channels = rows.shape
    slots = both // local
    hidden = first_weight.shape[-1]
    count = sources * slots
    wide = jax.ShapeDtypeStruct((local, count, hidden), BF)
    return pl.pallas_call(
        expert_forward_body,
        name="expert_forward",
        grid=(local, hidden // FF_CHUNK),
        out_shape=[jax.ShapeDtypeStruct(rows.shape, BF), wide, wide],
        in_specs=[
            pl.BlockSpec((sources, slots, channels), lambda e, f: (0, e, 0)),
            pl.BlockSpec((1, channels, FF_CHUNK), lambda e, f: (e, 0, f)),
            pl.BlockSpec((1, 1, FF_CHUNK), lambda e, f: (e, 0, f)),
            pl.BlockSpec((1, FF_CHUNK, channels), lambda e, f: (e, f, 0)),
            pl.BlockSpec((1, 1, channels), lambda e, f: (e, 0, 0)),
        ],
        out_specs=[
            pl.BlockSpec((sources, slots, channels), lambda e, f: (0, e, 0)),
            pl.BlockSpec((1, count, FF_CHUNK), lambda e, f: (e, 0, f)),
            pl.BlockSpec((1, count, FF_CHUNK), lambda e, f: (e, 0, f)),
        ],
        scratch_shapes=[pltpu.VMEM((count, FF_CHUNK), FL), pltpu.VMEM((count, channels), FL)],
        compiler_params=pltpu.CompilerParams(vmem_limit_bytes=VMEM_BYTES),
        cost_estimate=pl.CostEstimate(
            flops=4 * local * count * hidden * channels,
            bytes_accessed=8 * local * count * hidden,
            transcendentals=local * count * hidden,
        ),
    )(rows, first_weight, first_bias, second_weight, second_bias)


def expert_backward_body(
    rows_ref, win_ref, wout_ref, slope_ref, result_ref, dpre_ref, dbias_ref, sum_scr
):
    step = pl.program_id(1)
    sources, slots, channels = rows_ref.shape
    rows = rows_ref[...].reshape(sources * slots, channels)
    dpre = mm_nt(rows, wout_ref[0]) * slope_ref[0].astype(FL)
    dbias_ref[0] = jnp.sum(dpre, 0, keepdims=True)
    dpre_ref[0] = dpre.astype(BF)
    now = mm_nt(dpre_ref[0], win_ref[0])

    @pl.when(step == 0)
    def _():
        sum_scr[...] = now

    @pl.when(step > 0)
    def _():
        sum_scr[...] += now

    @pl.when(step == pl.num_programs(1) - 1)
    def _():
        result_ref[...] = sum_scr[...].astype(BF).reshape(sources, slots, channels)


def expert_backward(rows, first_weight, second_weight, slope, local):
    sources, both, channels = rows.shape
    slots = both // local
    hidden = first_weight.shape[-1]
    count = sources * slots
    return pl.pallas_call(
        expert_backward_body,
        name="expert_backward",
        grid=(local, hidden // FF_CHUNK),
        out_shape=[
            jax.ShapeDtypeStruct(rows.shape, BF),
            jax.ShapeDtypeStruct((local, count, hidden), BF),
            jax.ShapeDtypeStruct((local, 1, hidden), FL),
        ],
        in_specs=[
            pl.BlockSpec((sources, slots, channels), lambda e, f: (0, e, 0)),
            pl.BlockSpec((1, channels, FF_CHUNK), lambda e, f: (e, 0, f)),
            pl.BlockSpec((1, FF_CHUNK, channels), lambda e, f: (e, f, 0)),
            pl.BlockSpec((1, count, FF_CHUNK), lambda e, f: (e, 0, f)),
        ],
        out_specs=[
            pl.BlockSpec((sources, slots, channels), lambda e, f: (0, e, 0)),
            pl.BlockSpec((1, count, FF_CHUNK), lambda e, f: (e, 0, f)),
            pl.BlockSpec((1, 1, FF_CHUNK), lambda e, f: (e, 0, f)),
        ],
        scratch_shapes=[pltpu.VMEM((count, channels), FL)],
        compiler_params=pltpu.CompilerParams(vmem_limit_bytes=VMEM_BYTES),
        cost_estimate=pl.CostEstimate(
            flops=4 * local * count * hidden * channels,
            bytes_accessed=6 * local * count * hidden,
            transcendentals=0,
        ),
    )(rows, first_weight, second_weight, slope)


def expert_weight_body(*refs):
    (*ins, din_ref, dout_ref, dbias_ref) = refs
    din = dout = dbias = None
    for rows_ref, dpre_ref, hidden_ref, back_ref in zip(*(ins[i::4] for i in range(4))):
        sources, slots, channels = rows_ref.shape
        rows = rows_ref[...].reshape(sources * slots, channels)
        back = back_ref[...].reshape(sources * slots, channels)
        now = mm_tn(rows, dpre_ref[0])
        then = mm_tn(hidden_ref[0], back)
        sums = jnp.sum(back.astype(FL), 0, keepdims=True)
        if din is None:
            din, dout, dbias = now, then, sums
        else:
            din, dout, dbias = din + now, dout + then, dbias + sums
    din_ref[0] = din.astype(BF)
    dout_ref[0] = dout.astype(BF)
    dbias_ref[0] = dbias


def expert_weight_grads(rows, dpre, hidden, back, local):
    sources, both, channels = rows[0].shape
    slots = both // local
    count = sources * slots
    width = hidden[0].shape[-1]
    args, specs = [], []
    token_spec = pl.BlockSpec((sources, slots, channels), lambda e, f: (0, e, 0))
    wide_spec = pl.BlockSpec((1, count, FF_CHUNK), lambda e, f: (e, 0, f))
    for four in zip(rows, dpre, hidden, back):
        args += four
        specs += [token_spec, wide_spec, wide_spec, token_spec]
    return pl.pallas_call(
        expert_weight_body,
        name="expert_weight_grads",
        grid=(local, width // FF_CHUNK),
        out_shape=[
            jax.ShapeDtypeStruct((local, channels, width), BF),
            jax.ShapeDtypeStruct((local, width, channels), BF),
            jax.ShapeDtypeStruct((local, 1, channels), FL),
        ],
        in_specs=specs,
        out_specs=[
            pl.BlockSpec((1, channels, FF_CHUNK), lambda e, f: (e, 0, f)),
            pl.BlockSpec((1, FF_CHUNK, channels), lambda e, f: (e, f, 0)),
            pl.BlockSpec((1, 1, channels), lambda e, f: (e, 0, 0)),
        ],
        compiler_params=pltpu.CompilerParams(vmem_limit_bytes=VMEM_BYTES),
        cost_estimate=pl.CostEstimate(
            flops=8 * local * count * width * channels,
            bytes_accessed=8 * local * count * width,
            transcendentals=0,
        ),
    )(*args)


def swapped(rows):
    return lax.all_to_all(rows, "dp", split_axis=0, concat_axis=0, tiled=True)


def gathered(shard):
    count = lax.axis_size("dp")
    copies = jnp.broadcast_to(shard[None], (count,) + shard.shape)
    return swapped(copies).reshape(count * shard.shape[0], shard.shape[1])


def crossed(array, axis, bit):
    count = lax.axis_size(axis)
    return lax.ppermute(array, axis, [(i, i ^ bit) for i in range(count)])


def summed(array, axes):
    for axis in axes:
        bit = 1
        while bit < lax.axis_size(axis):
            array = array + crossed(array, axis, bit)
            bit *= 2
    return array


def dense_sum(grad):
    count = lax.axis_size("dp")
    grad = grad.reshape(count, grad.shape[0] // count, grad.shape[1])
    part = jnp.sum(swapped(grad).astype(FL), 0).astype(BF)
    bit = 1
    held = part[None]
    while bit < lax.axis_size("row"):
        held = jnp.concatenate([held, crossed(held, "row", bit)], 0)
        bit *= 2
    return jnp.sum(held.astype(FL), 0)


def on_device(
    patches,
    unpadded_patch_size,
    patch_expert_index,
    cotangent,
    query_key_value_weight,
    query_projection_bias,
    value_projection_bias,
    log_cosine_scale,
    bias_network_first_weight,
    bias_network_first_bias,
    bias_network_second_weight,
    output_projection_weight,
    output_projection_bias,
    attention_norm_gain,
    attention_norm_bias,
    routing_weight,
    expert_first_weight,
    expert_first_bias,
    expert_second_weight,
    expert_second_bias,
    expert_norm_gain,
    expert_norm_bias,
    patch_merging_weight,
    merging_norm_gain,
    merging_norm_bias,
):
    micro_count, _, band_rows, band_cols, channels = patches.shape
    micros = range(micro_count)
    half_rows = band_rows // 2
    win_count = band_cols // WINDOW_SIDE
    win_area = WINDOW_SIDE * WINDOW_SIDE
    tokens = band_rows * band_cols
    half = tokens // 2
    experts = routing_weight.shape[1]
    dp_size = lax.axis_size("dp")
    local = experts // dp_size
    capacity = (5 * tokens + 4 * experts - 1) // (4 * experts)
    slots = -(-capacity // 16) * 16
    buffer_rows = experts * slots
    total_rows = band_rows * lax.axis_size("row")
    row_start = band_rows * lax.axis_index("row")

    weight_qkv = gathered(query_key_value_weight)
    weight_late = gathered(
        jnp.concatenate(
            [output_projection_weight, jnp.pad(routing_weight, ((0, 0), (0, LANES - experts)))], 1
        )
    )
    weight_proj, weight_router = weight_late[:, :channels], weight_late[:, channels:]
    weight_merge = lax.all_gather(patch_merging_weight, "dp", axis=0, tiled=True)

    bands = patches.reshape(micro_count, tokens, channels)
    below = passed_along(bands[:, :half], "row", -1)

    table, table_back = jax.vjp(
        position_table,
        bias_network_first_weight,
        bias_network_first_bias,
        bias_network_second_weight,
    )
    bias_keys = spread_table(table)
    bias_rows = jnp.swapaxes(bias_keys, 1, 2)
    masks = [
        window_mask(
            row_start,
            total_rows,
            band_cols,
            unpadded_patch_size[m, 0, 0],
            unpadded_patch_size[m, 0, 1],
        )
        for m in micros
    ]
    masks_keys = [jnp.swapaxes(mask, 1, 2) for mask in masks]

    chosen = patch_expert_index.reshape(micro_count, tokens)
    one_hot = (chosen[:, :, None] == jnp.arange(experts)[None, None, :]).astype(FL)
    before = jnp.cumsum(one_hot, 1) - 1.0
    slot = jnp.sum(one_hot * before, -1).astype(jnp.int32)
    dest = jnp.where(slot < capacity, chosen * slots + slot, -1)

    lane = jnp.arange(LANES)
    head_marks = jnp.broadcast_to(
        ((lane // HEAD_DIM)[None, None, :] == jnp.arange(TILE_HEADS)[:, None, None]),
        (TILE_HEADS, win_area, LANES),
    ).astype(BF)
    block_ones = (
        ((jnp.arange(2 * LANES) % LANES) // HEAD_DIM)[:, None] == (lane // HEAD_DIM)[None, :]
    ).astype(BF)
    scale_lanes = jnp.repeat(jnp.exp(log_cosine_scale), HEAD_DIM)[None, :]
    qbias = query_projection_bias[None, :]
    vbias = value_projection_bias[None, :]
    attn_small = jnp.stack([output_projection_bias, attention_norm_gain, attention_norm_bias])
    moe_small = jnp.stack([expert_norm_gain, expert_norm_bias])
    merge_small = jnp.stack([merging_norm_gain, merging_norm_bias])
    first_bias = expert_first_bias[:, None, :]
    second_bias = expert_second_bias[:, None, :]

    grid_scratch = ((channels // LANES, band_rows * (band_cols + 8), LANES), FL)
    win_scratch = ((channels // LANES, tokens, LANES), FL)

    attended = [None] * micro_count
    arrived = [None] * micro_count
    routed = [None] * micro_count
    received = [None] * micro_count
    expert_out = [None] * micro_count
    returned = [None] * micro_count
    merged = [None] * micro_count
    back_res = [None] * micro_count
    expert_back = [None] * micro_count
    back_sent = [None] * micro_count
    settled = [None] * micro_count
    finished = [None] * micro_count
    outputs = [None] * micro_count
    input_grads = [None] * micro_count

    for m in micros:
        attended[m] = call_kernel(
            functools.partial(attend_forward_body, band_cols=band_cols, channels=channels),
            "attend_forward",
            [
                ((half, channels), BF),
                ((half, channels), BF),
                ((tokens, channels), BF),
                ((tokens, 3 * channels), BF),
                ((tokens, 2 * channels), FL),
            ],
            [
                bands[m],
                below[m],
                weight_qkv,
                qbias,
                vbias,
                scale_lanes,
                bias_rows,
                masks[m],
                head_marks,
                block_ones,
            ],
            [grid_scratch, win_scratch],
            flops=8 * 10**9,
        )
        arrived[m] = passed_along(attended[m][1], "row", 1)
        routed[m] = call_kernel(
            functools.partial(route_body, experts=experts),
            "route",
            [
                ((tokens, channels), FL),
                ((tokens, channels), BF),
                ((tokens, LANES), FL),
                ((tokens, channels), BF),
                ((buffer_rows, channels), BF),
            ],
            [
                arrived[m],
                attended[m][0],
                bands[m],
                weight_proj,
                attn_small,
                weight_router,
                chosen[m][:, None],
                dest[m][None, :],
            ],
            flops=4 * 10**9,
        )
        received[m] = swapped(routed[m][4].reshape(dp_size, local * slots, channels))
    for m in micros:
        expert_out[m] = expert_forward(
            received[m], expert_first_weight, first_bias, expert_second_weight, second_bias, local
        )
        returned[m] = swapped(expert_out[m][0])
    for m in micros:
        merged[m] = call_kernel(
            functools.partial(merge_body, experts=experts, band_cols=band_cols),
            "merge",
            [
                ((tokens // 4, 2 * channels), BF),
                ((tokens // 4, 4 * channels), BF),
                ((tokens // 4, 2 * channels), BF),
                ((tokens, channels), FL),
                ((tokens, LANES), BF),
                ((buffer_rows, channels), BF),
                ((8, 2 * channels), FL),
            ],
            [
                returned[m].reshape(buffer_rows, channels),
                dest[m][:, None],
                dest[m][None, :],
                chosen[m][:, None],
                routed[m][2],
                routed[m][0],
                moe_small,
                weight_merge,
                merge_small,
                cotangent[m, 0].reshape(tokens // 4, 2 * channels),
            ],
            [
                ((tokens, channels), FL),
                ((tokens, channels), FL),
                ((tokens, LANES), FL),
                ((channels // LANES, tokens, LANES), FL),
                ((tokens, channels), BF),
            ],
            flops=6 * 10**9,
        )
        outputs[m] = merged[m][0].reshape(band_rows // 2, band_cols // 2, 2 * channels)
        back_res[m] = swapped(merged[m][5].reshape(dp_size, local * slots, channels))
    for m in micros:
        expert_back[m] = expert_backward(
            back_res[m], expert_first_weight, expert_second_weight, expert_out[m][2], local
        )
        back_sent[m] = swapped(expert_back[m][0])

    grad_ein, grad_eout, grad_eout_bias = expert_weight_grads(
        received, [b[1] for b in expert_back], [b[1] for b in expert_out], back_res, local
    )
    grad_ein_bias = sum(b[2] for b in expert_back)
    grad_merge = merge_weight_grad([b[1] for b in merged], [b[2] for b in merged], channels)
    sum_ein, sum_eout = lax.psum((grad_ein, grad_eout), "row")
    sum_merge = dense_sum(grad_merge)
    expert_bias = summed(
        jnp.concatenate([grad_ein_bias[:, 0], grad_eout_bias[:, 0]], 1), ("row",)
    )

    for m in micros:
        settled[m] = call_kernel(
            settle_body,
            "settle",
            [
                ((tokens, channels), FL),
                ((tokens, channels), BF),
                ((tokens, channels), BF),
                ((8, channels), FL),
            ],
            [
                back_sent[m].reshape(buffer_rows, channels),
                dest[m][:, None],
                merged[m][3],
                merged[m][4],
                weight_router,
                routed[m][1],
                routed[m][2],
                attn_small,
                weight_proj,
            ],
            flops=3 * 10**9,
        )
        lifted = passed_along(settled[m][2][:half], "row", -1)
        finished[m] = call_kernel(
            functools.partial(attend_backward_body, band_cols=band_cols, channels=channels),
            "attend_backward",
            [
                ((half, channels), FL),
                ((half, channels), BF),
                ((channels, 3 * channels), FL),
                ((HEAD_COUNT, win_area, win_area), FL),
                ((8, channels), FL),
            ],
            [
                settled[m][2][half:],
                lifted,
                weight_qkv,
                scale_lanes,
                bias_keys,
                masks_keys[m],
                head_marks,
                block_ones,
                *attended[m][2:],
            ],
            [grid_scratch, win_scratch, ((tokens, 3 * channels), BF)],
            flops=16 * 10**9,
        )
        passed = passed_along(finished[m][1], "row", 1).astype(FL)
        input_grads[m] = (
            (settled[m][0] + jnp.concatenate([passed, finished[m][0]], 0))
            .astype(BF)
            .reshape(band_rows, band_cols, channels)
        )

    dense_args = []
    for m in micros:
        dense_args += [arrived[m], attended[m][0], settled[m][1], routed[m][3], merged[m][4]]
    grad_proj, grad_router = call_kernel(
        dense_body,
        "dense_weight_grads",
        [((channels, channels), BF), ((channels, LANES), BF)],
        dense_args,
    )
    sum_late = dense_sum(jnp.concatenate([grad_proj, grad_router], 1))
    sum_proj = sum_late[:, :channels]
    sum_router = sum_late[:, channels : channels + experts]
    sum_qkv = dense_sum(sum(f[2] for f in finished).astype(BF))

    both = ("row", "dp")
    settle_sums = sum(s[3] for s in settled)
    merge_sums = sum(b[6] for b in merged)
    early = summed(jnp.concatenate([settle_sums, merge_sums], 1), both)
    settle_sums, merge_sums = early[:, :channels], early[:, channels:]
    attn_sums = sum(f[4] for f in finished)
    dtable = gather_table(sum(f[3] for f in finished))
    late = jnp.concatenate([dtable.reshape(-1), attn_sums[:3].reshape(-1)])
    late = jnp.pad(late, (0, -late.size % 1024)).reshape(-1, 1024)
    late = summed(late, both).reshape(-1)
    dtable = late[: dtable.size].reshape(dtable.shape)
    attn_sums = late[dtable.size : dtable.size + 3 * channels].reshape(3, channels)
    grad_first, grad_first_bias, grad_second = table_back(dtable)
    sum_qbias, sum_vbias, sum_scale = attn_sums[0], attn_sums[1], attn_sums[2, ::HEAD_DIM]
    sum_proj_bias, sum_again, sum_ashift = settle_sums[0], settle_sums[1], settle_sums[2]
    sum_mgain, sum_mshift = merge_sums[2, :channels], merge_sums[3, :channels]
    sum_rgain, sum_rshift = merge_sums[0], merge_sums[1]
    hidden = expert_first_weight.shape[-1]
    sum_ein_bias, sum_eout_bias = expert_bias[:, :hidden], expert_bias[:, hidden:]
    return (
        jnp.stack(outputs)[:, None],
        jnp.stack(input_grads)[:, None],
        sum_qkv,
        sum_qbias,
        sum_vbias,
        sum_scale,
        grad_first,
        grad_first_bias,
        grad_second,
        sum_proj,
        sum_proj_bias,
        sum_again,
        sum_ashift,
        sum_router,
        sum_ein.astype(FL),
        sum_ein_bias,
        sum_eout.astype(FL),
        sum_eout_bias,
        sum_mgain,
        sum_mshift,
        sum_merge,
        sum_rgain,
        sum_rshift,
    )


def solution(mesh):
    return jax.shard_map(
        on_device,
        mesh=mesh,
        in_specs=(
            P(None, "dp", "row", None, None),
            P(None, "dp", None),
            P(None, "dp", "row", None, None),
            P(None, "dp", "row", None, None),
            P("dp", None),
            P(),
            P(),
            P(),
            P(),
            P(),
            P(),
            P("dp", None),
            P(),
            P(),
            P(),
            P("dp", None),
            P("dp", None, None),
            P("dp", None),
            P("dp", None, None),
            P("dp", None),
            P(),
            P(),
            P("dp", None),
            P(),
            P(),
        ),
        out_specs=(
            P(None, "dp", "row", None, None),
            P(None, "dp", "row", None, None),
            P("dp", None),
            P(),
            P(),
            P(),
            P(),
            P(),
            P(),
            P("dp", None),
            P(),
            P(),
            P(),
            P("dp", None),
            P("dp", None, None),
            P("dp", None),
            P("dp", None, None),
            P("dp", None),
            P(),
            P(),
            P("dp", None),
            P(),
            P(),
        ),
        check_vma=False,
    )
```

```python
import functools

import jax
import jax.numpy as jnp
from jax import lax
from jax.experimental import pallas as pl
from jax.experimental.pallas import tpu as pltpu
from jax.sharding import PartitionSpec as P

HEAD_COUNT = 12
HEAD_DIM = 32
WINDOW_SIDE = 12
LANES = 128
SHEAR = 384
ZONES = 16
UNROLL = 2
COST_SCALE = 0.4
TILE_HEADS = LANES // HEAD_DIM


PRECISION_HIGH = lax.Precision.HIGHEST
EPS_NORM = 1e-05
EPS_UNIT = 1e-06
MASK_FILL = -100.0
BF = jnp.bfloat16
FL = jnp.float32
VMEM_BYTES = 52 * 2**20


def cost(micros):
    return pl.CostEstimate(
        flops=int(micros * COST_SCALE * 1.1e9), bytes_accessed=10**5, transcendentals=0
    )


def passed_along(array, axis, by):
    count = lax.axis_size(axis)
    return lax.ppermute(array, axis, [(i, (i + by) % count) for i in range(count)])


def exact_error_gelu(values):
    return jax.nn.gelu(values, approximate=False)


def position_table(
    bias_network_first_weight, bias_network_first_bias, bias_network_second_weight
):
    span_axis = (jnp.arange(2 * WINDOW_SIDE - 1, dtype=FL) - (WINDOW_SIDE - 1)) * (
        8.0 / (WINDOW_SIDE - 1)
    )
    span_axis = jnp.sign(span_axis) * jnp.log2(jnp.abs(span_axis) + 1.0) / 3.0
    grid_rows = jnp.broadcast_to(span_axis[:, None], (2 * WINDOW_SIDE - 1, 2 * WINDOW_SIDE - 1))
    relative_coordinates = jnp.stack([grid_rows, grid_rows.T], -1)
    hidden_activation = exact_error_gelu(
        jnp.einsum(
            "plr,rt->plt", relative_coordinates, bias_network_first_weight, precision=PRECISION_HIGH
        )
        + bias_network_first_bias
    )
    return 16.0 * jax.nn.sigmoid(
        jnp.einsum(
            "qvw,wk->qvk", hidden_activation, bias_network_second_weight, precision=PRECISION_HIGH
        )
    )


def toeplitz_lines(table):
    side = WINDOW_SIDE
    heads = table.shape[-1]
    by_head = table.transpose(2, 0, 1)
    above = by_head[:, :, side - 1 :].reshape(heads, -1)
    below = jnp.pad(by_head[:, :, : side - 1], ((0, 0), (0, 0), (1, 0))).reshape(heads, -1)
    lines = jnp.pad(
        jnp.stack([above, below], 1), ((0, 0), (0, 0), (0, SHEAR - above.shape[1]))
    )
    lines = jnp.stack(
        [
            jnp.roll(lines[:, 0], -side * (side - 1), -1),
            jnp.roll(lines[:, 1], -side * side, -1),
        ],
        1,
    )
    back = jnp.roll(jnp.flip(lines, -1), 1, -1)
    return jnp.concatenate([lines, back], 1)


def table_of_lines(lines):
    side = WINDOW_SIDE
    spans = 2 * side - 1
    above = lines[:, 0, side - 1 : side - 1 + spans * side].reshape(-1, spans, side)
    below = jnp.pad(lines[:, 1], ((0, 0), (1, 0)))[:, : spans * side].reshape(-1, spans, side)
    return jnp.concatenate([below[:, :, 1:], above], 2).transpose(1, 2, 0)


def mask_operands(row_start, total_rows, total_cols, valid_rows, valid_cols):
    half_win = WINDOW_SIDE // 2
    rows_at = row_start + jnp.arange(WINDOW_SIDE)
    cols_at = jnp.arange(total_cols)
    row_zone = (rows_at >= total_rows - WINDOW_SIDE).astype(jnp.int32) + (
        rows_at >= total_rows - half_win
    ).astype(jnp.int32)
    col_zone = (cols_at >= total_cols - WINDOW_SIDE).astype(jnp.int32) + (
        cols_at >= total_cols - half_win
    ).astype(jnp.int32)
    zone_ids = 3 * row_zone[:, None] + col_zone[None, :]
    outside = ((rows_at + half_win) % total_rows >= valid_rows)[:, None] | (
        (cols_at + half_win) % total_cols >= valid_cols
    )[None, :]
    codes = zone_ids + jnp.where(outside, ZONES, 0)
    win_count = total_cols // WINDOW_SIDE
    codes = (
        codes.reshape(WINDOW_SIDE, win_count, WINDOW_SIDE)
        .transpose(1, 0, 2)
        .reshape(win_count, WINDOW_SIDE * WINDOW_SIDE)
    )
    zones, out = codes % ZONES, codes // ZONES
    mask = jnp.where(zones[:, :, None] != zones[:, None, :], MASK_FILL, 0.0) + jnp.where(
        out[:, None, :] > 0, MASK_FILL, 0.0
    )
    peak = jnp.max(mask, -1)[:, :, None]
    lane = jnp.arange(LANES)
    same = zones[:, :, None] == lane
    query = jnp.where(
        lane < ZONES,
        jnp.where(same, -MASK_FILL, 0.0),
        jnp.where(lane == ZONES, MASK_FILL, jnp.where(lane == ZONES + 1, MASK_FILL - peak, 0.0)),
    )
    key = jnp.where(
        lane < ZONES,
        jnp.where(same, 1.0, 0.0),
        jnp.where(lane == ZONES, out[:, :, None], jnp.where(lane == ZONES + 1, 1.0, 0.0)),
    )
    return (
        query.astype(BF).reshape(-1, LANES),
        key.astype(BF).reshape(-1, LANES),
    )


def plus(left, right):
    return left.astype(FL) + right.astype(FL)


def mm(left, right):
    return jnp.dot(left, right, preferred_element_type=FL)


def mm_nt(left, right):
    return lax.dot_general(left, right, (((1,), (1,)), ((), ())), preferred_element_type=FL)


def mm_tn(left, right):
    return lax.dot_general(left, right, (((0,), (0,)), ((), ())), preferred_element_type=FL)


def skipping(body, count, extra):
    def run(*refs):
        return body(*refs[:count], *refs[count + extra :])

    return run


def call_kernel(body, name, outs, args, scratch=(), micros=5, after=()):
    specs, arrays = [], []
    for arg in args:
        array, spec = arg if isinstance(arg, tuple) else (arg, None)
        if spec is None:
            spec = pl.BlockSpec(array.shape, lambda i, rank=array.ndim: (0,) * rank)
        specs.append(spec)
        arrays.append(array)
    return pl.pallas_call(
        skipping(body, len(args), len(after)),
        name=name,
        grid=(1,),
        out_shape=[jax.ShapeDtypeStruct(s, d) for s, d in outs],
        in_specs=specs + [pl.BlockSpec(memory_space=pl.ANY)] * len(after),
        out_specs=[pl.BlockSpec(s, lambda i, rank=len(s): (0,) * rank) for s, _ in outs],
        scratch_shapes=[pltpu.VMEM(s, d) for s, d in scratch],
        compiler_params=pltpu.CompilerParams(vmem_limit_bytes=VMEM_BYTES),
        cost_estimate=cost(micros),
    )(*arrays, *after)


def rows_at(start, size):
    return pl.ds(pl.multiple_of(start, 16), size)


def head_sums(values, block_ones):
    high = values.astype(BF)
    rest = (values - high.astype(FL)).astype(BF)
    return mm(jnp.concatenate([high, rest], 1), block_ones)


def tiles_of(channels):
    return [slice(LANES * t, LANES * (t + 1)) for t in range(channels // LANES)]


def to_windows(sources, grid_ref, win_ref, band_cols, channels):
    half_win = WINDOW_SIDE // 2
    pitch = band_cols + 8
    win_area = WINDOW_SIDE * WINDOW_SIDE
    for i in range(WINDOW_SIDE):
        value = sources(i).astype(FL)
        for t, lanes in enumerate(tiles_of(channels)):
            grid_ref[t, i * pitch : i * pitch + band_cols, :] = value[:, lanes]
            grid_ref[t, i * pitch + band_cols : (i + 1) * pitch, :] = value[0:8, lanes]
    for t in range(channels // LANES):
        for n in range(band_cols // WINDOW_SIDE):
            for i in range(WINDOW_SIDE):
                at = i * pitch + n * WINDOW_SIDE + half_win
                to = n * win_area + i * WINDOW_SIDE
                win_ref[t, to : to + WINDOW_SIDE, :] = grid_ref[t, at : at + WINDOW_SIDE, :]


def from_windows(put, grid_ref, win_ref, band_cols, channels):
    half_win = WINDOW_SIDE // 2
    pitch = band_cols + 8
    win_area = WINDOW_SIDE * WINDOW_SIDE
    for t in range(channels // LANES):
        for n in range(band_cols // WINDOW_SIDE):
            for i in range(WINDOW_SIDE):
                to = i * pitch + n * WINDOW_SIDE + half_win
                at = n * win_area + i * WINDOW_SIDE
                grid_ref[t, to : to + WINDOW_SIDE, :] = win_ref[t, at : at + WINDOW_SIDE, :]
        for i in range(WINDOW_SIDE):
            grid_ref[t, i * pitch : i * pitch + half_win, :] = grid_ref[
                t, i * pitch + band_cols : i * pitch + band_cols + half_win, :
            ]
    for i in range(WINDOW_SIDE):
        put(
            i,
            jnp.concatenate(
                [
                    grid_ref[t, i * pitch : i * pitch + band_cols, :]
                    for t in range(channels // LANES)
                ],
                1,
            ),
        )


def stacked(tile, heads_ref):
    return jnp.concatenate([tile] * TILE_HEADS, 0) * heads_ref[...]


def spread_body(lines_ref, rows_ref, keys_ref):
    area = WINDOW_SIDE * WINDOW_SIDE
    row = lax.broadcasted_iota(jnp.int32, (area, area), 0) % WINDOW_SIDE
    lane = lax.broadcasted_iota(jnp.int32, (area, area), 1) % WINDOW_SIDE

    def shear(line):
        wide = jnp.broadcast_to(line, (area, SHEAR))
        return pltpu.roll(wide, 0, 1, stride=1, stride_axis=0)[:, 0:area]

    def step(t, carry):
        rows, keys = [], []
        for k in range(TILE_HEADS):
            lines = lines_ref[t * TILE_HEADS + k]
            keys.append(jnp.where(lane >= row, shear(lines[0:1]), shear(lines[1:2])))
            rows.append(jnp.where(row >= lane, shear(lines[2:3]), shear(lines[3:4])))
        rows_ref[t] = jnp.concatenate(rows, 1)
        keys_ref[t] = jnp.concatenate(keys, 1)
        return carry

    lax.fori_loop(0, rows_ref.shape[0], step, 0)


def fold_body(*refs):
    (*ins, out_ref) = refs
    area = WINDOW_SIDE * WINDOW_SIDE
    row = lax.broadcasted_iota(jnp.int32, (area, area), 0)
    lane = lax.broadcasted_iota(jnp.int32, (area, area), 1)
    turn = jnp.where(row + lane == area - 1, 1.0, 0.0).astype(BF)
    later = lane % WINDOW_SIDE >= (area - 1 - row) % WINDOW_SIDE
    blank = jnp.zeros((area, SHEAR - area), FL)

    def fold(values):
        wide = jnp.concatenate([values, blank], 1)
        return jnp.sum(pltpu.roll(wide, 0, 1, stride=1, stride_axis=0), 0, keepdims=True)

    def step(value, head):
        total = None
        for _ in range(3):
            part = value.astype(BF)
            value = value - part.astype(FL)
            now = mm(turn, part)
            total = now if total is None else total + now
        out_ref[head, 0:1, :] = fold(jnp.where(later, total, 0.0))
        out_ref[head, 1:2, :] = fold(jnp.where(later, 0.0, total))

    for t, ref in enumerate(ins):
        value = ref[...]
        for k in range(TILE_HEADS):
            step(value[:, k * area : (k + 1) * area], t * TILE_HEADS + k)


def slot_body(
    place_ref,
    experts_ref,
    column_ref,
    dest_column_ref,
    dest_row_ref,
    *,
    experts,
    local,
    slots,
    capacity,
):
    tokens = experts_ref.shape[1]

    def place(expert):
        upper = jnp.where(expert >= experts // 2, 1, 0)
        inner = expert - upper * (experts // 2)
        apart = upper ^ place_ref[0]
        member = (inner // local) ^ place_ref[1]
        return ((2 * member + apart) * local + inner % local) * slots

    block = LANES
    lower = (
        lax.broadcasted_iota(jnp.int32, (block, block), 0)
        > lax.broadcasted_iota(jnp.int32, (block, block), 1)
    ).astype(FL).astype(BF)
    upper = (
        lax.broadcasted_iota(jnp.int32, (block, block), 0)
        < lax.broadcasted_iota(jnp.int32, (block, block), 1)
    ).astype(FL).astype(BF)
    lane = lax.broadcasted_iota(jnp.int32, (block, LANES), 1)
    sublane = lax.broadcasted_iota(jnp.int32, (LANES, block), 0)
    seen_row = jnp.zeros((1, LANES), FL)
    seen_column = jnp.zeros((LANES, 1), FL)
    for c in range(tokens // block):
        line = experts_ref[:, c * block : (c + 1) * block]
        across = jnp.where(sublane == line, 1.0, 0.0)
        column = jnp.broadcast_to(line.astype(FL), (block, block)).T[:, 0:1].astype(jnp.int32)
        down = jnp.where(lane == column, 1.0, 0.0)
        before = mm(lower, down.astype(BF)) + seen_row
        slot = jnp.sum(down * before, 1, keepdims=True).astype(jnp.int32)
        column_ref[c * block : (c + 1) * block, :] = column
        dest_column_ref[c * block : (c + 1) * block, :] = jnp.where(
            slot < capacity, place(column) + slot, -1
        )
        before = mm(across.astype(BF), upper) + seen_column
        slot = jnp.sum(across * before, 0, keepdims=True).astype(jnp.int32)
        dest_row_ref[:, c * block : (c + 1) * block] = jnp.where(
            slot < capacity, place(line) + slot, -1
        )
        seen_row = seen_row + jnp.sum(down, 0, keepdims=True)
        seen_column = seen_column + jnp.sum(across, 1, keepdims=True)


def slot_tables(chosen, my_place, experts, local, slots, capacity):
    tokens = chosen.shape[1]
    vmem = pl.BlockSpec(memory_space=pltpu.VMEM)
    column = jax.ShapeDtypeStruct((tokens, 1), jnp.int32)
    return pl.pallas_call(
        functools.partial(
            slot_body, experts=experts, local=local, slots=slots, capacity=capacity
        ),
        name="slot_tables",
        in_specs=[pl.BlockSpec(memory_space=pltpu.SMEM), vmem],
        out_specs=[vmem] * 3,
        out_shape=[column, column, jax.ShapeDtypeStruct((1, tokens), jnp.int32)],
    )(my_place, chosen)


def attend_forward_body(
    band_ref,
    below_ref,
    weight_ref,
    qbias_ref,
    vbias_ref,
    scale_ref,
    bias_ref,
    query_zone_ref,
    key_zone_ref,
    heads_ref,
    block_ref,
    own_ref,
    send_ref,
    win_ref,
    qkv_ref,
    inv_ref,
    grid_scr,
    win_scr,
    *,
    band_cols,
    channels,
):
    tokens = band_ref.shape[0]
    half = tokens // 2
    win_area = WINDOW_SIDE * WINDOW_SIDE
    tiles = tiles_of(channels)

    def source(i):
        if i < WINDOW_SIDE // 2:
            return band_ref[half + i * band_cols : half + (i + 1) * band_cols, :]
        at = (i - WINDOW_SIDE // 2) * band_cols
        return below_ref[at : at + band_cols, :]

    to_windows(source, grid_scr, win_scr, band_cols, channels)
    block_ones = block_ref[...]
    chunk = 2 * win_area

    def project(c, carry):
        rows = rows_at(c * chunk, chunk)
        low = jnp.concatenate([win_scr[t, rows, :] for t in range(len(tiles))], 1).astype(BF)
        win_ref[rows, :] = low
        qkv = mm(low, weight_ref[...])
        for lanes in tiles:
            key_lanes = slice(channels + lanes.start, channels + lanes.stop)
            value_lanes = slice(2 * channels + lanes.start, 2 * channels + lanes.stop)
            query = qkv[:, lanes] + qbias_ref[:, lanes]
            inverse = (
                lax.rsqrt(head_sums(query * query, block_ones) + EPS_UNIT) * scale_ref[:, lanes]
            )
            inv_ref[rows, lanes] = inverse
            qkv_ref[rows, lanes] = (query * inverse).astype(BF)
            key = qkv[:, key_lanes]
            inverse = lax.rsqrt(head_sums(key * key, block_ones) + EPS_UNIT)
            inv_ref[rows, key_lanes] = inverse
            qkv_ref[rows, key_lanes] = (key * inverse).astype(BF)
            qkv_ref[rows, value_lanes] = (qkv[:, value_lanes] + vbias_ref[:, lanes]).astype(BF)
        return carry

    lax.fori_loop(0, tokens // chunk, project, 0)

    def attend(n, carry):
        rows = rows_at(n * win_area, win_area)
        query_zone = query_zone_ref[rows, :]
        key_zone = jnp.concatenate([key_zone_ref[rows, :]] * TILE_HEADS, 0)
        for t, lanes in enumerate(tiles):
            query = qkv_ref[rows, lanes]
            key = qkv_ref[rows, channels + lanes.start : channels + lanes.stop]
            value = qkv_ref[rows, 2 * channels + lanes.start : 2 * channels + lanes.stop]
            scores = mm_nt(
                jnp.concatenate([query, query_zone], 1),
                jnp.concatenate([stacked(key, heads_ref), key_zone], 1),
            )
            powers = jnp.exp(scores + bias_ref[t]).astype(BF)
            mixed = mm(powers, jnp.concatenate([stacked(value, heads_ref), heads_ref[...]], 1))
            win_scr[t, rows, :] = mixed[:, :LANES] / mixed[:, LANES:]
        return carry

    lax.fori_loop(0, tokens // win_area, attend, 0, unroll=UNROLL)

    def put(i, value):
        if i < WINDOW_SIDE // 2:
            own_ref[i * band_cols : (i + 1) * band_cols, :] = value.astype(BF)
        else:
            at = (i - WINDOW_SIDE // 2) * band_cols
            send_ref[at : at + band_cols, :] = value.astype(BF)

    from_windows(put, grid_scr, win_scr, band_cols, channels)


def window_body(own_ref, lifted_ref, out_ref, grid_scr, win_scr, *, band_cols, channels):
    def source(i):
        ref = own_ref if i < WINDOW_SIDE // 2 else lifted_ref
        at = (i % (WINDOW_SIDE // 2)) * band_cols
        return ref[at : at + band_cols, :]

    to_windows(source, grid_scr, win_scr, band_cols, channels)
    for t, lanes in enumerate(tiles_of(channels)):
        out_ref[:, lanes] = win_scr[t].astype(BF)


def attend_backward_body(*refs, summed_before):
    (
        back_ref,
        query_ref,
        key_ref,
        value_ref,
        query_inv_ref,
        key_inv_ref,
        scale_ref,
        win_ref,
        bias_ref,
        query_zone_ref,
        key_zone_ref,
        heads_ref,
        block_ref,
        *rest,
    ) = refs
    if summed_before:
        dweight_before_ref, dbias_before_ref, *rest = rest
    dqkv_ref, dweight_ref, dbias_ref, small_ref = rest
    tokens = back_ref.shape[0]
    win_area = WINDOW_SIDE * WINDOW_SIDE
    block_ones = block_ref[...]
    if summed_before:
        dbias_ref[...] = dbias_before_ref[...]
    else:
        dbias_ref[...] = jnp.zeros_like(dbias_ref)
    small_ref[...] = jnp.zeros_like(small_ref)

    def attend(n, carry):
        rows = rows_at(n * win_area, win_area)
        query = query_ref[rows, :]
        key = key_ref[rows, :]
        queries = stacked(query, heads_ref)
        backs = stacked(back_ref[rows, :], heads_ref)
        query_zone = jnp.concatenate([query_zone_ref[rows, :]] * TILE_HEADS, 0)
        scores = mm_nt(
            jnp.concatenate([key, key_zone_ref[rows, :]], 1),
            jnp.concatenate([queries, query_zone], 1),
        )
        powers = jnp.exp(scores + bias_ref[0])
        probs = powers * (1.0 / jnp.sum(powers, 0, keepdims=True))
        weighted = probs * mm_nt(value_ref[rows, :], backs)
        dscores = weighted - probs * jnp.sum(weighted, 0, keepdims=True)
        dbias_ref[...] += dscores
        dlow = dscores.astype(BF)
        dvalue = mm(probs.astype(BF), backs)
        dkey = mm(dlow, queries)
        dquery = mm_tn(dlow, key) * heads_ref[...].astype(FL)
        dquery = sum(dquery[k * win_area : (k + 1) * win_area] for k in range(TILE_HEADS))
        scale = scale_ref[...]
        unit = query.astype(FL)
        along = head_sums(unit * dquery, block_ones)
        dquery = query_inv_ref[rows, :] * (dquery - unit * along / (scale * scale))
        unit = key.astype(FL)
        dkey = key_inv_ref[rows, :] * (dkey - unit * head_sums(unit * dkey, block_ones))
        for part, grad in enumerate((dquery, dkey, dvalue)):
            dqkv_ref[rows, part * LANES : (part + 1) * LANES] = grad.astype(BF)
        small_ref[0:1, :] += jnp.sum(dquery, 0, keepdims=True)
        small_ref[1:2, :] += jnp.sum(dvalue, 0, keepdims=True)
        small_ref[2:3, :] += jnp.sum(along, 0, keepdims=True)
        return carry

    lax.fori_loop(0, tokens // win_area, attend, 0, unroll=UNROLL)
    dweight = mm_tn(win_ref[...], dqkv_ref[...])
    if summed_before:
        dweight = dweight + dweight_before_ref[...]
    dweight_ref[...] = dweight.astype(dweight_ref.dtype)


def input_grad_body(
    first_ref,
    second_ref,
    third_ref,
    weight_ref,
    own_ref,
    send_ref,
    grid_scr,
    win_scr,
    *,
    band_cols,
    channels,
):
    tokens = first_ref.shape[0]
    tiles = tiles_of(channels)
    chunk = 2 * WINDOW_SIDE * WINDOW_SIDE

    def project(c, carry):
        rows = rows_at(c * chunk, chunk)
        parts = [ref[rows, :] for ref in (first_ref, second_ref, third_ref)]
        wide = jnp.concatenate([p[:, lanes] for lanes in tiles for p in parts], 1)
        back = mm_nt(wide, weight_ref[...])
        for t, lanes in enumerate(tiles):
            win_scr[t, rows, :] = back[:, lanes]
        return carry

    lax.fori_loop(0, tokens // chunk, project, 0)

    def put(i, value):
        if i < WINDOW_SIDE // 2:
            own_ref[i * band_cols : (i + 1) * band_cols, :] = value
        else:
            at = (i - WINDOW_SIDE // 2) * band_cols
            send_ref[at : at + band_cols, :] = value.astype(BF)

    from_windows(put, grid_scr, win_scr, band_cols, channels)


def lane_mean(values):
    return jnp.sum(values, -1, keepdims=True) * (1.0 / values.shape[-1])


def normalised(values):
    centred = values - lane_mean(values)
    inverse = lax.rsqrt(lane_mean(centred * centred) + EPS_NORM)
    return centred * inverse, inverse


def normalised_back(back, gain, unit, inverse):
    back = back * gain
    return inverse * (back - lane_mean(back) - unit * lane_mean(back * unit))


CHUNK = 576


def pack_rows(dest_row_ref, rows_ref, out_refs):
    tokens = rows_ref.shape[0]
    start = 0
    for ref in out_refs:
        place = lax.broadcasted_iota(jnp.int32, (ref.shape[0], tokens), 0) + start
        chosen = jnp.where(place == dest_row_ref[...], 1.0, 0.0).astype(BF)
        ref[...] = mm(chosen, rows_ref[...]).astype(BF)
        start += ref.shape[0]


def unpack_rows(dest_col, buffer):
    place = lax.broadcasted_iota(jnp.int32, (dest_col.shape[0], buffer.shape[0]), 1)
    chosen = jnp.where(place == dest_col, 1.0, 0.0).astype(BF)
    return mm(chosen, buffer)


def route_body(
    arrived_ref,
    own_ref,
    band_ref,
    weight_ref,
    small_ref,
    router_ref,
    expert_ref,
    dest_row_ref,
    resid_ref,
    unit_ref,
    aux_ref,
    low_ref,
    *sent_refs,
    experts,
):
    half = arrived_ref.shape[0]
    lane = lax.broadcasted_iota(jnp.int32, (CHUNK, LANES), 1)
    for part, ref in enumerate((arrived_ref, own_ref)):

        def step(c, carry, part=part, ref=ref):
            rows = rows_at(part * half + c * CHUNK, CHUNK)
            projected = mm(ref[rows_at(c * CHUNK, CHUNK), :], weight_ref[...]) + small_ref[0:1, :]
            unit, inverse = normalised(projected)
            unit_ref[rows, :] = unit.astype(BF)
            resid = band_ref[rows, :].astype(FL) + unit * small_ref[1:2, :] + small_ref[2:3, :]
            resid_ref[rows, :] = resid
            low = resid.astype(BF)
            low_ref[rows, :] = low
            logits = jnp.where(lane < experts, mm(low, router_ref[...]), -1e30)
            powers = jnp.exp(logits - jnp.max(logits, -1, keepdims=True))
            probs = powers / jnp.sum(powers, -1, keepdims=True)
            gate = jnp.sum(
                jnp.where(lane == expert_ref[rows, :], probs, 0.0), -1, keepdims=True
            )
            aux_ref[rows, :] = jnp.where(
                lane == LANES - 1, gate, jnp.where(lane == LANES - 2, inverse, probs)
            )
            return carry

        lax.fori_loop(0, half // CHUNK, step, 0)
    pack_rows(dest_row_ref, low_ref, sent_refs)


def merge_body(*refs, experts, band_cols, members):
    returned_refs, refs = refs[:members], refs[members:]
    (
        dest_col_ref,
        dest_row_ref,
        expert_ref,
        aux_ref,
        resid_ref,
        small_ref,
        weight_ref,
        wide_ref,
        cotangent_ref,
        final_ref,
        merged_ref,
        dreduced_ref,
        dresid_ref,
        dlogits_ref,
        sums_ref,
    ) = refs[:15]
    sent_refs = refs[15 : 15 + members]
    unit_scr, picked_scr, inverse_scr, token_scr, back_scr = refs[15 + members :]
    returned = jnp.concatenate([ref[...] for ref in returned_refs], 0)
    tokens, channels = resid_ref.shape
    tiles = tiles_of(channels)
    lane = lax.broadcasted_iota(jnp.int32, (CHUNK, LANES), 1)

    def combine(c, carry):
        rows = rows_at(c * CHUNK, CHUNK)
        picked = unpack_rows(dest_col_ref[rows, :], returned)
        picked_scr[rows, :] = picked
        gate = aux_ref[rows, :][:, LANES - 1 : LANES]
        unit, inverse = normalised(gate * picked)
        unit_scr[rows, :] = unit
        inverse_scr[rows, :] = jnp.broadcast_to(inverse, (CHUNK, LANES))
        resid = resid_ref[rows, :] + unit * small_ref[0:1, :] + small_ref[1:2, :]
        for t, lanes in enumerate(tiles):
            token_scr[t, rows, :] = resid[:, lanes]
        return carry

    lax.fori_loop(0, tokens // CHUNK, combine, 0)
    pairs = band_cols // 2
    for i in range(WINDOW_SIDE // 2):
        for k in range(4):
            start = (2 * i + k % 2) * band_cols + k // 2
            for t in range(len(tiles)):
                at = k * channels + t * LANES
                merged_ref[i * pairs : (i + 1) * pairs, at : at + LANES] = token_scr[
                    t, pl.ds(start, pairs, stride=2), :
                ].astype(BF)
    unit, inverse = normalised(mm(merged_ref[...], weight_ref[...]))
    final_ref[...] = (unit * wide_ref[0:1, :] + wide_ref[1:2, :]).astype(BF)
    back = cotangent_ref[...].astype(FL)
    sums_ref[...] = jnp.zeros_like(sums_ref)
    sums_ref[0:1, :] = jnp.sum(back * unit, 0, keepdims=True)
    sums_ref[1:2, :] = jnp.sum(back, 0, keepdims=True)
    dreduced = normalised_back(back, wide_ref[0:1, :], unit, inverse).astype(BF)
    dreduced_ref[...] = dreduced
    for k in range(4):
        part = mm_nt(dreduced, weight_ref[k * channels : (k + 1) * channels, :])
        for i in range(WINDOW_SIDE // 2):
            start = (2 * i + k % 2) * band_cols + k // 2
            for t, lanes in enumerate(tiles):
                token_scr[t, pl.ds(start, pairs, stride=2), :] = part[
                    i * pairs : (i + 1) * pairs, lanes
                ]

    def spread(c, carry):
        rows = rows_at(c * CHUNK, CHUNK)
        back = jnp.concatenate([token_scr[t, rows, :] for t in range(len(tiles))], 1)
        dresid_ref[rows, :] = back
        unit = unit_scr[rows, :]
        sums_ref[2:3, 0:channels] += jnp.sum(back * unit, 0, keepdims=True)
        sums_ref[3:4, 0:channels] += jnp.sum(back, 0, keepdims=True)
        back = normalised_back(back, small_ref[0:1, :], unit, inverse_scr[rows, :][:, 0:1])
        aux = aux_ref[rows, :]
        gate = aux[:, LANES - 1 : LANES]
        dgate = jnp.sum(back * picked_scr[rows, :], -1, keepdims=True)
        back_scr[rows, :] = (back * gate).astype(BF)
        probs = jnp.where(lane < experts, aux, 0.0)
        chosen = jnp.where(lane == expert_ref[rows, :], 1.0, 0.0)
        dlogits_ref[rows, :] = (probs * (chosen - gate) * dgate).astype(BF)
        return carry

    lax.fori_loop(0, tokens // CHUNK, spread, 0)
    pack_rows(dest_row_ref, back_scr, sent_refs)


def settle_body(*refs, members):
    sent_refs, refs = refs[:members], refs[members:]
    (
        dest_col_ref,
        dresid_ref,
        dlogits_ref,
        router_ref,
        unit_ref,
        aux_ref,
        small_ref,
        weight_ref,
        done_ref,
        low_ref,
        rows_ref,
        sums_ref,
    ) = refs
    sent = jnp.concatenate([ref[...] for ref in sent_refs], 0)
    tokens, channels = dresid_ref.shape
    sums_ref[...] = jnp.zeros_like(sums_ref)

    def step(c, carry):
        rows = rows_at(c * CHUNK, CHUNK)
        back = dresid_ref[rows, :] + unpack_rows(dest_col_ref[rows, :], sent)
        back = back + mm_nt(dlogits_ref[rows, :], router_ref[...])
        done_ref[rows, :] = back
        unit = unit_ref[rows, :].astype(FL)
        sums_ref[1:2, :] += jnp.sum(back * unit, 0, keepdims=True)
        sums_ref[2:3, :] += jnp.sum(back, 0, keepdims=True)
        inverse = aux_ref[rows, :][:, LANES - 2 : LANES - 1]
        back = normalised_back(back, small_ref[1:2, :], unit, inverse)
        sums_ref[0:1, :] += jnp.sum(back, 0, keepdims=True)
        low = back.astype(BF)
        low_ref[rows, :] = low
        rows_ref[rows, :] = mm_nt(low, weight_ref[...]).astype(BF)
        return carry

    lax.fori_loop(0, tokens // CHUNK, step, 0)


def dense_body(*refs):
    (*ins, proj_ref, router_ref) = refs
    arrived, own, low, resid, dlogits = (ins[i::5] for i in range(5))
    half = arrived[0].shape[0]
    proj = router = None
    for a, o, b, r, d in zip(arrived, own, low, resid, dlogits):
        now = mm_tn(a[...], b[0:half, :]) + mm_tn(o[...], b[half:, :])
        then = mm_tn(r[...], d[...])
        proj = now if proj is None else proj + now
        router = then if router is None else router + then
    proj_ref[...] = proj.astype(BF)
    router_ref[...] = router.astype(BF)


def merge_weight_body(*refs):
    (*ins, out_ref) = refs
    total = None
    for left, right in zip(ins[0::2], ins[1::2]):
        now = mm_tn(left[...], right[...])
        total = now if total is None else total + now
    out_ref[...] = total.astype(BF)


def merge_weight_grad(merged, dreduced, channels, after):
    args, specs = [], []
    for left, right in zip(merged, dreduced):
        args += [left, right]
        specs += [
            pl.BlockSpec((left.shape[0], channels), lambda k: (0, k)),
            pl.BlockSpec(right.shape, lambda k: (0, 0)),
        ]
    return pl.pallas_call(
        skipping(merge_weight_body, len(args), len(after)),
        name="merge_weight_grad",
        grid=(4,),
        out_shape=jax.ShapeDtypeStruct((merged[0].shape[1], dreduced[0].shape[1]), BF),
        in_specs=specs + [pl.BlockSpec(memory_space=pl.ANY)] * len(after),
        out_specs=pl.BlockSpec((channels, dreduced[0].shape[1]), lambda k: (k, 0)),
        compiler_params=pltpu.CompilerParams(vmem_limit_bytes=VMEM_BYTES),
        cost_estimate=cost(5),
    )(*args, *after)


PIECE = 384


def spot_of(member, me, bits):
    apart = member ^ me
    spot = 0
    for k in range(bits):
        spot = spot | (((apart >> k) & 1) << (bits - 1 - k))
    return spot


def piece_home(expert, chunk, row_size, chunks):
    piece = expert * chunks + chunk
    return piece % row_size, piece // row_size


def expert_weight(own, other_refs, expert, chunk, local, chunks, me):
    row_size = len(other_refs)
    member, _ = piece_home(jnp.maximum(expert - local, 0), chunk, row_size, chunks)
    spot = spot_of(member, me, row_size.bit_length() - 1)
    weight = own
    for k, ref in enumerate(other_refs):
        weight = jnp.where((expert >= local) & (spot == k), ref[0], weight)
    return weight


def taken(refs, *counts):
    lists = []
    for count in counts:
        lists.append(refs[:count])
        refs = refs[count:]
    return lists + [refs]


def joined(refs):
    return jnp.concatenate([ref[...] for ref in refs], 0)


def put_parts(refs, value):
    start = 0
    for ref in refs:
        ref[...] = value[start : start + ref.shape[0]].astype(BF)
        start += ref.shape[0]


def expert_forward_body(me_ref, *refs, local, members, row_size):
    row_refs, (in_ref, in_bias_ref, out_ref, out_bias_ref), in_others, out_others, refs = taken(
        refs, members, 4, row_size, row_size
    )
    result_refs, (hidden_ref, slope_ref, pre_scr) = taken(refs, members)
    expert = pl.program_id(0)
    rows = joined(row_refs)
    count = rows.shape[0]
    chunks = in_ref.shape[2] // PIECE
    block = 64
    total = None
    for chunk in range(chunks):
        lanes = slice(chunk * PIECE, (chunk + 1) * PIECE)
        weight = expert_weight(
            in_ref[0, :, lanes], in_others, expert, chunk, local, chunks, me_ref[0]
        )
        pre_scr[...] = mm(rows, weight) + in_bias_ref[0, :, lanes]

        def activate(c, carry, lanes=lanes):
            at = rows_at(c * block, block)
            pre = pre_scr[at, :]
            cdf = 0.5 * (1.0 + lax.erf(pre * 0.7071067811865476))
            hidden_ref[0, at, lanes] = (pre * cdf).astype(BF)
            slope_ref[0, at, lanes] = (
                cdf + pre * (0.3989422804014327 * jnp.exp(-0.5 * pre * pre))
            ).astype(BF)
            return carry

        lax.fori_loop(0, count // block, activate, 0)
        weight = expert_weight(
            out_ref[0, lanes, :], out_others, expert, chunk, local, chunks, me_ref[0]
        )
        now = mm(hidden_ref[0, :, lanes], weight)
        total = now if total is None else total + now
    put_parts(result_refs, total + out_bias_ref[0])


def expert_specs(members, slots, channels, hidden, local, row_size):
    chunks = hidden // PIECE

    def other_at(k, me):
        return (jnp.maximum(k - local, 0) * chunks // row_size, 0, 0)

    def own_at(k, me):
        return (jnp.minimum(k, local - 1), 0, 0)

    return dict(
        tokens=pl.BlockSpec((slots, channels), lambda k, me: (k, 0)),
        wide=pl.BlockSpec((1, members * slots, hidden), lambda k, me: (k, 0, 0)),
        first=pl.BlockSpec((1, channels, hidden), own_at),
        second=pl.BlockSpec((1, hidden, channels), own_at),
        other=pl.BlockSpec((1, PIECE, PIECE), other_at),
        bias=pl.BlockSpec((1, 1, hidden), lambda k, me: (k, 0, 0)),
        low_bias=pl.BlockSpec((1, 1, channels), lambda k, me: (k, 0, 0)),
    )


def call_expert(
    body, name, me, steps, in_specs, out_specs, outs, scratch, args, micros, after=()
):
    return pl.pallas_call(
        skipping(body, 1 + len(args), len(after)),
        name=name,
        grid_spec=pltpu.PrefetchScalarGridSpec(
            num_scalar_prefetch=1,
            grid=(steps,),
            in_specs=in_specs + [pl.BlockSpec(memory_space=pl.ANY)] * len(after),
            out_specs=out_specs,
            scratch_shapes=scratch,
        ),
        out_shape=outs,
        compiler_params=pltpu.CompilerParams(vmem_limit_bytes=VMEM_BYTES),
        cost_estimate=cost(micros),
    )(me, *args, *after)


def expert_forward(
    me, rows, first, second, first_other, second_other, first_bias, second_bias, after
):
    members, row_size = len(rows), len(first_other)
    local, channels, hidden = first.shape
    slots = rows[0].shape[0] // (2 * local)
    count = members * slots
    spec = expert_specs(members, slots, channels, hidden, local, row_size)
    wide = jax.ShapeDtypeStruct((2 * local, count, hidden), BF)
    outs = call_expert(
        functools.partial(
            expert_forward_body, local=local, members=members, row_size=row_size
        ),
        "expert_forward",
        me,
        2 * local,
        [spec["tokens"]] * members
        + [spec["first"], spec["bias"], spec["second"], spec["low_bias"]]
        + [spec["other"]] * (2 * row_size),
        [spec["tokens"]] * members + [spec["wide"], spec["wide"]],
        [jax.ShapeDtypeStruct(rows[0].shape, BF)] * members + [wide, wide],
        [pltpu.VMEM((count, PIECE), FL)],
        [*rows, first, first_bias, second, second_bias, *first_other, *second_other],
        19,
        after,
    )
    return outs[:members], outs[members], outs[members + 1]


def expert_backward_body(me_ref, *refs, local, members, row_size):
    row_refs, (in_ref, out_ref, slope_ref), in_others, out_others, refs = taken(
        refs, members, 3, row_size, row_size
    )
    result_refs, (dpre_ref, dbias_ref) = taken(refs, members)
    expert = pl.program_id(0)
    rows = joined(row_refs)
    chunks = in_ref.shape[2] // PIECE
    total = None
    for chunk in range(chunks):
        lanes = slice(chunk * PIECE, (chunk + 1) * PIECE)
        weight = expert_weight(
            out_ref[0, lanes, :], out_others, expert, chunk, local, chunks, me_ref[0]
        )
        dpre = mm_nt(rows, weight) * slope_ref[0, :, lanes].astype(FL)
        dbias_ref[0, :, lanes] = jnp.sum(dpre, 0, keepdims=True)
        low = dpre.astype(BF)
        dpre_ref[0, :, lanes] = low
        weight = expert_weight(
            in_ref[0, :, lanes], in_others, expert, chunk, local, chunks, me_ref[0]
        )
        now = mm_nt(low, weight)
        total = now if total is None else total + now
    put_parts(result_refs, total)


def expert_backward(me, rows, first, second, first_other, second_other, slope, after):
    members, row_size = len(rows), len(first_other)
    local, channels, hidden = first.shape
    slots = rows[0].shape[0] // (2 * local)
    count = members * slots
    spec = expert_specs(members, slots, channels, hidden, local, row_size)
    outs = call_expert(
        functools.partial(
            expert_backward_body, local=local, members=members, row_size=row_size
        ),
        "expert_backward",
        me,
        2 * local,
        [spec["tokens"]] * members
        + [spec["first"], spec["second"], spec["wide"]]
        + [spec["other"]] * (2 * row_size),
        [spec["tokens"]] * members + [spec["wide"], spec["bias"]],
        [jax.ShapeDtypeStruct(rows[0].shape, BF)] * members
        + [
            jax.ShapeDtypeStruct((2 * local, count, hidden), BF),
            jax.ShapeDtypeStruct((2 * local, 1, hidden), FL),
        ],
        [],
        [*rows, first, second, slope, *first_other, *second_other],
        12,
        after,
    )
    return outs[:members], outs[members], outs[members + 1]


def expert_weight_body(me_ref, *refs, local, members, micros, tokens_left):
    token_refs, wide_refs, (keep_ref, send_ref, dbias_ref) = taken(
        refs, members * micros, micros
    )
    expert = pl.program_id(0)
    half = keep_ref.shape[1]
    row_size = 2 * half
    chunks = wide_refs[0].shape[2] // PIECE
    rows = [joined(token_refs[m * members : (m + 1) * members]) for m in range(micros)]
    dbias_ref[0] = sum(jnp.sum(part.astype(FL), 0, keepdims=True) for part in rows)
    for chunk in range(chunks):
        lanes = slice(chunk * PIECE, (chunk + 1) * PIECE)
        total = None
        for part, ref in zip(rows, wide_refs):
            wide = ref[0, :, lanes]
            now = mm_tn(part, wide) if tokens_left else mm_tn(wide, part)
            total = now if total is None else total + now
        low = total.astype(BF)
        member, _ = piece_home(expert % local, chunk, row_size, chunks)
        spot = spot_of(member, me_ref[0], row_size.bit_length() - 1)

        @pl.when(spot < half)
        def _():
            keep_ref[0, spot, 0] = low

        @pl.when(spot >= half)
        def _():
            send_ref[0, spot - half, 0] = low


def expert_weight_grads(me, tokens, wide, local, row_size, tokens_left, after):
    members, micros = len(tokens[0]), len(tokens)
    together, channels = tokens[0][0].shape
    slots = together // (2 * local)
    width = wide[0].shape[-1]
    chunks = width // PIECE
    subs = local * chunks // row_size
    spec = expert_specs(members, slots, channels, width, local, row_size)
    half_shape = (2, row_size // 2, subs, PIECE, PIECE)
    half_spec = pl.BlockSpec(
        (1, row_size // 2, 1, PIECE, PIECE),
        lambda k, me: (k // local, 0, (k % local) * chunks // row_size, 0, 0),
    )
    half_out = jax.ShapeDtypeStruct(half_shape, BF)
    return call_expert(
        functools.partial(
            expert_weight_body,
            local=local,
            members=members,
            micros=micros,
            tokens_left=tokens_left,
        ),
        "expert_weight_grads",
        me,
        2 * local,
        [spec["tokens"]] * (members * micros) + [spec["wide"]] * micros,
        [half_spec] * 2 + [spec["low_bias"]],
        [half_out] * 2 + [jax.ShapeDtypeStruct((2 * local, 1, channels), FL)],
        [],
        [part for parts in tokens for part in parts] + list(wide),
        13,
        after,
    )


def add_pieces_body(keep_ref, got_ref, *out_refs):
    half = keep_ref.shape[1] // 2
    for group in range(2):
        if half:
            for k in range(half):
                out_refs[0][group, k] = plus(keep_ref[group, k], got_ref[group, k]).astype(BF)
                at = half + k
                out_refs[1][group, k] = plus(keep_ref[group, at], got_ref[group, at]).astype(BF)
        else:
            total = plus(keep_ref[group, 0], got_ref[group, 0])
            out_refs[group][...] = total.astype(out_refs[group].dtype)


def add_pieces(keep, got, after):
    groups, count = keep.shape[:2]
    if count > 1:
        shape = (groups, count // 2) + keep.shape[2:]
        outs = [(shape, BF), (shape, BF)]
    else:
        outs = [(keep.shape[2:], FL), (keep.shape[2:], BF)]
    return call_kernel(add_pieces_body, "add_pieces", outs, [keep, got], micros=3, after=after)


def add_halves_body(own_ref, got_ref, out_ref):
    out_ref[...] = plus(own_ref[...], got_ref[...]).astype(BF)


def add_halves(own, got, after):
    (total,) = call_kernel(
        add_halves_body, "add_halves", [(own.shape, BF)], [own, got], micros=2, after=after
    )
    return total


def place_body(me_ref, *refs, chunks, first):
    (*piece_refs, full_ref) = refs
    row_size = len(piece_refs)
    for c in range(chunks):
        member, _ = piece_home(pl.program_id(0), c, row_size, chunks)
        spot = spot_of(member, me_ref[0], row_size.bit_length() - 1)
        span = slice(c * PIECE, (c + 1) * PIECE)
        value = piece_refs[0][0]
        for k in range(1, row_size):
            value = jnp.where(spot == k, piece_refs[k][0], value)
        if first:
            full_ref[0, :, span] = value.astype(FL)
        else:
            full_ref[0, span, :] = value.astype(FL)


def place_pieces(me, pieces, local, hidden, first, after):
    row_size = len(pieces)
    chunks = hidden // PIECE
    shape = (local, PIECE, hidden) if first else (local, hidden, PIECE)
    return call_expert(
        functools.partial(place_body, chunks=chunks, first=first),
        "place_pieces",
        me,
        local,
        [pl.BlockSpec((1, PIECE, PIECE), lambda e, me: (e * chunks // row_size, 0, 0))]
        * row_size,
        [pl.BlockSpec((1,) + shape[1:], lambda e, me: (e, 0, 0))],
        [jax.ShapeDtypeStruct(shape, FL)],
        [],
        list(pieces),
        4,
        after,
    )[0]


def swapped(rows):
    return lax.all_to_all(rows, "dp", split_axis=0, concat_axis=0, tiled=True)


def exchanged(blocks):
    return [blocks[0]] + [crossed(block, "dp", k) for k, block in enumerate(blocks) if k]


def bits_of(axis):
    return [1 << k for k in reversed(range(lax.axis_size(axis).bit_length() - 1))]


def spread_over_row(piece):
    held = [piece]
    for bit in bits_of("row"):
        held = held + [crossed(part, "row", bit) for part in held]
    return held


def gathered(shard):
    count = lax.axis_size("dp")
    copies = jnp.broadcast_to(shard[None], (count,) + shard.shape)
    return swapped(copies).reshape(count * shard.shape[0], shard.shape[1])


def copy_body(in_ref, out_ref):
    out_ref[...] = in_ref[...]


def held_back(array, after):
    (copy,) = call_kernel(
        copy_body, "hold", [(array.shape, array.dtype)], [array], micros=1, after=after
    )
    return copy


def crossed(array, axis, bit):
    count = lax.axis_size(axis)
    return lax.ppermute(array, axis, [(i, i ^ bit) for i in range(count)])


def summed(array, axes):
    for axis in axes:
        bit = 1
        while bit < lax.axis_size(axis):
            array = array + crossed(array, axis, bit)
            bit *= 2
    return array


def dense_sum(grad):
    count = lax.axis_size("dp")
    half = count // 2
    place = lax.axis_index("dp")
    rows = grad.shape[0] // count
    grad = grad.reshape(2, half, rows, grad.shape[1])
    blocks = [
        lax.dynamic_index_in_dim(grad, (place % half) ^ k, 1, keepdims=False) for k in range(half)
    ]
    part = sum(block.astype(FL) for block in exchanged(blocks))
    mine = lax.dynamic_index_in_dim(part, place // half, 0, keepdims=False)
    other = lax.dynamic_index_in_dim(part, 1 - place // half, 0, keepdims=False).astype(BF)
    part = plus(mine, crossed(other, "dp", half)).astype(BF)
    held = spread_over_row(part)
    sums = held
    while len(sums) > 1:
        sums = [plus(left, right) for left, right in zip(sums[::2], sums[1::2])]
    return sums[0].astype(FL), [other, part, held[-1]]


def on_device(
    patches,
    unpadded_patch_size,
    patch_expert_index,
    cotangent,
    query_key_value_weight,
    query_projection_bias,
    value_projection_bias,
    log_cosine_scale,
    bias_network_first_weight,
    bias_network_first_bias,
    bias_network_second_weight,
    output_projection_weight,
    output_projection_bias,
    attention_norm_gain,
    attention_norm_bias,
    routing_weight,
    expert_first_weight,
    expert_first_bias,
    expert_second_weight,
    expert_second_bias,
    expert_norm_gain,
    expert_norm_bias,
    patch_merging_weight,
    merging_norm_gain,
    merging_norm_bias,
):
    micro_count, _, band_rows, band_cols, channels = patches.shape
    micros = range(micro_count)
    half_rows = band_rows // 2
    win_count = band_cols // WINDOW_SIDE
    win_area = WINDOW_SIDE * WINDOW_SIDE
    tokens = band_rows * band_cols
    half = tokens // 2
    experts = routing_weight.shape[1]
    dp_size = lax.axis_size("dp")
    local = experts // dp_size
    capacity = (5 * tokens + 4 * experts - 1) // (4 * experts)
    slots = -(-capacity // 16) * 16
    block_rows = 2 * local * slots
    members = dp_size // 2
    row_size = lax.axis_size("row")
    me = lax.axis_index("row").astype(jnp.int32)[None]
    my_place = lax.axis_index("dp").astype(jnp.int32)
    my_place = jnp.stack([my_place // members, my_place % members])
    total_rows = band_rows * lax.axis_size("row")
    row_start = band_rows * lax.axis_index("row")

    dense = gathered(
        jnp.concatenate(
            [
                query_key_value_weight,
                output_projection_weight,
                jnp.pad(routing_weight, ((0, 0), (0, LANES - experts))),
            ],
            1,
        )
    )
    weight_qkv = dense[:, : 3 * channels]
    weight_proj = dense[:, 3 * channels : 4 * channels]
    weight_router = dense[:, 4 * channels :]

    bands = patches.reshape(micro_count, tokens, channels)
    below = passed_along(bands[:, :half], "row", -1)

    table, table_back = jax.vjp(
        position_table,
        bias_network_first_weight,
        bias_network_first_bias,
        bias_network_second_weight,
    )
    tile_count = channels // LANES
    bias_shape = ((tile_count, win_area, TILE_HEADS * win_area), FL)
    bias_rows, bias_keys = call_kernel(
        spread_body, "spread_bias", [bias_shape, bias_shape], [toeplitz_lines(table)]
    )
    zones = [
        mask_operands(
            row_start,
            total_rows,
            band_cols,
            unpadded_patch_size[m, 0, 0],
            unpadded_patch_size[m, 0, 1],
        )
        for m in micros
    ]

    dest_cols, dest_rows, chosen_cols = [], [], []
    for m in micros:
        chosen = patch_expert_index[m].reshape(1, tokens)
        column, dest_col, dest_row = slot_tables(
            chosen, my_place, experts, local, slots, capacity
        )
        chosen_cols.append(column)
        dest_cols.append(dest_col)
        dest_rows.append(dest_row)

    hidden = expert_first_weight.shape[-1]
    chunks = hidden // PIECE
    subs = local * chunks // row_size
    first_piece, second_piece = [], []
    for sub in range(subs):
        piece = sub * row_size + me[0]
        at, start = piece // chunks, (piece % chunks) * PIECE
        first_piece.append(
            lax.dynamic_slice(expert_first_weight, (at, 0, start), (1, channels, PIECE))
        )
        second_piece.append(
            lax.dynamic_slice(expert_second_weight, (at, start, 0), (1, PIECE, channels))
        )
    first_got = crossed(jnp.concatenate(first_piece), "dp", members)
    second_got = crossed(held_back(jnp.concatenate(second_piece), [first_got]), "dp", members)
    first_other = spread_over_row(first_got)
    second_other = spread_over_row(second_got)
    expert_bias = jnp.concatenate([expert_first_bias, expert_second_bias], 1)
    expert_bias = jnp.concatenate([expert_bias, crossed(expert_bias, "dp", members)], 0)

    lane = jnp.arange(LANES)
    head_marks = jnp.repeat(
        (lane // HEAD_DIM)[None, :] == jnp.arange(TILE_HEADS)[:, None], win_area, 0
    ).astype(BF)
    block_ones = (
        ((jnp.arange(2 * LANES) % LANES) // HEAD_DIM)[:, None] == (lane // HEAD_DIM)[None, :]
    ).astype(BF)
    scale_lanes = jnp.repeat(jnp.exp(log_cosine_scale), HEAD_DIM)[None, :]
    qbias = query_projection_bias[None, :]
    vbias = value_projection_bias[None, :]
    attn_small = jnp.stack([output_projection_bias, attention_norm_gain, attention_norm_bias])
    moe_small = jnp.stack([expert_norm_gain, expert_norm_bias])
    merge_small = jnp.stack([merging_norm_gain, merging_norm_bias])
    first_bias = expert_bias[:, None, :hidden]
    second_bias = expert_bias[:, None, hidden:]

    grid_scratch = ((channels // LANES, band_rows * (band_cols + 8), LANES), FL)
    win_scratch = ((channels // LANES, tokens, LANES), FL)

    none = [None] * micro_count
    attended, arrived, routed, received = list(none), list(none), list(none), list(none)
    expert_out, returned, merged, back_res = list(none), list(none), list(none), list(none)
    expert_back, back_sent, settled, finished = list(none), list(none), list(none), list(none)
    outputs, input_grads, input_parts = list(none), list(none), list(none)

    forward_after = [[first_got], []]
    route_after = [[second_got, first_other[1]], []]
    for m in micros:
        attended[m] = call_kernel(
            functools.partial(attend_forward_body, band_cols=band_cols, channels=channels),
            "attend_forward",
            [
                ((half, channels), BF),
                ((half, channels), BF),
                ((tokens, channels), BF),
                ((tokens, 3 * channels), BF),
                ((tokens, 2 * channels), FL),
            ],
            [
                bands[m],
                below[m],
                weight_qkv,
                qbias,
                vbias,
                scale_lanes,
                bias_rows,
                *zones[m],
                head_marks,
                block_ones,
            ],
            [grid_scratch, win_scratch],
            micros=16,
            after=(forward_after[m] if m < 2 else []) + [a[0] for a in attended[:m][-1:]],
        )
        arrived[m] = passed_along(attended[m][1], "row", 1)
    for m in micros:
        routed[m] = call_kernel(
            functools.partial(route_body, experts=experts),
            "route",
            [
                ((tokens, channels), FL),
                ((tokens, channels), BF),
                ((tokens, LANES), FL),
                ((tokens, channels), BF),
            ]
            + [((block_rows, channels), BF)] * members,
            [
                arrived[m],
                attended[m][0],
                bands[m],
                weight_proj,
                attn_small,
                weight_router,
                chosen_cols[m],
                dest_rows[m],
            ],
            micros=12,
            after=[attended[-1][0] if m == 0 else routed[m - 1][2]]
            + (route_after[m] if m < 2 else []),
        )
        if m == 0:
            shard = held_back(patch_merging_weight, [routed[m][2]])
            weight_merge = lax.all_gather(shard, "dp", axis=0, tiled=True)
        received[m] = exchanged(routed[m][4:])
    for m in micros:
        expert_out[m] = expert_forward(
            me,
            received[m],
            expert_first_weight,
            expert_second_weight,
            first_other,
            second_other,
            first_bias,
            second_bias,
            [routed[-1][2] if m == 0 else expert_out[m - 1][0][0]],
        )
        returned[m] = exchanged(expert_out[m][0])
    for m in micros:
        merged[m] = call_kernel(
            functools.partial(
                merge_body, experts=experts, band_cols=band_cols, members=members
            ),
            "merge",
            [
                ((tokens // 4, 2 * channels), BF),
                ((tokens // 4, 4 * channels), BF),
                ((tokens // 4, 2 * channels), BF),
                ((tokens, channels), FL),
                ((tokens, LANES), BF),
                ((8, 2 * channels), FL),
            ]
            + [((block_rows, channels), BF)] * members,
            [
                *returned[m],
                dest_cols[m],
                dest_rows[m],
                chosen_cols[m],
                routed[m][2],
                routed[m][0],
                moe_small,
                weight_merge,
                merge_small,
                cotangent[m, 0].reshape(tokens // 4, 2 * channels),
            ],
            [
                ((tokens, channels), FL),
                ((tokens, channels), FL),
                ((tokens, LANES), FL),
                ((channels // LANES, tokens, LANES), FL),
                ((tokens, channels), BF),
            ],
            micros=14,
            after=[expert_out[-1][0][0] if m == 0 else merged[m - 1][0]],
        )
        outputs[m] = merged[m][0].reshape(band_rows // 2, band_cols // 2, 2 * channels)
        back_res[m] = exchanged(merged[m][6:])
    for m in micros:
        expert_back[m] = expert_backward(
            me,
            back_res[m],
            expert_first_weight,
            expert_second_weight,
            first_other,
            second_other,
            expert_out[m][2],
            [merged[-1][0] if m == 0 else expert_back[m - 1][2]],
        )
        back_sent[m] = exchanged(expert_back[m][0])

    def settle(m, after):
        return call_kernel(
            functools.partial(settle_body, members=members),
            "settle",
            [
                ((tokens, channels), FL),
                ((tokens, channels), BF),
                ((tokens, channels), BF),
                ((8, channels), FL),
            ],
            [
                *back_sent[m],
                dest_cols[m],
                merged[m][3],
                merged[m][4],
                weight_router,
                routed[m][1],
                routed[m][2],
                attn_small,
                weight_proj,
            ],
            micros=7,
            after=after,
        )

    grad_merge = merge_weight_grad(
        [b[1] for b in merged], [b[2] for b in merged], channels, [expert_back[-1][2]]
    )
    sum_merge, merge_steps = dense_sum(grad_merge)
    settled[0] = settle(0, [grad_merge])
    in_keep, in_send, _ = expert_weight_grads(
        me, received, [b[1] for b in expert_back], local, row_size, True, [settled[0][3]]
    )
    for m in micros[1:]:
        settled[m] = settle(m, [in_keep])
    out_keep, out_send, grad_eout_bias = expert_weight_grads(
        me, back_res, [b[1] for b in expert_out], local, row_size, False, [settled[-1][3]]
    )

    state = dict(
        first=dict(keep=in_keep, send=in_send), second=dict(keep=out_keep, send=out_send)
    )
    row_bits = list(reversed(bits_of("row")))
    latest = out_keep

    def transfer(kind):
        at = state[kind]
        step = at.setdefault("step", 0)
        if step < len(row_bits):
            at["got"] = crossed(at["send"], "row", row_bits[step])
        else:
            at["got"] = crossed(at["send"], "dp", members)

    def advance(kind):
        nonlocal latest
        at = state[kind]
        if at["step"] < len(row_bits):
            at["keep"], at["send"] = add_pieces(at["keep"], at["got"], [latest])
            latest = at["send"]
        else:
            at["held"] = spread_over_row(add_halves(at["keep"], at["got"], [latest]))
            latest = at["held"][0]
            return
        at["step"] += 1
        transfer(kind)

    transfer("first")
    transfer("second")
    plan = {
        "start": ["first"],
        (0, 1): ["first", "second"],
        (1, 0): ["first", "second"],
        "end": ["second"],
    }
    for _ in range(len(row_bits) - 2):
        plan[(0, 1)] = plan[(0, 1)] + ["first", "second"]

    def advance_at(place):
        for kind in plan.get(place, ()):
            advance(kind)

    advance_at("start")
    dense_args = []
    for m in micros:
        dense_args += [arrived[m], attended[m][0], settled[m][1], routed[m][3], merged[m][4]]
    grad_proj, grad_router = call_kernel(
        dense_body,
        "dense_weight_grads",
        [((channels, channels), BF), ((channels, LANES), BF)],
        dense_args,
        micros=4,
        after=[latest, merge_steps[0]],
    )
    latest = grad_router

    tile_after = {(0, 1): merge_steps[1:2], (1, 0): merge_steps[2:]}
    tile_sums = [None] * tile_count
    tile_smalls = [None] * tile_count
    weight_grads = [grad_proj, grad_router]
    for m in micros:
        lifted = passed_along(settled[m][2][:half], "row", -1)
        (back_windows,) = call_kernel(
            functools.partial(window_body, band_cols=band_cols, channels=channels),
            "window_grads",
            [((tokens, channels), BF)],
            [settled[m][2][half:], lifted],
            [grid_scratch, win_scratch],
            micros=3,
            after=[latest],
        )
        latest = back_windows
        win, qkv, inverse = attended[m][2:]
        last = m == micro_count - 1
        grads = []
        for t in range(tile_count):

            def part(array, rows, at):
                return (array, pl.BlockSpec((rows, LANES), lambda i, at=at: (0, at)))

            args = [
                part(back_windows, tokens, t),
                part(qkv, tokens, t),
                part(qkv, tokens, tile_count + t),
                part(qkv, tokens, 2 * tile_count + t),
                part(inverse, tokens, t),
                part(inverse, tokens, tile_count + t),
                part(scale_lanes, 1, t),
                win,
                (
                    bias_keys,
                    pl.BlockSpec((1,) + bias_shape[0][1:], lambda i, t=t: (t, 0, 0)),
                ),
                *zones[m],
                head_marks,
                block_ones,
            ]
            if m:
                args += tile_sums[t]
            dqkv, dweight, dbias, small = call_kernel(
                functools.partial(attend_backward_body, summed_before=m > 0),
                "attend_backward",
                [
                    ((tokens, 3 * LANES), BF),
                    ((channels, 3 * LANES), BF if last else FL),
                    (bias_shape[0][1:], FL),
                    ((8, LANES), FL),
                ],
                args,
                micros=10,
                after=[latest] + tile_after.get((m, t), []),
            )
            latest = small
            tile_sums[t] = [dweight, dbias]
            tile_smalls[t] = small if m == 0 else tile_smalls[t] + small
            grads.append(dqkv)
            if last:
                weight_grads.append(dweight)
                if t == tile_count - 2:
                    sum_first, _ = dense_sum(jnp.concatenate(weight_grads, 1))
                if t == tile_count - 1:
                    sum_last, last_steps = dense_sum(dweight)
            advance_at((m, t))
        if last:
            (lines,) = call_kernel(
                fold_body,
                "fold_bias",
                [((HEAD_COUNT, 8, SHEAR), FL)],
                [sums[1] for sums in tile_sums],
                micros=3,
                after=[latest],
            )
            latest = lines
        input_parts[m] = call_kernel(
            functools.partial(input_grad_body, band_cols=band_cols, channels=channels),
            "input_grad",
            [((half, channels), FL), ((half, channels), BF)],
            grads + [weight_qkv],
            [grid_scratch, win_scratch],
            micros=5,
            after=[latest],
        )
        latest = input_parts[m][1]
        passed = passed_along(input_parts[m][1], "row", 1).astype(FL)
        input_grads[m] = (
            (settled[m][0] + jnp.concatenate([passed, input_parts[m][0]], 0))
            .astype(BF)
            .reshape(band_rows, band_cols, channels)
        )
    advance_at("end")
    sum_ein = place_pieces(me, state["first"]["held"], local, hidden, True, [latest])
    sum_eout = place_pieces(me, state["second"]["held"], local, hidden, False, [])
    sum_proj = sum_first[:, :channels]
    sum_router = sum_first[:, channels : channels + experts]
    sum_qkv = jnp.concatenate([sum_first[:, channels + LANES :], sum_last], 1)
    sum_qkv = sum_qkv.reshape(-1, tile_count, 3, LANES).swapaxes(1, 2).reshape(-1, 3 * channels)

    settle_sums = sum(s[3] for s in settled)
    merge_sums = sum(b[5] for b in merged)
    dtable = table_of_lines(lines)
    attn_sums = jnp.concatenate(tile_smalls, 1)[:3]
    parts = [
        dtable,
        attn_sums,
        settle_sums[:3],
        merge_sums[:2],
        merge_sums[2:4, :channels],
    ]
    bias_parts = [sum(b[2] for b in expert_back), grad_eout_bias]
    flat = jnp.concatenate([part.reshape(-1) for part in parts])
    flat = jnp.pad(flat, (0, -flat.size % 1024)).reshape(-1, 1024)
    biases = jnp.concatenate([part.reshape(-1) for part in bias_parts])
    biases = jnp.pad(biases, (0, -biases.size % 1024)).reshape(-1, 1024)
    both = summed(jnp.concatenate([flat, biases], 0), ("row",))
    flat, biases = summed(both[: flat.shape[0]], ("dp",)).reshape(-1), both[flat.shape[0] :]
    found, at = [], 0
    for part in parts:
        found.append(flat[at : at + part.size].reshape(part.shape))
        at += part.size
    dtable, attn_sums, settle_sums, merge_sums, moe_sums = found
    biases = biases.reshape(-1)
    in_bias = biases[: 2 * local * hidden].reshape(2 * local, hidden)
    out_bias = biases[2 * local * hidden : 2 * local * (hidden + channels)]
    out_bias = out_bias.reshape(2 * local, channels)
    other_bias = crossed(
        jnp.concatenate([in_bias[local:], out_bias[local:]], 1), "dp", members
    )
    sum_ein_bias = in_bias[:local] + other_bias[:, :hidden]
    sum_eout_bias = out_bias[:local] + other_bias[:, hidden:]
    grad_first, grad_first_bias, grad_second = table_back(dtable)
    sum_qbias, sum_vbias, sum_scale = attn_sums[0], attn_sums[1], attn_sums[2, ::HEAD_DIM]
    sum_proj_bias, sum_again, sum_ashift = settle_sums[0], settle_sums[1], settle_sums[2]
    sum_rgain, sum_rshift = merge_sums[0], merge_sums[1]
    sum_mgain, sum_mshift = moe_sums[0], moe_sums[1]
    return (
        jnp.stack(outputs)[:, None],
        jnp.stack(input_grads)[:, None],
        sum_qkv,
        sum_qbias,
        sum_vbias,
        sum_scale,
        grad_first,
        grad_first_bias,
        grad_second,
        sum_proj,
        sum_proj_bias,
        sum_again,
        sum_ashift,
        sum_router,
        sum_ein,
        sum_ein_bias,
        sum_eout,
        sum_eout_bias,
        sum_mgain,
        sum_mshift,
        sum_merge,
        sum_rgain,
        sum_rshift,
    )


def solution(mesh):
    return jax.shard_map(
        on_device,
        mesh=mesh,
        in_specs=(
            P(None, "dp", "row", None, None),
            P(None, "dp", None),
            P(None, "dp", "row", None, None),
            P(None, "dp", "row", None, None),
            P("dp", None),
            P(),
            P(),
            P(),
            P(),
            P(),
            P(),
            P("dp", None),
            P(),
            P(),
            P(),
            P("dp", None),
            P("dp", None, None),
            P("dp", None),
            P("dp", None, None),
            P("dp", None),
            P(),
            P(),
            P("dp", None),
            P(),
            P(),
        ),
        out_specs=(
            P(None, "dp", "row", None, None),
            P(None, "dp", "row", None, None),
            P("dp", None),
            P(),
            P(),
            P(),
            P(),
            P(),
            P(),
            P("dp", None),
            P(),
            P(),
            P(),
            P("dp", None),
            P("dp", None, None),
            P("dp", None),
            P("dp", None, None),
            P("dp", None),
            P(),
            P(),
            P("dp", None),
            P(),
            P(),
        ),
        check_vma=False,
    )
```

```python
import functools

import jax
import jax.numpy as jnp
from jax import lax
from jax.experimental import pallas as pl
from jax.experimental.pallas import tpu as pltpu
from jax.sharding import PartitionSpec as P

HEAD_COUNT = 12
HEAD_DIM = 32
WINDOW_SIDE = 12
LANES = 128
SHEAR = 384
ZONES = 16
UNROLL = 2
COST_SCALE = 0.4
TILE_HEADS = LANES // HEAD_DIM


PRECISION_HIGH = lax.Precision.HIGHEST
EPS_NORM = 1e-05
EPS_UNIT = 1e-06
MASK_FILL = -100.0
BF = jnp.bfloat16
FL = jnp.float32
VMEM_BYTES = 52 * 2**20


def cost(micros):
    return pl.CostEstimate(
        flops=int(micros * COST_SCALE * 1.1e9), bytes_accessed=10**5, transcendentals=0
    )


def passed_along(array, axis, by):
    count = lax.axis_size(axis)
    return lax.ppermute(array, axis, [(i, (i + by) % count) for i in range(count)])


def exact_error_gelu(values):
    return jax.nn.gelu(values, approximate=False)


SPANS = 2 * WINDOW_SIDE - 1
AREA = WINDOW_SIDE * WINDOW_SIDE


def span_coordinate(steps):
    size = jnp.abs(steps) * (8.0 / (WINDOW_SIDE - 1))
    value = jnp.log2(size + 1.0) / 3.0
    return jnp.where(steps < 0, -value, value)


def bias_network(first_ref, second_ref):
    shape = (2 * SHEAR, 1)
    row = lax.broadcasted_iota(jnp.int32, shape, 0)
    below = row >= SHEAR
    place = jnp.where(below, row - SHEAR + 1, row - (WINDOW_SIDE - 1))
    held = jnp.clip(place, 0, SPANS * WINDOW_SIDE - 1)
    column = held % WINDOW_SIDE
    valid = (held == place) & (jnp.logical_not(below) | (column > 0))
    rows_apart = (held // WINDOW_SIDE - (WINDOW_SIDE - 1)).astype(FL)
    columns_apart = jnp.where(below, column - WINDOW_SIDE, column).astype(FL)
    down, across = span_coordinate(rows_apart), span_coordinate(columns_apart)
    pre = down * first_ref[0:1, :] + across * first_ref[1:2, :] + first_ref[2:3, :]
    cdf = 0.5 * (1.0 + lax.erf(pre * 0.7071067811865476))
    hidden = pre * cdf
    slope = cdf + pre * (0.3989422804014327 * jnp.exp(-0.5 * pre * pre))
    level = jax.nn.sigmoid(
        lax.dot_general(
            hidden,
            second_ref[...],
            (((1,), (0,)), ((), ())),
            precision=PRECISION_HIGH,
            preferred_element_type=FL,
        )
    )
    return down, across, valid, hidden, slope, level


def mask_operands(row_start, total_rows, total_cols, valid_rows, valid_cols):
    half_win = WINDOW_SIDE // 2
    rows_at = row_start + jnp.arange(WINDOW_SIDE)
    cols_at = jnp.arange(total_cols)
    row_zone = (rows_at >= total_rows - WINDOW_SIDE).astype(jnp.int32) + (
        rows_at >= total_rows - half_win
    ).astype(jnp.int32)
    col_zone = (cols_at >= total_cols - WINDOW_SIDE).astype(jnp.int32) + (
        cols_at >= total_cols - half_win
    ).astype(jnp.int32)
    zone_ids = 3 * row_zone[:, None] + col_zone[None, :]
    outside = ((rows_at + half_win) % total_rows >= valid_rows)[:, None] | (
        (cols_at + half_win) % total_cols >= valid_cols
    )[None, :]
    codes = zone_ids + jnp.where(outside, ZONES, 0)
    win_count = total_cols // WINDOW_SIDE
    codes = (
        codes.reshape(WINDOW_SIDE, win_count, WINDOW_SIDE)
        .transpose(1, 0, 2)
        .reshape(win_count, WINDOW_SIDE * WINDOW_SIDE)
    )
    zones, out = codes % ZONES, codes // ZONES
    mask = jnp.where(zones[:, :, None] != zones[:, None, :], MASK_FILL, 0.0) + jnp.where(
        out[:, None, :] > 0, MASK_FILL, 0.0
    )
    peak = jnp.max(mask, -1)[:, :, None]
    lane = jnp.arange(LANES)
    same = zones[:, :, None] == lane
    query = jnp.where(
        lane < ZONES,
        jnp.where(same, -MASK_FILL, 0.0),
        jnp.where(lane == ZONES, MASK_FILL, jnp.where(lane == ZONES + 1, MASK_FILL - peak, 0.0)),
    )
    key = jnp.where(
        lane < ZONES,
        jnp.where(same, 1.0, 0.0),
        jnp.where(lane == ZONES, out[:, :, None], jnp.where(lane == ZONES + 1, 1.0, 0.0)),
    )
    return (
        query.astype(BF).reshape(-1, LANES),
        key.astype(BF).reshape(-1, LANES),
    )


def plus(left, right):
    return left.astype(FL) + right.astype(FL)


def mm(left, right):
    return jnp.dot(left, right, preferred_element_type=FL)


def mm_nt(left, right):
    return lax.dot_general(left, right, (((1,), (1,)), ((), ())), preferred_element_type=FL)


def mm_tn(left, right):
    return lax.dot_general(left, right, (((0,), (0,)), ((), ())), preferred_element_type=FL)


def skipping(body, count, extra):
    def run(*refs):
        return body(*refs[:count], *refs[count + extra :])

    return run


def call_kernel(body, name, outs, args, scratch=(), micros=5, after=()):
    specs, arrays = [], []
    for arg in args:
        array, spec = arg if isinstance(arg, tuple) else (arg, None)
        if spec is None:
            spec = pl.BlockSpec(array.shape, lambda i, rank=array.ndim: (0,) * rank)
        specs.append(spec)
        arrays.append(array)
    return pl.pallas_call(
        skipping(body, len(args), len(after)),
        name=name,
        grid=(1,),
        out_shape=[jax.ShapeDtypeStruct(s, d) for s, d in outs],
        in_specs=specs + [pl.BlockSpec(memory_space=pl.ANY)] * len(after),
        out_specs=[pl.BlockSpec(s, lambda i, rank=len(s): (0,) * rank) for s, _ in outs],
        scratch_shapes=[pltpu.VMEM(s, d) for s, d in scratch],
        compiler_params=pltpu.CompilerParams(vmem_limit_bytes=VMEM_BYTES),
        cost_estimate=cost(micros),
    )(*arrays, *after)


def rows_at(start, size):
    return pl.ds(pl.multiple_of(start, 16), size)


def head_sums(values, block_ones):
    high = values.astype(BF)
    rest = (values - high.astype(FL)).astype(BF)
    return mm(jnp.concatenate([high, rest], 1), block_ones)


def tiles_of(channels):
    return [slice(LANES * t, LANES * (t + 1)) for t in range(channels // LANES)]


def to_windows(sources, grid_ref, win_ref, band_cols, channels):
    half_win = WINDOW_SIDE // 2
    pitch = band_cols + 8
    win_area = WINDOW_SIDE * WINDOW_SIDE
    for i in range(WINDOW_SIDE):
        value = sources(i).astype(FL)
        for t, lanes in enumerate(tiles_of(channels)):
            grid_ref[t, i * pitch : i * pitch + band_cols, :] = value[:, lanes]
            grid_ref[t, i * pitch + band_cols : (i + 1) * pitch, :] = value[0:8, lanes]
    for t in range(channels // LANES):
        for n in range(band_cols // WINDOW_SIDE):
            for i in range(WINDOW_SIDE):
                at = i * pitch + n * WINDOW_SIDE + half_win
                to = n * win_area + i * WINDOW_SIDE
                win_ref[t, to : to + WINDOW_SIDE, :] = grid_ref[t, at : at + WINDOW_SIDE, :]


def from_windows(put, grid_ref, win_ref, band_cols, channels):
    half_win = WINDOW_SIDE // 2
    pitch = band_cols + 8
    win_area = WINDOW_SIDE * WINDOW_SIDE
    for t in range(channels // LANES):
        for n in range(band_cols // WINDOW_SIDE):
            for i in range(WINDOW_SIDE):
                to = i * pitch + n * WINDOW_SIDE + half_win
                at = n * win_area + i * WINDOW_SIDE
                grid_ref[t, to : to + WINDOW_SIDE, :] = win_ref[t, at : at + WINDOW_SIDE, :]
        for i in range(WINDOW_SIDE):
            grid_ref[t, i * pitch : i * pitch + half_win, :] = grid_ref[
                t, i * pitch + band_cols : i * pitch + band_cols + half_win, :
            ]
    for i in range(WINDOW_SIDE):
        put(
            i,
            jnp.concatenate(
                [
                    grid_ref[t, i * pitch : i * pitch + band_cols, :]
                    for t in range(channels // LANES)
                ],
                1,
            ),
        )


def stacked(tile, heads_ref):
    return jnp.concatenate([tile] * TILE_HEADS, 0) * heads_ref[...]


def spread_body(first_ref, second_ref, rows_ref, keys_ref):
    row = lax.broadcasted_iota(jnp.int32, (AREA, AREA), 0) % WINDOW_SIDE
    lane = lax.broadcasted_iota(jnp.int32, (AREA, AREA), 1) % WINDOW_SIDE
    *_, level = bias_network(first_ref, second_ref)
    wide = jnp.concatenate([16.0 * level, jnp.zeros((2 * SHEAR, LANES - HEAD_COUNT), FL)], 1)
    lines = wide.T

    def shear(line):
        wide = pltpu.roll(jnp.broadcast_to(line, (AREA, SHEAR)), SHEAR - (AREA - 1), 1)
        return pltpu.roll(wide, 0, 1, stride=1, stride_axis=0)[:, 0:AREA]

    for t in range(rows_ref.shape[0]):
        rows, keys = [], []
        for k in range(TILE_HEADS):
            line = lines[t * TILE_HEADS + k : t * TILE_HEADS + k + 1]
            key = jnp.where(lane >= row, shear(line[:, :SHEAR]), shear(line[:, SHEAR:]))
            keys.append(key)
            rows.append(key.T)
        rows_ref[t] = jnp.concatenate(rows, 1)
        keys_ref[t] = jnp.concatenate(keys, 1)


LINE_ROWS = 2 * HEAD_COUNT
ATTN_AT = LINE_ROWS
SETTLE_AT = ATTN_AT + 3
MERGE_AT = SETTLE_AT + 3
SUM_ROWS = 40


def fold_body(*refs, tile_count, micro_count):
    dbias_refs, attn_refs, settle_refs, merge_refs, dpre_refs, (dout_ref, out_ref) = taken(
        refs, tile_count, tile_count * micro_count, micro_count, micro_count, micro_count
    )
    row = lax.broadcasted_iota(jnp.int32, (AREA, AREA), 0)
    lane = lax.broadcasted_iota(jnp.int32, (AREA, AREA), 1)
    turn = jnp.where(row + lane == AREA - 1, 1.0, 0.0).astype(BF)
    later = lane % WINDOW_SIDE >= (AREA - 1 - row) % WINDOW_SIDE
    blank = jnp.zeros((AREA, SHEAR - AREA), FL)

    def fold(values):
        wide = jnp.concatenate([values, blank], 1)
        return jnp.sum(pltpu.roll(wide, 0, 1, stride=1, stride_axis=0), 0, keepdims=True)

    channels = out_ref.shape[1]
    out_ref[...] = jnp.zeros_like(out_ref)
    for t, ref in enumerate(dbias_refs):
        values = ref[...]
        for k in range(TILE_HEADS):
            value = values[:, k * AREA : (k + 1) * AREA]
            total = None
            for _ in range(3):
                part = value.astype(BF)
                value = value - part.astype(FL)
                now = mm(turn, part)
                total = now if total is None else total + now
            head = t * TILE_HEADS + k
            out_ref[head : head + 1, :] = fold(jnp.where(later, total, 0.0))
            at = HEAD_COUNT + head
            out_ref[at : at + 1, :] = fold(jnp.where(later, 0.0, total))
        lanes = slice(t * LANES, (t + 1) * LANES)
        out_ref[ATTN_AT : ATTN_AT + 3, lanes] = sum(
            attn_refs[m * tile_count + t][0:3, :] for m in range(micro_count)
        )
    out_ref[SETTLE_AT : SETTLE_AT + 3, :] = sum(ref[0:3, :] for ref in settle_refs)
    merge = sum(ref[0:4, :] for ref in merge_refs)
    for k, (at, half) in enumerate(((0, 0), (0, 1), (1, 0), (1, 1), (2, 0), (3, 0))):
        out_ref[MERGE_AT + k : MERGE_AT + k + 1, :] = merge[
            at : at + 1, half * channels : (half + 1) * channels
        ]
    experts, _, hidden = dpre_refs[0].shape
    chunks = hidden // channels
    for e in range(experts):
        total = sum(ref[e] for ref in dpre_refs)
        for c in range(chunks):
            at = SUM_ROWS + e * chunks + c
            out_ref[at : at + 1, :] = total[:, c * channels : (c + 1) * channels]
        at = SUM_ROWS + experts * chunks + e
        out_ref[at : at + 1, :] = dout_ref[e]


def bias_network_back_body(sums_ref, first_ref, second_ref, dfirst_ref, dsecond_ref):
    down, across, valid, hidden, slope, level = bias_network(first_ref, second_ref)
    lines = jnp.concatenate(
        [sums_ref[0:HEAD_COUNT, :], sums_ref[HEAD_COUNT : 2 * HEAD_COUNT, :]], 1
    )
    lines = jnp.concatenate([lines, jnp.zeros((LANES - HEAD_COUNT, 2 * SHEAR), FL)], 0)
    grad = lines.T[:, 0:HEAD_COUNT]
    grad = jnp.where(valid, grad * 16.0 * level * (1.0 - level), 0.0)
    dsecond_ref[...] = lax.dot_general(
        hidden,
        grad,
        (((0,), (0,)), ((), ())),
        precision=PRECISION_HIGH,
        preferred_element_type=FL,
    )
    dpre = slope * lax.dot_general(
        grad,
        second_ref[...],
        (((1,), (1,)), ((), ())),
        precision=PRECISION_HIGH,
        preferred_element_type=FL,
    )
    dfirst_ref[0:1, :] = jnp.sum(down * dpre, 0, keepdims=True)
    dfirst_ref[1:2, :] = jnp.sum(across * dpre, 0, keepdims=True)
    dfirst_ref[2:3, :] = jnp.sum(dpre, 0, keepdims=True)


def slot_body(
    place_ref,
    experts_ref,
    column_ref,
    dest_column_ref,
    dest_row_ref,
    *,
    experts,
    local,
    slots,
    capacity,
):
    tokens = experts_ref.shape[1]

    def place(expert):
        upper = jnp.where(expert >= experts // 2, 1, 0)
        inner = expert - upper * (experts // 2)
        apart = upper ^ place_ref[0]
        member = (inner // local) ^ place_ref[1]
        return ((2 * member + apart) * local + inner % local) * slots

    block = LANES
    lower = (
        lax.broadcasted_iota(jnp.int32, (block, block), 0)
        > lax.broadcasted_iota(jnp.int32, (block, block), 1)
    ).astype(FL).astype(BF)
    upper = (
        lax.broadcasted_iota(jnp.int32, (block, block), 0)
        < lax.broadcasted_iota(jnp.int32, (block, block), 1)
    ).astype(FL).astype(BF)
    lane = lax.broadcasted_iota(jnp.int32, (block, LANES), 1)
    sublane = lax.broadcasted_iota(jnp.int32, (LANES, block), 0)
    seen_row = jnp.zeros((1, LANES), FL)
    seen_column = jnp.zeros((LANES, 1), FL)
    for c in range(tokens // block):
        line = experts_ref[:, c * block : (c + 1) * block]
        across = jnp.where(sublane == line, 1.0, 0.0)
        column = jnp.broadcast_to(line.astype(FL), (block, block)).T[:, 0:1].astype(jnp.int32)
        down = jnp.where(lane == column, 1.0, 0.0)
        before = mm(lower, down.astype(BF)) + seen_row
        slot = jnp.sum(down * before, 1, keepdims=True).astype(jnp.int32)
        column_ref[c * block : (c + 1) * block, :] = column
        dest_column_ref[c * block : (c + 1) * block, :] = jnp.where(
            slot < capacity, place(column) + slot, -1
        )
        before = mm(across.astype(BF), upper) + seen_column
        slot = jnp.sum(across * before, 0, keepdims=True).astype(jnp.int32)
        dest_row_ref[:, c * block : (c + 1) * block] = jnp.where(
            slot < capacity, place(line) + slot, -1
        )
        seen_row = seen_row + jnp.sum(down, 0, keepdims=True)
        seen_column = seen_column + jnp.sum(across, 1, keepdims=True)


def slot_tables(chosen, my_place, experts, local, slots, capacity, after):
    tokens = chosen.shape[1]
    vmem = pl.BlockSpec(memory_space=pltpu.VMEM)
    column = jax.ShapeDtypeStruct((tokens, 1), jnp.int32)
    return pl.pallas_call(
        skipping(
            functools.partial(
                slot_body, experts=experts, local=local, slots=slots, capacity=capacity
            ),
            2,
            1,
        ),
        name="slot_tables",
        in_specs=[
            pl.BlockSpec(memory_space=pltpu.SMEM),
            vmem,
            pl.BlockSpec(memory_space=pl.ANY),
        ],
        out_specs=[vmem] * 3,
        out_shape=[column, column, jax.ShapeDtypeStruct((1, tokens), jnp.int32)],
        cost_estimate=cost(3),
    )(my_place, chosen, after)


def attend_forward_body(
    band_ref,
    below_ref,
    weight_ref,
    qbias_ref,
    vbias_ref,
    scale_ref,
    bias_ref,
    query_zone_ref,
    key_zone_ref,
    heads_ref,
    block_ref,
    own_ref,
    send_ref,
    win_ref,
    qkv_ref,
    inv_ref,
    grid_scr,
    win_scr,
    *,
    band_cols,
    channels,
):
    tokens = band_ref.shape[0]
    half = tokens // 2
    win_area = WINDOW_SIDE * WINDOW_SIDE
    tiles = tiles_of(channels)

    def source(i):
        if i < WINDOW_SIDE // 2:
            return band_ref[half + i * band_cols : half + (i + 1) * band_cols, :]
        at = (i - WINDOW_SIDE // 2) * band_cols
        return below_ref[at : at + band_cols, :]

    to_windows(source, grid_scr, win_scr, band_cols, channels)
    block_ones = block_ref[...]
    chunk = 2 * win_area

    def project(c, carry):
        rows = rows_at(c * chunk, chunk)
        low = jnp.concatenate([win_scr[t, rows, :] for t in range(len(tiles))], 1).astype(BF)
        win_ref[rows, :] = low
        qkv = mm(low, weight_ref[...])
        for lanes in tiles:
            key_lanes = slice(channels + lanes.start, channels + lanes.stop)
            value_lanes = slice(2 * channels + lanes.start, 2 * channels + lanes.stop)
            query = qkv[:, lanes] + qbias_ref[:, lanes]
            inverse = (
                lax.rsqrt(head_sums(query * query, block_ones) + EPS_UNIT) * scale_ref[:, lanes]
            )
            inv_ref[rows, lanes] = inverse
            qkv_ref[rows, lanes] = (query * inverse).astype(BF)
            key = qkv[:, key_lanes]
            inverse = lax.rsqrt(head_sums(key * key, block_ones) + EPS_UNIT)
            inv_ref[rows, key_lanes] = inverse
            qkv_ref[rows, key_lanes] = (key * inverse).astype(BF)
            qkv_ref[rows, value_lanes] = (qkv[:, value_lanes] + vbias_ref[:, lanes]).astype(BF)
        return carry

    lax.fori_loop(0, tokens // chunk, project, 0)

    def attend(n, carry):
        rows = rows_at(n * win_area, win_area)
        query_zone = query_zone_ref[rows, :]
        key_zone = jnp.concatenate([key_zone_ref[rows, :]] * TILE_HEADS, 0)
        for t, lanes in enumerate(tiles):
            query = qkv_ref[rows, lanes]
            key = qkv_ref[rows, channels + lanes.start : channels + lanes.stop]
            value = qkv_ref[rows, 2 * channels + lanes.start : 2 * channels + lanes.stop]
            scores = mm_nt(
                jnp.concatenate([query, query_zone], 1),
                jnp.concatenate([stacked(key, heads_ref), key_zone], 1),
            )
            powers = jnp.exp(scores + bias_ref[t]).astype(BF)
            mixed = mm(powers, jnp.concatenate([stacked(value, heads_ref), heads_ref[...]], 1))
            win_scr[t, rows, :] = mixed[:, :LANES] / mixed[:, LANES:]
        return carry

    lax.fori_loop(0, tokens // win_area, attend, 0, unroll=UNROLL)

    def put(i, value):
        if i < WINDOW_SIDE // 2:
            own_ref[i * band_cols : (i + 1) * band_cols, :] = value.astype(BF)
        else:
            at = (i - WINDOW_SIDE // 2) * band_cols
            send_ref[at : at + band_cols, :] = value.astype(BF)

    from_windows(put, grid_scr, win_scr, band_cols, channels)


def window_body(own_ref, lifted_ref, out_ref, grid_scr, win_scr, *, band_cols, channels):
    def source(i):
        ref = own_ref if i < WINDOW_SIDE // 2 else lifted_ref
        at = (i % (WINDOW_SIDE // 2)) * band_cols
        return ref[at : at + band_cols, :]

    to_windows(source, grid_scr, win_scr, band_cols, channels)
    for t, lanes in enumerate(tiles_of(channels)):
        out_ref[:, lanes] = win_scr[t].astype(BF)


def attend_backward_body(*refs, summed_before):
    (
        back_ref,
        query_ref,
        key_ref,
        value_ref,
        query_inv_ref,
        key_inv_ref,
        scale_ref,
        win_ref,
        bias_ref,
        query_zone_ref,
        key_zone_ref,
        heads_ref,
        block_ref,
        *rest,
    ) = refs
    if summed_before:
        dweight_before_ref, dbias_before_ref, *rest = rest
    dqkv_ref, dweight_ref, dbias_ref, small_ref = rest
    tokens = back_ref.shape[0]
    win_area = WINDOW_SIDE * WINDOW_SIDE
    block_ones = block_ref[...]
    if summed_before:
        dbias_ref[...] = dbias_before_ref[...]
    else:
        dbias_ref[...] = jnp.zeros_like(dbias_ref)
    small_ref[...] = jnp.zeros_like(small_ref)

    def attend(n, carry):
        rows = rows_at(n * win_area, win_area)
        query = query_ref[rows, :]
        key = key_ref[rows, :]
        queries = stacked(query, heads_ref)
        backs = stacked(back_ref[rows, :], heads_ref)
        query_zone = jnp.concatenate([query_zone_ref[rows, :]] * TILE_HEADS, 0)
        scores = mm_nt(
            jnp.concatenate([key, key_zone_ref[rows, :]], 1),
            jnp.concatenate([queries, query_zone], 1),
        )
        powers = jnp.exp(scores + bias_ref[0])
        probs = powers * (1.0 / jnp.sum(powers, 0, keepdims=True))
        weighted = probs * mm_nt(value_ref[rows, :], backs)
        dscores = weighted - probs * jnp.sum(weighted, 0, keepdims=True)
        dbias_ref[...] += dscores
        dlow = dscores.astype(BF)
        dvalue = mm(probs.astype(BF), backs)
        dkey = mm(dlow, queries)
        dquery = mm_tn(dlow, key) * heads_ref[...].astype(FL)
        dquery = sum(dquery[k * win_area : (k + 1) * win_area] for k in range(TILE_HEADS))
        scale = scale_ref[...]
        unit = query.astype(FL)
        along = head_sums(unit * dquery, block_ones)
        dquery = query_inv_ref[rows, :] * (dquery - unit * along / (scale * scale))
        unit = key.astype(FL)
        dkey = key_inv_ref[rows, :] * (dkey - unit * head_sums(unit * dkey, block_ones))
        for part, grad in enumerate((dquery, dkey, dvalue)):
            dqkv_ref[rows, part * LANES : (part + 1) * LANES] = grad.astype(BF)
        small_ref[0:1, :] += jnp.sum(dquery, 0, keepdims=True)
        small_ref[1:2, :] += jnp.sum(dvalue, 0, keepdims=True)
        small_ref[2:3, :] += jnp.sum(along, 0, keepdims=True)
        return carry

    lax.fori_loop(0, tokens // win_area, attend, 0, unroll=UNROLL)
    dweight = mm_tn(win_ref[...], dqkv_ref[...])
    if summed_before:
        dweight = dweight + dweight_before_ref[...]
    dweight_ref[...] = dweight.astype(dweight_ref.dtype)


def input_grad_body(
    first_ref,
    second_ref,
    third_ref,
    weight_ref,
    own_ref,
    send_ref,
    grid_scr,
    win_scr,
    *,
    band_cols,
    channels,
):
    tokens = first_ref.shape[0]
    tiles = tiles_of(channels)
    chunk = 2 * WINDOW_SIDE * WINDOW_SIDE

    def project(c, carry):
        rows = rows_at(c * chunk, chunk)
        parts = [ref[rows, :] for ref in (first_ref, second_ref, third_ref)]
        wide = jnp.concatenate([p[:, lanes] for lanes in tiles for p in parts], 1)
        back = mm_nt(wide, weight_ref[...])
        for t, lanes in enumerate(tiles):
            win_scr[t, rows, :] = back[:, lanes]
        return carry

    lax.fori_loop(0, tokens // chunk, project, 0)

    def put(i, value):
        if i < WINDOW_SIDE // 2:
            own_ref[i * band_cols : (i + 1) * band_cols, :] = value
        else:
            at = (i - WINDOW_SIDE // 2) * band_cols
            send_ref[at : at + band_cols, :] = value.astype(BF)

    from_windows(put, grid_scr, win_scr, band_cols, channels)


def lane_mean(values):
    return jnp.sum(values, -1, keepdims=True) * (1.0 / values.shape[-1])


def normalised(values):
    centred = values - lane_mean(values)
    inverse = lax.rsqrt(lane_mean(centred * centred) + EPS_NORM)
    return centred * inverse, inverse


def normalised_back(back, gain, unit, inverse):
    back = back * gain
    return inverse * (back - lane_mean(back) - unit * lane_mean(back * unit))


CHUNK = 576


def pack_rows(dest_row_ref, rows_ref, out_refs):
    tokens = rows_ref.shape[0]
    start = 0
    for ref in out_refs:
        place = lax.broadcasted_iota(jnp.int32, (ref.shape[0], tokens), 0) + start
        chosen = jnp.where(place == dest_row_ref[...], 1.0, 0.0).astype(BF)
        ref[...] = mm(chosen, rows_ref[...]).astype(BF)
        start += ref.shape[0]


def unpack_rows(dest_col, buffer):
    place = lax.broadcasted_iota(jnp.int32, (dest_col.shape[0], buffer.shape[0]), 1)
    chosen = jnp.where(place == dest_col, 1.0, 0.0).astype(BF)
    return mm(chosen, buffer)


def route_body(
    arrived_ref,
    own_ref,
    band_ref,
    weight_ref,
    small_ref,
    router_ref,
    expert_ref,
    dest_row_ref,
    resid_ref,
    unit_ref,
    aux_ref,
    low_ref,
    *sent_refs,
    experts,
):
    half = arrived_ref.shape[0]
    lane = lax.broadcasted_iota(jnp.int32, (CHUNK, LANES), 1)
    for part, ref in enumerate((arrived_ref, own_ref)):

        def step(c, carry, part=part, ref=ref):
            rows = rows_at(part * half + c * CHUNK, CHUNK)
            projected = mm(ref[rows_at(c * CHUNK, CHUNK), :], weight_ref[...]) + small_ref[0:1, :]
            unit, inverse = normalised(projected)
            unit_ref[rows, :] = unit.astype(BF)
            resid = band_ref[rows, :].astype(FL) + unit * small_ref[1:2, :] + small_ref[2:3, :]
            resid_ref[rows, :] = resid
            low = resid.astype(BF)
            low_ref[rows, :] = low
            logits = jnp.where(lane < experts, mm(low, router_ref[...]), -1e30)
            powers = jnp.exp(logits - jnp.max(logits, -1, keepdims=True))
            probs = powers / jnp.sum(powers, -1, keepdims=True)
            gate = jnp.sum(
                jnp.where(lane == expert_ref[rows, :], probs, 0.0), -1, keepdims=True
            )
            aux_ref[rows, :] = jnp.where(
                lane == LANES - 1, gate, jnp.where(lane == LANES - 2, inverse, probs)
            )
            return carry

        lax.fori_loop(0, half // CHUNK, step, 0)
    pack_rows(dest_row_ref, low_ref, sent_refs)


def merge_body(*refs, experts, band_cols, members):
    returned_refs, refs = refs[:members], refs[members:]
    (
        dest_col_ref,
        dest_row_ref,
        expert_ref,
        aux_ref,
        resid_ref,
        small_ref,
        weight_ref,
        wide_ref,
        cotangent_ref,
        final_ref,
        merged_ref,
        dreduced_ref,
        dresid_ref,
        dlogits_ref,
        sums_ref,
    ) = refs[:15]
    sent_refs = refs[15 : 15 + members]
    unit_scr, picked_scr, inverse_scr, token_scr, back_scr = refs[15 + members :]
    returned = jnp.concatenate([ref[...] for ref in returned_refs], 0)
    tokens, channels = resid_ref.shape
    tiles = tiles_of(channels)
    lane = lax.broadcasted_iota(jnp.int32, (CHUNK, LANES), 1)

    def combine(c, carry):
        rows = rows_at(c * CHUNK, CHUNK)
        picked = unpack_rows(dest_col_ref[rows, :], returned)
        picked_scr[rows, :] = picked
        gate = aux_ref[rows, :][:, LANES - 1 : LANES]
        unit, inverse = normalised(gate * picked)
        unit_scr[rows, :] = unit
        inverse_scr[rows, :] = jnp.broadcast_to(inverse, (CHUNK, LANES))
        resid = resid_ref[rows, :] + unit * small_ref[0:1, :] + small_ref[1:2, :]
        for t, lanes in enumerate(tiles):
            token_scr[t, rows, :] = resid[:, lanes]
        return carry

    lax.fori_loop(0, tokens // CHUNK, combine, 0)
    pairs = band_cols // 2
    for i in range(WINDOW_SIDE // 2):
        for k in range(4):
            start = (2 * i + k % 2) * band_cols + k // 2
            for t in range(len(tiles)):
                at = k * channels + t * LANES
                merged_ref[i * pairs : (i + 1) * pairs, at : at + LANES] = token_scr[
                    t, pl.ds(start, pairs, stride=2), :
                ].astype(BF)
    unit, inverse = normalised(mm(merged_ref[...], weight_ref[...]))
    final_ref[...] = (unit * wide_ref[0:1, :] + wide_ref[1:2, :]).astype(BF)
    back = cotangent_ref[...].astype(FL)
    sums_ref[...] = jnp.zeros_like(sums_ref)
    sums_ref[0:1, :] = jnp.sum(back * unit, 0, keepdims=True)
    sums_ref[1:2, :] = jnp.sum(back, 0, keepdims=True)
    dreduced = normalised_back(back, wide_ref[0:1, :], unit, inverse).astype(BF)
    dreduced_ref[...] = dreduced
    for k in range(4):
        part = mm_nt(dreduced, weight_ref[k * channels : (k + 1) * channels, :])
        for i in range(WINDOW_SIDE // 2):
            start = (2 * i + k % 2) * band_cols + k // 2
            for t, lanes in enumerate(tiles):
                token_scr[t, pl.ds(start, pairs, stride=2), :] = part[
                    i * pairs : (i + 1) * pairs, lanes
                ]

    def spread(c, carry):
        rows = rows_at(c * CHUNK, CHUNK)
        back = jnp.concatenate([token_scr[t, rows, :] for t in range(len(tiles))], 1)
        dresid_ref[rows, :] = back
        unit = unit_scr[rows, :]
        sums_ref[2:3, 0:channels] += jnp.sum(back * unit, 0, keepdims=True)
        sums_ref[3:4, 0:channels] += jnp.sum(back, 0, keepdims=True)
        back = normalised_back(back, small_ref[0:1, :], unit, inverse_scr[rows, :][:, 0:1])
        aux = aux_ref[rows, :]
        gate = aux[:, LANES - 1 : LANES]
        dgate = jnp.sum(back * picked_scr[rows, :], -1, keepdims=True)
        back_scr[rows, :] = (back * gate).astype(BF)
        probs = jnp.where(lane < experts, aux, 0.0)
        chosen = jnp.where(lane == expert_ref[rows, :], 1.0, 0.0)
        dlogits_ref[rows, :] = (probs * (chosen - gate) * dgate).astype(BF)
        return carry

    lax.fori_loop(0, tokens // CHUNK, spread, 0)
    pack_rows(dest_row_ref, back_scr, sent_refs)


def settle_body(*refs, members):
    sent_refs, refs = refs[:members], refs[members:]
    (
        dest_col_ref,
        dresid_ref,
        dlogits_ref,
        router_ref,
        unit_ref,
        aux_ref,
        small_ref,
        weight_ref,
        done_ref,
        low_ref,
        rows_ref,
        sums_ref,
    ) = refs
    sent = jnp.concatenate([ref[...] for ref in sent_refs], 0)
    tokens, channels = dresid_ref.shape
    sums_ref[...] = jnp.zeros_like(sums_ref)

    def step(c, carry):
        rows = rows_at(c * CHUNK, CHUNK)
        back = dresid_ref[rows, :] + unpack_rows(dest_col_ref[rows, :], sent)
        back = back + mm_nt(dlogits_ref[rows, :], router_ref[...])
        done_ref[rows, :] = back
        unit = unit_ref[rows, :].astype(FL)
        sums_ref[1:2, :] += jnp.sum(back * unit, 0, keepdims=True)
        sums_ref[2:3, :] += jnp.sum(back, 0, keepdims=True)
        inverse = aux_ref[rows, :][:, LANES - 2 : LANES - 1]
        back = normalised_back(back, small_ref[1:2, :], unit, inverse)
        sums_ref[0:1, :] += jnp.sum(back, 0, keepdims=True)
        low = back.astype(BF)
        low_ref[rows, :] = low
        rows_ref[rows, :] = mm_nt(low, weight_ref[...]).astype(BF)
        return carry

    lax.fori_loop(0, tokens // CHUNK, step, 0)


def dense_body(*refs):
    (*ins, proj_ref, router_ref) = refs
    arrived, own, low, resid, dlogits = (ins[i::5] for i in range(5))
    half = arrived[0].shape[0]
    proj = router = None
    for a, o, b, r, d in zip(arrived, own, low, resid, dlogits):
        now = mm_tn(a[...], b[0:half, :]) + mm_tn(o[...], b[half:, :])
        then = mm_tn(r[...], d[...])
        proj = now if proj is None else proj + now
        router = then if router is None else router + then
    proj_ref[...] = proj.astype(BF)
    router_ref[...] = router.astype(BF)


def merge_weight_body(*refs):
    (*ins, out_ref) = refs
    total = None
    for left, right in zip(ins[0::2], ins[1::2]):
        now = mm_tn(left[...], right[...])
        total = now if total is None else total + now
    out_ref[...] = total.astype(BF)


def merge_weight_grad(merged, dreduced, channels, after):
    args, specs = [], []
    for left, right in zip(merged, dreduced):
        args += [left, right]
        specs += [
            pl.BlockSpec((left.shape[0], channels), lambda k: (0, k)),
            pl.BlockSpec(right.shape, lambda k: (0, 0)),
        ]
    return pl.pallas_call(
        skipping(merge_weight_body, len(args), len(after)),
        name="merge_weight_grad",
        grid=(4,),
        out_shape=jax.ShapeDtypeStruct((merged[0].shape[1], dreduced[0].shape[1]), BF),
        in_specs=specs + [pl.BlockSpec(memory_space=pl.ANY)] * len(after),
        out_specs=pl.BlockSpec((channels, dreduced[0].shape[1]), lambda k: (k, 0)),
        compiler_params=pltpu.CompilerParams(vmem_limit_bytes=VMEM_BYTES),
        cost_estimate=cost(5),
    )(*args, *after)


PIECE = 384


def spot_of(member, me, bits):
    apart = member ^ me
    spot = 0
    for k in range(bits):
        spot = spot | (((apart >> k) & 1) << (bits - 1 - k))
    return spot


def piece_home(expert, chunk, row_size, chunks):
    piece = expert * chunks + chunk
    return piece % row_size, piece // row_size


def expert_weight(own, other_refs, expert, chunk, local, chunks, me):
    row_size = len(other_refs)
    member, _ = piece_home(jnp.maximum(expert - local, 0), chunk, row_size, chunks)
    spot = spot_of(member, me, row_size.bit_length() - 1)
    weight = own
    for k, ref in enumerate(other_refs):
        weight = jnp.where((expert >= local) & (spot == k), ref[0], weight)
    return weight


def taken(refs, *counts):
    lists = []
    for count in counts:
        lists.append(refs[:count])
        refs = refs[count:]
    return lists + [refs]


def joined(refs):
    return jnp.concatenate([ref[...] for ref in refs], 0)


def put_parts(refs, value):
    start = 0
    for ref in refs:
        ref[...] = value[start : start + ref.shape[0]].astype(BF)
        start += ref.shape[0]


def expert_forward_body(me_ref, *refs, local, members, row_size):
    row_refs, (in_ref, in_bias_ref, out_ref, out_bias_ref), in_others, out_others, refs = taken(
        refs, members, 4, row_size, row_size
    )
    result_refs, (hidden_ref, slope_ref, pre_scr) = taken(refs, members)
    expert = pl.program_id(0)
    rows = joined(row_refs)
    count = rows.shape[0]
    chunks = in_ref.shape[2] // PIECE
    block = 64
    total = None
    for chunk in range(chunks):
        lanes = slice(chunk * PIECE, (chunk + 1) * PIECE)
        weight = expert_weight(
            in_ref[0, :, lanes], in_others, expert, chunk, local, chunks, me_ref[0]
        )
        pre_scr[...] = mm(rows, weight) + in_bias_ref[0, :, lanes]

        def activate(c, carry, lanes=lanes):
            at = rows_at(c * block, block)
            pre = pre_scr[at, :]
            cdf = 0.5 * (1.0 + lax.erf(pre * 0.7071067811865476))
            hidden_ref[0, at, lanes] = (pre * cdf).astype(BF)
            slope_ref[0, at, lanes] = (
                cdf + pre * (0.3989422804014327 * jnp.exp(-0.5 * pre * pre))
            ).astype(BF)
            return carry

        lax.fori_loop(0, count // block, activate, 0)
        weight = expert_weight(
            out_ref[0, lanes, :], out_others, expert, chunk, local, chunks, me_ref[0]
        )
        now = mm(hidden_ref[0, :, lanes], weight)
        total = now if total is None else total + now
    put_parts(result_refs, total + out_bias_ref[0])


def expert_specs(members, slots, channels, hidden, local, row_size):
    chunks = hidden // PIECE

    def other_at(k, me):
        return (jnp.maximum(k - local, 0) * chunks // row_size, 0, 0)

    def own_at(k, me):
        return (jnp.minimum(k, local - 1), 0, 0)

    return dict(
        tokens=pl.BlockSpec((slots, channels), lambda k, me: (k, 0)),
        wide=pl.BlockSpec((1, members * slots, hidden), lambda k, me: (k, 0, 0)),
        first=pl.BlockSpec((1, channels, hidden), own_at),
        second=pl.BlockSpec((1, hidden, channels), own_at),
        other=pl.BlockSpec((1, PIECE, PIECE), other_at),
        bias=pl.BlockSpec((1, 1, hidden), lambda k, me: (k, 0, 0)),
        low_bias=pl.BlockSpec((1, 1, channels), lambda k, me: (k, 0, 0)),
    )


def call_expert(
    body, name, me, steps, in_specs, out_specs, outs, scratch, args, micros, after=()
):
    return pl.pallas_call(
        skipping(body, 1 + len(args), len(after)),
        name=name,
        grid_spec=pltpu.PrefetchScalarGridSpec(
            num_scalar_prefetch=1,
            grid=(steps,),
            in_specs=in_specs + [pl.BlockSpec(memory_space=pl.ANY)] * len(after),
            out_specs=out_specs,
            scratch_shapes=scratch,
        ),
        out_shape=outs,
        compiler_params=pltpu.CompilerParams(vmem_limit_bytes=VMEM_BYTES),
        cost_estimate=cost(micros),
    )(me, *args, *after)


def expert_forward(
    me, rows, first, second, first_other, second_other, first_bias, second_bias, after
):
    members, row_size = len(rows), len(first_other)
    local, channels, hidden = first.shape
    slots = rows[0].shape[0] // (2 * local)
    count = members * slots
    spec = expert_specs(members, slots, channels, hidden, local, row_size)
    wide = jax.ShapeDtypeStruct((2 * local, count, hidden), BF)
    outs = call_expert(
        functools.partial(
            expert_forward_body, local=local, members=members, row_size=row_size
        ),
        "expert_forward",
        me,
        2 * local,
        [spec["tokens"]] * members
        + [spec["first"], spec["bias"], spec["second"], spec["low_bias"]]
        + [spec["other"]] * (2 * row_size),
        [spec["tokens"]] * members + [spec["wide"], spec["wide"]],
        [jax.ShapeDtypeStruct(rows[0].shape, BF)] * members + [wide, wide],
        [pltpu.VMEM((count, PIECE), FL)],
        [*rows, first, first_bias, second, second_bias, *first_other, *second_other],
        19,
        after,
    )
    return outs[:members], outs[members], outs[members + 1]


def expert_backward_body(me_ref, *refs, local, members, row_size):
    row_refs, (in_ref, out_ref, slope_ref), in_others, out_others, refs = taken(
        refs, members, 3, row_size, row_size
    )
    result_refs, (dpre_ref, dbias_ref) = taken(refs, members)
    expert = pl.program_id(0)
    rows = joined(row_refs)
    chunks = in_ref.shape[2] // PIECE
    total = None
    for chunk in range(chunks):
        lanes = slice(chunk * PIECE, (chunk + 1) * PIECE)
        weight = expert_weight(
            out_ref[0, lanes, :], out_others, expert, chunk, local, chunks, me_ref[0]
        )
        dpre = mm_nt(rows, weight) * slope_ref[0, :, lanes].astype(FL)
        dbias_ref[0, :, lanes] = jnp.sum(dpre, 0, keepdims=True)
        low = dpre.astype(BF)
        dpre_ref[0, :, lanes] = low
        weight = expert_weight(
            in_ref[0, :, lanes], in_others, expert, chunk, local, chunks, me_ref[0]
        )
        now = mm_nt(low, weight)
        total = now if total is None else total + now
    put_parts(result_refs, total)


def expert_backward(me, rows, first, second, first_other, second_other, slope, after):
    members, row_size = len(rows), len(first_other)
    local, channels, hidden = first.shape
    slots = rows[0].shape[0] // (2 * local)
    count = members * slots
    spec = expert_specs(members, slots, channels, hidden, local, row_size)
    outs = call_expert(
        functools.partial(
            expert_backward_body, local=local, members=members, row_size=row_size
        ),
        "expert_backward",
        me,
        2 * local,
        [spec["tokens"]] * members
        + [spec["first"], spec["second"], spec["wide"]]
        + [spec["other"]] * (2 * row_size),
        [spec["tokens"]] * members + [spec["wide"], spec["bias"]],
        [jax.ShapeDtypeStruct(rows[0].shape, BF)] * members
        + [
            jax.ShapeDtypeStruct((2 * local, count, hidden), BF),
            jax.ShapeDtypeStruct((2 * local, 1, hidden), FL),
        ],
        [],
        [*rows, first, second, slope, *first_other, *second_other],
        12,
        after,
    )
    return outs[:members], outs[members], outs[members + 1]


def expert_weight_body(me_ref, *refs, local, members, micros, tokens_left):
    token_refs, wide_refs, (keep_ref, send_ref, dbias_ref) = taken(
        refs, members * micros, micros
    )
    expert = pl.program_id(0)
    half = keep_ref.shape[1]
    row_size = 2 * half
    chunks = wide_refs[0].shape[2] // PIECE
    rows = [joined(token_refs[m * members : (m + 1) * members]) for m in range(micros)]
    dbias_ref[0] = sum(jnp.sum(part.astype(FL), 0, keepdims=True) for part in rows)
    for chunk in range(chunks):
        lanes = slice(chunk * PIECE, (chunk + 1) * PIECE)
        total = None
        for part, ref in zip(rows, wide_refs):
            wide = ref[0, :, lanes]
            now = mm_tn(part, wide) if tokens_left else mm_tn(wide, part)
            total = now if total is None else total + now
        low = total.astype(BF)
        member, _ = piece_home(expert % local, chunk, row_size, chunks)
        spot = spot_of(member, me_ref[0], row_size.bit_length() - 1)

        @pl.when(spot < half)
        def _():
            keep_ref[0, spot, 0] = low

        @pl.when(spot >= half)
        def _():
            send_ref[0, spot - half, 0] = low


def expert_weight_grads(me, tokens, wide, local, row_size, tokens_left, after):
    members, micros = len(tokens[0]), len(tokens)
    together, channels = tokens[0][0].shape
    slots = together // (2 * local)
    width = wide[0].shape[-1]
    chunks = width // PIECE
    subs = local * chunks // row_size
    spec = expert_specs(members, slots, channels, width, local, row_size)
    half_shape = (2, row_size // 2, subs, PIECE, PIECE)
    half_spec = pl.BlockSpec(
        (1, row_size // 2, 1, PIECE, PIECE),
        lambda k, me: (k // local, 0, (k % local) * chunks // row_size, 0, 0),
    )
    half_out = jax.ShapeDtypeStruct(half_shape, BF)
    return call_expert(
        functools.partial(
            expert_weight_body,
            local=local,
            members=members,
            micros=micros,
            tokens_left=tokens_left,
        ),
        "expert_weight_grads",
        me,
        2 * local,
        [spec["tokens"]] * (members * micros) + [spec["wide"]] * micros,
        [half_spec] * 2 + [spec["low_bias"]],
        [half_out] * 2 + [jax.ShapeDtypeStruct((2 * local, 1, channels), FL)],
        [],
        [part for parts in tokens for part in parts] + list(wide),
        13,
        after,
    )


def add_pieces_body(keep_ref, got_ref, *out_refs):
    half = keep_ref.shape[1] // 2
    for group in range(2):
        if half:
            for k in range(half):
                out_refs[0][group, k] = plus(keep_ref[group, k], got_ref[group, k]).astype(BF)
                at = half + k
                out_refs[1][group, k] = plus(keep_ref[group, at], got_ref[group, at]).astype(BF)
        else:
            total = plus(keep_ref[group, 0], got_ref[group, 0])
            out_refs[group][...] = total.astype(out_refs[group].dtype)


def add_pieces(keep, got, after):
    groups, count = keep.shape[:2]
    if count > 1:
        shape = (groups, count // 2) + keep.shape[2:]
        outs = [(shape, BF), (shape, BF)]
    else:
        outs = [(keep.shape[2:], FL), (keep.shape[2:], BF)]
    return call_kernel(add_pieces_body, "add_pieces", outs, [keep, got], micros=3, after=after)


def add_halves_body(own_ref, got_ref, out_ref):
    out_ref[...] = plus(own_ref[...], got_ref[...]).astype(out_ref.dtype)


def add_halves(own, got, after, dtype=BF, micros=2):
    (total,) = call_kernel(
        add_halves_body, "add_halves", [(own.shape, dtype)], [own, got], micros=micros, after=after
    )
    return total


def add_blocks_body(*refs):
    (*block_refs, mine_ref, other_ref) = refs
    for half, ref in enumerate((mine_ref, other_ref)):
        ref[...] = sum(block[half].astype(FL) for block in block_refs).astype(ref.dtype)


def add_blocks(blocks, after):
    shape = blocks[0].shape[1:]
    return call_kernel(
        add_blocks_body,
        "add_blocks",
        [(shape, FL), (shape, BF)],
        blocks,
        micros=0.2,
        after=after,
    )


def place_body(me_ref, *refs, chunks, first):
    (*piece_refs, full_ref) = refs
    row_size = len(piece_refs)
    for c in range(chunks):
        member, _ = piece_home(pl.program_id(0), c, row_size, chunks)
        spot = spot_of(member, me_ref[0], row_size.bit_length() - 1)
        span = slice(c * PIECE, (c + 1) * PIECE)
        value = piece_refs[0][0]
        for k in range(1, row_size):
            value = jnp.where(spot == k, piece_refs[k][0], value)
        if first:
            full_ref[0, :, span] = value.astype(FL)
        else:
            full_ref[0, span, :] = value.astype(FL)


def place_pieces(me, pieces, local, hidden, first, after):
    row_size = len(pieces)
    chunks = hidden // PIECE
    shape = (local, PIECE, hidden) if first else (local, hidden, PIECE)
    return call_expert(
        functools.partial(place_body, chunks=chunks, first=first),
        "place_pieces",
        me,
        local,
        [pl.BlockSpec((1, PIECE, PIECE), lambda e, me: (e * chunks // row_size, 0, 0))]
        * row_size,
        [pl.BlockSpec((1,) + shape[1:], lambda e, me: (e, 0, 0))],
        [jax.ShapeDtypeStruct(shape, FL)],
        [],
        list(pieces),
        4,
        after,
    )[0]


def swapped(rows):
    return lax.all_to_all(rows, "dp", split_axis=0, concat_axis=0, tiled=True)


def exchanged(blocks):
    return [blocks[0]] + [crossed(block, "dp", k) for k, block in enumerate(blocks) if k]


def bits_of(axis):
    return [1 << k for k in reversed(range(lax.axis_size(axis).bit_length() - 1))]


def spread_over_row(piece):
    held = [piece]
    for bit in bits_of("row"):
        held = held + [crossed(part, "row", bit) for part in held]
    return held


def join_body(me_ref, *refs, count):
    part_refs, out_refs = taken(refs, count)
    width = part_refs[0].shape[1]
    for c in range(count):
        spot = spot_of(c, me_ref[0], count.bit_length() - 1)
        value = part_refs[0][...]
        for k in range(1, count):
            value = jnp.where(spot == k, part_refs[k][...], value)
        start = 0
        for ref in out_refs:
            low, high = max(start, c * width), min(start + ref.shape[1], (c + 1) * width)
            if low < high:
                ref[:, low - start : high - start] = value[:, low - c * width : high - c * width]
            start += ref.shape[1]


def join_columns(me, parts, widths):
    rows = parts[0].shape[0]
    vmem = pl.BlockSpec(memory_space=pltpu.VMEM)
    return pl.pallas_call(
        functools.partial(join_body, count=len(parts)),
        name="join_columns",
        in_specs=[pl.BlockSpec(memory_space=pltpu.SMEM)] + [vmem] * len(parts),
        out_specs=[vmem] * len(widths),
        out_shape=[jax.ShapeDtypeStruct((rows, width), BF) for width in widths],
        cost_estimate=cost(2),
    )(me, *parts)


def gathered(shard):
    count = lax.axis_size("dp")
    copies = jnp.broadcast_to(shard[None], (count,) + shard.shape)
    return swapped(copies).reshape(count * shard.shape[0], shard.shape[1])


def side_by_side_body(*refs):
    (*ins, out_ref) = refs
    start = 0
    for ref in ins:
        out_ref[:, start : start + ref.shape[1]] = ref[...]
        start += ref.shape[1]


def copy_body(in_ref, out_ref):
    out_ref[...] = in_ref[...]


def held_back(array, after):
    (copy,) = call_kernel(
        copy_body, "hold", [(array.shape, array.dtype)], [array], micros=1, after=after
    )
    return copy


def crossed(array, axis, bit):
    count = lax.axis_size(axis)
    return lax.ppermute(array, axis, [(i, i ^ bit) for i in range(count)])


def summed(array, axes):
    for axis in axes:
        bit = 1
        while bit < lax.axis_size(axis):
            array = array + crossed(array, axis, bit)
            bit *= 2
    return array


def dense_blocks(grad):
    count = lax.axis_size("dp")
    half = count // 2
    place = lax.axis_index("dp")
    rows = grad.shape[0] // count
    grad = grad.reshape(2, half, rows, grad.shape[1])
    mine, other = place // half, 1 - place // half
    blocks = [
        jnp.concatenate(
            [
                lax.dynamic_slice(
                    grad, (h, (place % half) ^ k, 0, 0), (1, 1, rows, grad.shape[3])
                )[0]
                for h in (mine, other)
            ]
        )
        for k in range(half)
    ]
    return exchanged(blocks)


def dense_spread(part):
    held = spread_over_row(part)
    sums = held
    while len(sums) > 1:
        sums = [plus(left, right) for left, right in zip(sums[::2], sums[1::2])]
    return sums[0].astype(FL), held


def on_device(
    patches,
    unpadded_patch_size,
    patch_expert_index,
    cotangent,
    query_key_value_weight,
    query_projection_bias,
    value_projection_bias,
    log_cosine_scale,
    bias_network_first_weight,
    bias_network_first_bias,
    bias_network_second_weight,
    output_projection_weight,
    output_projection_bias,
    attention_norm_gain,
    attention_norm_bias,
    routing_weight,
    expert_first_weight,
    expert_first_bias,
    expert_second_weight,
    expert_second_bias,
    expert_norm_gain,
    expert_norm_bias,
    patch_merging_weight,
    merging_norm_gain,
    merging_norm_bias,
):
    micro_count, _, band_rows, band_cols, channels = patches.shape
    micros = range(micro_count)
    half_rows = band_rows // 2
    win_count = band_cols // WINDOW_SIDE
    win_area = WINDOW_SIDE * WINDOW_SIDE
    tokens = band_rows * band_cols
    half = tokens // 2
    experts = routing_weight.shape[1]
    dp_size = lax.axis_size("dp")
    local = experts // dp_size
    capacity = (5 * tokens + 4 * experts - 1) // (4 * experts)
    slots = -(-capacity // 16) * 16
    block_rows = 2 * local * slots
    members = dp_size // 2
    row_size = lax.axis_size("row")
    me = lax.axis_index("row").astype(jnp.int32)[None]
    my_place = lax.axis_index("dp").astype(jnp.int32)
    my_place = jnp.stack([my_place // members, my_place % members])
    total_rows = band_rows * lax.axis_size("row")
    row_start = band_rows * lax.axis_index("row")

    wide = 4 * channels + LANES
    shard = jnp.concatenate(
        [query_key_value_weight, output_projection_weight, routing_weight], 1
    )
    parts = -(-wide // (8 * LANES)) * 8 * LANES
    shard = jnp.pad(shard, ((0, 0), (0, parts - shard.shape[1])))
    parts //= row_size
    shard = lax.dynamic_slice(shard, (0, me[0] * parts), (shard.shape[0], parts))
    columns = gathered(shard)
    held = spread_over_row(columns)
    weight_qkv, weight_proj, weight_router = join_columns(
        me, held, [3 * channels, channels, LANES]
    )

    bands = patches.reshape(micro_count, tokens, channels)
    below = passed_along(bands[:, :half], "row", -1)

    zones = [
        mask_operands(
            row_start,
            total_rows,
            band_cols,
            unpadded_patch_size[m, 0, 0],
            unpadded_patch_size[m, 0, 1],
        )
        for m in micros
    ]

    dest_cols, dest_rows, chosen_cols = [], [], []
    for m in micros:
        chosen = patch_expert_index[m].reshape(1, tokens)
        column, dest_col, dest_row = slot_tables(
            chosen, my_place, experts, local, slots, capacity, columns
        )
        chosen_cols.append(column)
        dest_cols.append(dest_col)
        dest_rows.append(dest_row)

    network_first = jnp.concatenate(
        [bias_network_first_weight, bias_network_first_bias[None]], 0
    )
    tile_count = channels // LANES
    bias_shape = ((tile_count, win_area, TILE_HEADS * win_area), FL)
    bias_rows, bias_keys = call_kernel(
        spread_body, "spread_bias", [bias_shape, bias_shape], [network_first, bias_network_second_weight], after=[held[1], dest_rows[-1]]
    )
    hidden = expert_first_weight.shape[-1]
    chunks = hidden // PIECE
    subs = local * chunks // row_size
    first_piece, second_piece = [], []
    for sub in range(subs):
        piece = sub * row_size + me[0]
        at, start = piece // chunks, (piece % chunks) * PIECE
        first_piece.append(
            lax.dynamic_slice(expert_first_weight, (at, 0, start), (1, channels, PIECE))
        )
        second_piece.append(
            lax.dynamic_slice(expert_second_weight, (at, start, 0), (1, PIECE, channels))
        )
    first_got = crossed(jnp.concatenate(first_piece), "dp", members)
    second_got = crossed(held_back(jnp.concatenate(second_piece), [first_got]), "dp", members)
    first_other = spread_over_row(first_got)
    second_other = spread_over_row(second_got)
    expert_bias = jnp.concatenate([expert_first_bias, expert_second_bias], 1)
    expert_bias = jnp.concatenate([expert_bias, crossed(expert_bias, "dp", members)], 0)

    lane = jnp.arange(LANES)
    head_marks = jnp.repeat(
        (lane // HEAD_DIM)[None, :] == jnp.arange(TILE_HEADS)[:, None], win_area, 0
    ).astype(BF)
    block_ones = (
        ((jnp.arange(2 * LANES) % LANES) // HEAD_DIM)[:, None] == (lane // HEAD_DIM)[None, :]
    ).astype(BF)
    scale_lanes = jnp.repeat(jnp.exp(log_cosine_scale), HEAD_DIM)[None, :]
    qbias = query_projection_bias[None, :]
    vbias = value_projection_bias[None, :]
    attn_small = jnp.stack([output_projection_bias, attention_norm_gain, attention_norm_bias])
    moe_small = jnp.stack([expert_norm_gain, expert_norm_bias])
    merge_small = jnp.stack([merging_norm_gain, merging_norm_bias])
    first_bias = expert_bias[:, None, :hidden]
    second_bias = expert_bias[:, None, hidden:]

    grid_scratch = ((channels // LANES, band_rows * (band_cols + 8), LANES), FL)
    win_scratch = ((channels // LANES, tokens, LANES), FL)

    none = [None] * micro_count
    attended, arrived, routed, received = list(none), list(none), list(none), list(none)
    expert_out, returned, merged, back_res = list(none), list(none), list(none), list(none)
    expert_back, back_sent, settled, finished = list(none), list(none), list(none), list(none)
    outputs, input_grads, input_parts = list(none), list(none), list(none)

    forward_after = [[first_got, *dest_rows], []]
    route_after = [[second_got, first_other[1]], []]
    for m in micros:
        attended[m] = call_kernel(
            functools.partial(attend_forward_body, band_cols=band_cols, channels=channels),
            "attend_forward",
            [
                ((half, channels), BF),
                ((half, channels), BF),
                ((tokens, channels), BF),
                ((tokens, 3 * channels), BF),
                ((tokens, 2 * channels), FL),
            ],
            [
                bands[m],
                below[m],
                weight_qkv,
                qbias,
                vbias,
                scale_lanes,
                bias_rows,
                *zones[m],
                head_marks,
                block_ones,
            ],
            [grid_scratch, win_scratch],
            micros=16,
            after=(forward_after[m] if m < 2 else []) + [a[0] for a in attended[:m][-1:]],
        )
        arrived[m] = passed_along(attended[m][1], "row", 1)
    for m in micros:
        routed[m] = call_kernel(
            functools.partial(route_body, experts=experts),
            "route",
            [
                ((tokens, channels), FL),
                ((tokens, channels), BF),
                ((tokens, LANES), FL),
                ((tokens, channels), BF),
            ]
            + [((block_rows, channels), BF)] * members,
            [
                arrived[m],
                attended[m][0],
                bands[m],
                weight_proj,
                attn_small,
                weight_router,
                chosen_cols[m],
                dest_rows[m],
            ],
            micros=12,
            after=[attended[-1][0] if m == 0 else routed[m - 1][2]]
            + (route_after[m] if m < 2 else [])
            + (received[m - 1][1:] if m else []),
        )
        if m == 0:
            shard = held_back(patch_merging_weight, [routed[m][2]])
            weight_merge = lax.all_gather(shard, "dp", axis=0, tiled=True)
        received[m] = exchanged(routed[m][4:])
    for m in micros:
        expert_out[m] = expert_forward(
            me,
            received[m],
            expert_first_weight,
            expert_second_weight,
            first_other,
            second_other,
            first_bias,
            second_bias,
            [routed[-1][2] if m == 0 else expert_out[m - 1][0][0]],
        )
        returned[m] = exchanged(expert_out[m][0])
    for m in micros:
        merged[m] = call_kernel(
            functools.partial(
                merge_body, experts=experts, band_cols=band_cols, members=members
            ),
            "merge",
            [
                ((tokens // 4, 2 * channels), BF),
                ((tokens // 4, 4 * channels), BF),
                ((tokens // 4, 2 * channels), BF),
                ((tokens, channels), FL),
                ((tokens, LANES), BF),
                ((8, 2 * channels), FL),
            ]
            + [((block_rows, channels), BF)] * members,
            [
                *returned[m],
                dest_cols[m],
                dest_rows[m],
                chosen_cols[m],
                routed[m][2],
                routed[m][0],
                moe_small,
                weight_merge,
                merge_small,
                cotangent[m, 0].reshape(tokens // 4, 2 * channels),
            ],
            [
                ((tokens, channels), FL),
                ((tokens, channels), FL),
                ((tokens, LANES), FL),
                ((channels // LANES, tokens, LANES), FL),
                ((tokens, channels), BF),
            ],
            micros=14,
            after=[expert_out[-1][0][0] if m == 0 else merged[m - 1][0]],
        )
        outputs[m] = merged[m][0].reshape(band_rows // 2, band_cols // 2, 2 * channels)
        back_res[m] = exchanged(merged[m][6:])
    for m in micros:
        expert_back[m] = expert_backward(
            me,
            back_res[m],
            expert_first_weight,
            expert_second_weight,
            first_other,
            second_other,
            expert_out[m][2],
            [merged[-1][0] if m == 0 else expert_back[m - 1][2]],
        )
        back_sent[m] = exchanged(expert_back[m][0])

    def settle(m, after):
        return call_kernel(
            functools.partial(settle_body, members=members),
            "settle",
            [
                ((tokens, channels), FL),
                ((tokens, channels), BF),
                ((tokens, channels), BF),
                ((8, channels), FL),
            ],
            [
                *back_sent[m],
                dest_cols[m],
                merged[m][3],
                merged[m][4],
                weight_router,
                routed[m][1],
                routed[m][2],
                attn_small,
                weight_proj,
            ],
            micros=7,
            after=after,
        )

    settled[0] = settle(0, [expert_back[-1][2]])
    in_keep, in_send, _ = expert_weight_grads(
        me, received, [b[1] for b in expert_back], local, row_size, True, [settled[0][3]]
    )
    for m in micros[1:]:
        settled[m] = settle(m, [in_keep])
    grad_merge = merge_weight_grad(
        [b[1] for b in merged], [b[2] for b in merged], channels, [settled[-1][3]]
    )
    out_keep, out_send, grad_eout_bias = expert_weight_grads(
        me, back_res, [b[1] for b in expert_out], local, row_size, False, [grad_merge]
    )

    merge_blocks = dense_blocks(grad_merge)

    state = dict(
        first=dict(keep=in_keep, send=in_send), second=dict(keep=out_keep, send=out_send)
    )
    row_bits = list(reversed(bits_of("row")))
    latest = out_keep

    def transfer(kind):
        at = state[kind]
        step = at.setdefault("step", 0)
        if step < len(row_bits):
            at["got"] = crossed(at["send"], "row", row_bits[step])
        else:
            at["got"] = crossed(at["send"], "dp", members)

    def advance(kind):
        nonlocal latest
        at = state[kind]
        if at["step"] < len(row_bits):
            at["keep"], at["send"] = add_pieces(at["keep"], at["got"], [latest])
            latest = at["send"]
        else:
            at["held"] = spread_over_row(add_halves(at["keep"], at["got"], [latest]))
            latest = at["held"][0]
            return
        at["step"] += 1
        transfer(kind)

    transfer("first")
    transfer("second")
    plan = {
        "start": ["first"],
        (0, 1): ["first", "second"],
        (1, 0): ["first", "second"],
    }
    for _ in range(len(row_bits) - 2):
        plan[(0, 1)] = plan[(0, 1)] + ["first", "second"]

    def advance_at(place):
        nonlocal latest, merge_sums, sum_merge
        if place == (0, 0):
            merge_sums = add_blocks(merge_blocks, [latest])
            latest = merge_sums[0]
        elif place == (0, tile_count - 1):
            mine, other = merge_sums
            latest = add_halves(mine, crossed(other, "dp", members), [latest])
            sum_merge, _ = dense_spread(latest)
        for kind in plan.get(place, ()):
            advance(kind)

    merge_sums = sum_merge = None

    advance_at("start")
    dense_args = []
    for m in micros:
        dense_args += [arrived[m], attended[m][0], settled[m][1], routed[m][3], merged[m][4]]
    grad_proj, grad_router = call_kernel(
        dense_body,
        "dense_weight_grads",
        [((channels, channels), BF), ((channels, LANES), BF)],
        dense_args,
        micros=4,
        after=[latest],
    )
    latest = grad_router

    tile_sums = [None] * tile_count
    tile_smalls = []
    weight_grads = [grad_proj, grad_router]
    for m in micros:
        lifted = passed_along(settled[m][2][:half], "row", -1)
        (back_windows,) = call_kernel(
            functools.partial(window_body, band_cols=band_cols, channels=channels),
            "window_grads",
            [((tokens, channels), BF)],
            [settled[m][2][half:], lifted],
            [grid_scratch, win_scratch],
            micros=3,
            after=[latest],
        )
        latest = back_windows
        win, qkv, inverse = attended[m][2:]
        last = m == micro_count - 1
        grads = []
        for t in range(tile_count):

            def part(array, rows, at):
                return (array, pl.BlockSpec((rows, LANES), lambda i, at=at: (0, at)))

            args = [
                part(back_windows, tokens, t),
                part(qkv, tokens, t),
                part(qkv, tokens, tile_count + t),
                part(qkv, tokens, 2 * tile_count + t),
                part(inverse, tokens, t),
                part(inverse, tokens, tile_count + t),
                part(scale_lanes, 1, t),
                win,
                (
                    bias_keys,
                    pl.BlockSpec((1,) + bias_shape[0][1:], lambda i, t=t: (t, 0, 0)),
                ),
                *zones[m],
                head_marks,
                block_ones,
            ]
            if m:
                args += tile_sums[t]
            dqkv, dweight, dbias, small = call_kernel(
                functools.partial(attend_backward_body, summed_before=m > 0),
                "attend_backward",
                [
                    ((tokens, 3 * LANES), BF),
                    ((channels, 3 * LANES), BF if last else FL),
                    (bias_shape[0][1:], FL),
                    ((8, LANES), FL),
                ],
                args,
                micros=0.5 if last and t else 10,
                after=[latest],
            )
            latest = small
            tile_sums[t] = [dweight, dbias]
            tile_smalls.append(small)
            grads.append(dqkv)
            if last:
                weight_grads.append(dweight)
            advance_at((m, t))
        if last:
            tall = SUM_ROWS + 2 * local * (hidden // channels + 1)
            (sums,) = call_kernel(
                functools.partial(
                    fold_body, tile_count=tile_count, micro_count=micro_count
                ),
                "fold_bias",
                [((-(-tall // 8) * 8, channels), FL)],
                [sums[1] for sums in tile_sums]
                + tile_smalls
                + [part[3] for part in settled]
                + [part[5] for part in merged]
                + [part[2] for part in expert_back]
                + [grad_eout_bias],
                micros=3,
                after=[latest, state["second"]["got"]],
            )
            latest = sums
            advance("second")
            (joined_grads,) = call_kernel(
                side_by_side_body,
                "join_grads",
                [((channels, sum(w.shape[1] for w in weight_grads)), BF)],
                weight_grads,
                micros=2,
                after=[latest],
            )
            latest = joined_grads
            dense = dense_blocks(joined_grads)
        input_parts[m] = call_kernel(
            functools.partial(input_grad_body, band_cols=band_cols, channels=channels),
            "input_grad",
            [((half, channels), FL), ((half, channels), BF)],
            grads + [weight_qkv],
            [grid_scratch, win_scratch],
            micros=5,
            after=[latest],
        )
        latest = input_parts[m][1]
        passed = passed_along(input_parts[m][1], "row", 1).astype(FL)
        input_grads[m] = (
            (settled[m][0] + jnp.concatenate([passed, input_parts[m][0]], 0))
            .astype(BF)
            .reshape(band_rows, band_cols, channels)
        )
    steps = [("row", 1 << k) for k in range(row_size.bit_length() - 1)]
    steps += [("dp", 1 << k) for k in range(dp_size.bit_length() - 1)]
    tail = ["blocks", "first", "part"]
    for k, (axis, bit) in enumerate(steps):
        if axis == "dp" and steps[k - 1][0] == "row":
            sums, biases = sums[:SUM_ROWS], sums[SUM_ROWS:tall]
        sums = latest = add_halves(sums, crossed(sums, axis, bit), [latest], FL, 0.2)
        job = tail.pop(0) if tail else None
        if job == "blocks":
            mine, other = add_blocks(dense, [latest])
            latest = mine
        elif job == "first":
            latest = sum_ein = place_pieces(
                me, state["first"]["held"], local, hidden, True, [latest]
            )
        elif job == "part":
            latest = part = add_halves(mine, crossed(other, "dp", members), [latest], BF, 0.2)
    sum_dense, held = dense_spread(part)
    sum_eout = place_pieces(me, state["second"]["held"], local, hidden, False, [latest])
    sum_proj = sum_dense[:, :channels]
    sum_router = sum_dense[:, channels : channels + experts]
    sum_qkv = sum_dense[:, channels + LANES :].reshape(-1, tile_count, 3, LANES)
    sum_qkv = sum_qkv.swapaxes(1, 2).reshape(-1, 3 * channels)
    in_bias = biases[: 2 * local * chunks].reshape(2 * local, hidden)
    out_bias = biases[2 * local * chunks :]
    other_bias = crossed(
        jnp.concatenate([in_bias[local:], out_bias[local:]], 1), "dp", members
    )
    sum_ein_bias = in_bias[:local] + other_bias[:, :hidden]
    sum_eout_bias = out_bias[:local] + other_bias[:, hidden:]
    grad_first, grad_second = call_kernel(
        bias_network_back_body,
        "bias_network_back",
        [(network_first.shape, FL), (bias_network_second_weight.shape, FL)],
        [sums, network_first, bias_network_second_weight],
        micros=0.2,
    )
    grad_first, grad_first_bias = grad_first[:2], grad_first[2]
    sum_qbias, sum_vbias, sum_scale = (
        sums[ATTN_AT],
        sums[ATTN_AT + 1],
        sums[ATTN_AT + 2, ::HEAD_DIM],
    )
    sum_proj_bias, sum_again, sum_ashift = (sums[SETTLE_AT + k] for k in range(3))
    sum_rgain = sums[MERGE_AT : MERGE_AT + 2].reshape(2 * channels)
    sum_rshift = sums[MERGE_AT + 2 : MERGE_AT + 4].reshape(2 * channels)
    sum_mgain, sum_mshift = sums[MERGE_AT + 4], sums[MERGE_AT + 5]
    return (
        jnp.stack(outputs)[:, None],
        jnp.stack(input_grads)[:, None],
        sum_qkv,
        sum_qbias,
        sum_vbias,
        sum_scale,
        grad_first,
        grad_first_bias,
        grad_second,
        sum_proj,
        sum_proj_bias,
        sum_again,
        sum_ashift,
        sum_router,
        sum_ein,
        sum_ein_bias,
        sum_eout,
        sum_eout_bias,
        sum_mgain,
        sum_mshift,
        sum_merge,
        sum_rgain,
        sum_rshift,
    )


def solution(mesh):
    return jax.shard_map(
        on_device,
        mesh=mesh,
        in_specs=(
            P(None, "dp", "row", None, None),
            P(None, "dp", None),
            P(None, "dp", "row", None, None),
            P(None, "dp", "row", None, None),
            P("dp", None),
            P(),
            P(),
            P(),
            P(),
            P(),
            P(),
            P("dp", None),
            P(),
            P(),
            P(),
            P("dp", None),
            P("dp", None, None),
            P("dp", None),
            P("dp", None, None),
            P("dp", None),
            P(),
            P(),
            P("dp", None),
            P(),
            P(),
        ),
        out_specs=(
            P(None, "dp", "row", None, None),
            P(None, "dp", "row", None, None),
            P("dp", None),
            P(),
            P(),
            P(),
            P(),
            P(),
            P(),
            P("dp", None),
            P(),
            P(),
            P(),
            P("dp", None),
            P("dp", None, None),
            P("dp", None),
            P("dp", None, None),
            P("dp", None),
            P(),
            P(),
            P("dp", None),
            P(),
            P(),
        ),
        check_vma=False,
    )
```

```python
import functools

import jax
import jax.numpy as jnp
from jax import lax
from jax.experimental import pallas as pl
from jax.experimental.pallas import tpu as pltpu
from jax.sharding import PartitionSpec as P

HEAD_COUNT = 12
HEAD_DIM = 32
WINDOW_SIDE = 12
LANES = 128
SHEAR = 384
ZONES = 16
UNROLL = 4
COST_SCALE = 0.4
TILE_HEADS = LANES // HEAD_DIM


PRECISION_HIGH = lax.Precision.HIGHEST
EPS_NORM = 1e-05
EPS_UNIT = 1e-06
MASK_FILL = -100.0
BF = jnp.bfloat16
FL = jnp.float32
VMEM_BYTES = 52 * 2**20


def cost(micros):
    return pl.CostEstimate(
        flops=int(micros * COST_SCALE * 1.1e9), bytes_accessed=10**5, transcendentals=0
    )


def passed_along(array, axis, by):
    count = lax.axis_size(axis)
    return lax.ppermute(array, axis, [(i, (i + by) % count) for i in range(count)])


def exact_error_gelu(values):
    return jax.nn.gelu(values, approximate=False)


SPANS = 2 * WINDOW_SIDE - 1
AREA = WINDOW_SIDE * WINDOW_SIDE


def span_coordinate(steps):
    size = jnp.abs(steps) * (8.0 / (WINDOW_SIDE - 1))
    value = jnp.log2(size + 1.0) / 3.0
    return jnp.where(steps < 0, -value, value)


def bias_network(first_ref, second_ref):
    shape = (2 * SHEAR, 1)
    row = lax.broadcasted_iota(jnp.int32, shape, 0)
    below = row >= SHEAR
    place = jnp.where(below, row - SHEAR + 1, row - (WINDOW_SIDE - 1))
    held = jnp.clip(place, 0, SPANS * WINDOW_SIDE - 1)
    column = held % WINDOW_SIDE
    valid = (held == place) & (jnp.logical_not(below) | (column > 0))
    rows_apart = (held // WINDOW_SIDE - (WINDOW_SIDE - 1)).astype(FL)
    columns_apart = jnp.where(below, column - WINDOW_SIDE, column).astype(FL)
    down, across = span_coordinate(rows_apart), span_coordinate(columns_apart)
    pre = down * first_ref[0:1, :] + across * first_ref[1:2, :] + first_ref[2:3, :]
    cdf = 0.5 * (1.0 + lax.erf(pre * 0.7071067811865476))
    hidden = pre * cdf
    slope = cdf + pre * (0.3989422804014327 * jnp.exp(-0.5 * pre * pre))
    level = jax.nn.sigmoid(
        lax.dot_general(
            hidden,
            second_ref[...],
            (((1,), (0,)), ((), ())),
            precision=PRECISION_HIGH,
            preferred_element_type=FL,
        )
    )
    return down, across, valid, hidden, slope, level


def mask_operands(row_start, total_rows, total_cols, valid_rows, valid_cols):
    half_win = WINDOW_SIDE // 2
    rows_at = row_start + jnp.arange(WINDOW_SIDE)
    cols_at = jnp.arange(total_cols)
    row_zone = (rows_at >= total_rows - WINDOW_SIDE).astype(jnp.int32) + (
        rows_at >= total_rows - half_win
    ).astype(jnp.int32)
    col_zone = (cols_at >= total_cols - WINDOW_SIDE).astype(jnp.int32) + (
        cols_at >= total_cols - half_win
    ).astype(jnp.int32)
    zone_ids = 3 * row_zone[:, None] + col_zone[None, :]
    outside = ((rows_at + half_win) % total_rows >= valid_rows)[:, None] | (
        (cols_at + half_win) % total_cols >= valid_cols
    )[None, :]
    codes = zone_ids + jnp.where(outside, ZONES, 0)
    win_count = total_cols // WINDOW_SIDE
    codes = (
        codes.reshape(WINDOW_SIDE, win_count, WINDOW_SIDE)
        .transpose(1, 0, 2)
        .reshape(win_count, WINDOW_SIDE * WINDOW_SIDE)
    )
    zones, out = codes % ZONES, codes // ZONES
    mask = jnp.where(zones[:, :, None] != zones[:, None, :], MASK_FILL, 0.0) + jnp.where(
        out[:, None, :] > 0, MASK_FILL, 0.0
    )
    peak = jnp.max(mask, -1)[:, :, None]
    lane = jnp.arange(LANES)
    same = zones[:, :, None] == lane
    query = jnp.where(
        lane < ZONES,
        jnp.where(same, -MASK_FILL, 0.0),
        jnp.where(lane == ZONES, MASK_FILL, jnp.where(lane == ZONES + 1, MASK_FILL - peak, 0.0)),
    )
    key = jnp.where(
        lane < ZONES,
        jnp.where(same, 1.0, 0.0),
        jnp.where(lane == ZONES, out[:, :, None], jnp.where(lane == ZONES + 1, 1.0, 0.0)),
    )
    return (
        query.astype(BF).reshape(-1, LANES),
        key.astype(BF).reshape(-1, LANES),
    )


def plus(left, right):
    return left.astype(FL) + right.astype(FL)


def mm(left, right):
    return jnp.dot(left, right, preferred_element_type=FL)


def mm_nt(left, right):
    return lax.dot_general(left, right, (((1,), (1,)), ((), ())), preferred_element_type=FL)


def mm_tn(left, right):
    return lax.dot_general(left, right, (((0,), (0,)), ((), ())), preferred_element_type=FL)


def skipping(body, count, extra):
    def run(*refs):
        return body(*refs[:count], *refs[count + extra :])

    return run


def call_kernel(body, name, outs, args, scratch=(), micros=5, after=()):
    specs, arrays = [], []
    for arg in args:
        array, spec = arg if isinstance(arg, tuple) else (arg, None)
        if spec is None:
            spec = pl.BlockSpec(array.shape, lambda i, rank=array.ndim: (0,) * rank)
        specs.append(spec)
        arrays.append(array)
    return pl.pallas_call(
        skipping(body, len(args), len(after)),
        name=name,
        grid=(1,),
        out_shape=[jax.ShapeDtypeStruct(s, d) for s, d in outs],
        in_specs=specs + [pl.BlockSpec(memory_space=pl.ANY)] * len(after),
        out_specs=[pl.BlockSpec(s, lambda i, rank=len(s): (0,) * rank) for s, _ in outs],
        scratch_shapes=[pltpu.VMEM(s, d) for s, d in scratch],
        compiler_params=pltpu.CompilerParams(vmem_limit_bytes=VMEM_BYTES),
        cost_estimate=cost(micros),
    )(*arrays, *after)


def rows_at(start, size):
    return pl.ds(pl.multiple_of(start, 16), size)


def head_sums(values, block_ones):
    high = values.astype(BF)
    rest = (values - high.astype(FL)).astype(BF)
    return mm(jnp.concatenate([high, rest], 1), block_ones)


def tiles_of(channels):
    return [slice(LANES * t, LANES * (t + 1)) for t in range(channels // LANES)]


def to_windows(sources, grid_ref, win_ref, band_cols, channels):
    half_win = WINDOW_SIDE // 2
    pitch = band_cols + 8
    win_area = WINDOW_SIDE * WINDOW_SIDE
    for i in range(WINDOW_SIDE):
        value = sources(i).astype(FL)
        for t, lanes in enumerate(tiles_of(channels)):
            grid_ref[t, i * pitch : i * pitch + band_cols, :] = value[:, lanes]
            grid_ref[t, i * pitch + band_cols : (i + 1) * pitch, :] = value[0:8, lanes]
    for t in range(channels // LANES):
        for n in range(band_cols // WINDOW_SIDE):
            for i in range(WINDOW_SIDE):
                at = i * pitch + n * WINDOW_SIDE + half_win
                to = n * win_area + i * WINDOW_SIDE
                win_ref[t, to : to + WINDOW_SIDE, :] = grid_ref[t, at : at + WINDOW_SIDE, :]


def from_windows(put, grid_ref, win_ref, band_cols, channels):
    half_win = WINDOW_SIDE // 2
    pitch = band_cols + 8
    win_area = WINDOW_SIDE * WINDOW_SIDE
    for t in range(channels // LANES):
        for n in range(band_cols // WINDOW_SIDE):
            for i in range(WINDOW_SIDE):
                to = i * pitch + n * WINDOW_SIDE + half_win
                at = n * win_area + i * WINDOW_SIDE
                grid_ref[t, to : to + WINDOW_SIDE, :] = win_ref[t, at : at + WINDOW_SIDE, :]
        for i in range(WINDOW_SIDE):
            grid_ref[t, i * pitch : i * pitch + half_win, :] = grid_ref[
                t, i * pitch + band_cols : i * pitch + band_cols + half_win, :
            ]
    for i in range(WINDOW_SIDE):
        put(
            i,
            jnp.concatenate(
                [
                    grid_ref[t, i * pitch : i * pitch + band_cols, :]
                    for t in range(channels // LANES)
                ],
                1,
            ),
        )


def stacked(tile, heads_ref):
    return jnp.concatenate([tile] * TILE_HEADS, 0) * heads_ref[...]


def spread_body(first_ref, second_ref, rows_ref, keys_ref):
    row = lax.broadcasted_iota(jnp.int32, (AREA, AREA), 0) % WINDOW_SIDE
    lane = lax.broadcasted_iota(jnp.int32, (AREA, AREA), 1) % WINDOW_SIDE
    *_, level = bias_network(first_ref, second_ref)
    wide = jnp.concatenate([16.0 * level, jnp.zeros((2 * SHEAR, LANES - HEAD_COUNT), FL)], 1)
    lines = wide.T

    def shear(line):
        wide = pltpu.roll(jnp.broadcast_to(line, (AREA, SHEAR)), SHEAR - (AREA - 1), 1)
        return pltpu.roll(wide, 0, 1, stride=1, stride_axis=0)[:, 0:AREA]

    for t in range(rows_ref.shape[0]):
        rows, keys = [], []
        for k in range(TILE_HEADS):
            line = lines[t * TILE_HEADS + k : t * TILE_HEADS + k + 1]
            key = jnp.where(lane >= row, shear(line[:, :SHEAR]), shear(line[:, SHEAR:]))
            keys.append(key)
            rows.append(key.T)
        rows_ref[t] = jnp.concatenate(rows, 1)
        keys_ref[t] = jnp.concatenate(keys, 1)


LINE_ROWS = 2 * HEAD_COUNT
ATTN_AT = LINE_ROWS
SETTLE_AT = ATTN_AT + 3
MERGE_AT = SETTLE_AT + 3
SUM_ROWS = 40


def fold_body(*refs, tile_count, micro_count):
    dbias_refs, attn_refs, settle_refs, merge_refs, dpre_refs, (dout_ref, out_ref) = taken(
        refs, tile_count, tile_count * micro_count, micro_count, micro_count, micro_count
    )
    row = lax.broadcasted_iota(jnp.int32, (AREA, AREA), 0)
    lane = lax.broadcasted_iota(jnp.int32, (AREA, AREA), 1)
    turn = jnp.where(row + lane == AREA - 1, 1.0, 0.0).astype(BF)
    later = lane % WINDOW_SIDE >= (AREA - 1 - row) % WINDOW_SIDE
    blank = jnp.zeros((AREA, SHEAR - AREA), FL)

    def fold(values):
        wide = jnp.concatenate([values, blank], 1)
        return jnp.sum(pltpu.roll(wide, 0, 1, stride=1, stride_axis=0), 0, keepdims=True)

    channels = out_ref.shape[1]
    out_ref[...] = jnp.zeros_like(out_ref)
    for t, ref in enumerate(dbias_refs):
        values = ref[...]
        for k in range(TILE_HEADS):
            value = values[:, k * AREA : (k + 1) * AREA]
            total = None
            for _ in range(3):
                part = value.astype(BF)
                value = value - part.astype(FL)
                now = mm(turn, part)
                total = now if total is None else total + now
            head = t * TILE_HEADS + k
            out_ref[head : head + 1, :] = fold(jnp.where(later, total, 0.0))
            at = HEAD_COUNT + head
            out_ref[at : at + 1, :] = fold(jnp.where(later, 0.0, total))
        lanes = slice(t * LANES, (t + 1) * LANES)
        out_ref[ATTN_AT : ATTN_AT + 3, lanes] = sum(
            attn_refs[m * tile_count + t][0:3, :] for m in range(micro_count)
        )
    out_ref[SETTLE_AT : SETTLE_AT + 3, :] = sum(ref[0:3, :] for ref in settle_refs)
    merge = sum(ref[0:4, :] for ref in merge_refs)
    for k, (at, half) in enumerate(((0, 0), (0, 1), (1, 0), (1, 1), (2, 0), (3, 0))):
        out_ref[MERGE_AT + k : MERGE_AT + k + 1, :] = merge[
            at : at + 1, half * channels : (half + 1) * channels
        ]
    experts, _, hidden = dpre_refs[0].shape
    chunks = hidden // channels
    for e in range(experts):
        total = sum(ref[e] for ref in dpre_refs)
        for c in range(chunks):
            at = SUM_ROWS + e * chunks + c
            out_ref[at : at + 1, :] = total[:, c * channels : (c + 1) * channels]
        at = SUM_ROWS + experts * chunks + e
        out_ref[at : at + 1, :] = dout_ref[e]


def bias_network_back_body(sums_ref, first_ref, second_ref, dfirst_ref, dsecond_ref):
    down, across, valid, hidden, slope, level = bias_network(first_ref, second_ref)
    lines = jnp.concatenate(
        [sums_ref[0:HEAD_COUNT, :], sums_ref[HEAD_COUNT : 2 * HEAD_COUNT, :]], 1
    )
    lines = jnp.concatenate([lines, jnp.zeros((LANES - HEAD_COUNT, 2 * SHEAR), FL)], 0)
    grad = lines.T[:, 0:HEAD_COUNT]
    grad = jnp.where(valid, grad * 16.0 * level * (1.0 - level), 0.0)
    dsecond_ref[...] = lax.dot_general(
        hidden,
        grad,
        (((0,), (0,)), ((), ())),
        precision=PRECISION_HIGH,
        preferred_element_type=FL,
    )
    dpre = slope * lax.dot_general(
        grad,
        second_ref[...],
        (((1,), (1,)), ((), ())),
        precision=PRECISION_HIGH,
        preferred_element_type=FL,
    )
    dfirst_ref[0:1, :] = jnp.sum(down * dpre, 0, keepdims=True)
    dfirst_ref[1:2, :] = jnp.sum(across * dpre, 0, keepdims=True)
    dfirst_ref[2:3, :] = jnp.sum(dpre, 0, keepdims=True)


def slot_body(
    place_ref,
    experts_ref,
    column_ref,
    dest_column_ref,
    dest_row_ref,
    *,
    experts,
    local,
    slots,
    capacity,
):
    tokens = experts_ref.shape[1]

    def place(expert):
        upper = jnp.where(expert >= experts // 2, 1, 0)
        inner = expert - upper * (experts // 2)
        apart = upper ^ place_ref[0]
        member = (inner // local) ^ place_ref[1]
        return ((2 * member + apart) * local + inner % local) * slots

    block = LANES
    lower = (
        lax.broadcasted_iota(jnp.int32, (block, block), 0)
        > lax.broadcasted_iota(jnp.int32, (block, block), 1)
    ).astype(FL).astype(BF)
    upper = (
        lax.broadcasted_iota(jnp.int32, (block, block), 0)
        < lax.broadcasted_iota(jnp.int32, (block, block), 1)
    ).astype(FL).astype(BF)
    lane = lax.broadcasted_iota(jnp.int32, (block, LANES), 1)
    sublane = lax.broadcasted_iota(jnp.int32, (LANES, block), 0)
    seen_row = jnp.zeros((1, LANES), FL)
    seen_column = jnp.zeros((LANES, 1), FL)
    for c in range(tokens // block):
        line = experts_ref[:, c * block : (c + 1) * block]
        across = jnp.where(sublane == line, 1.0, 0.0)
        column = jnp.broadcast_to(line.astype(FL), (block, block)).T[:, 0:1].astype(jnp.int32)
        down = jnp.where(lane == column, 1.0, 0.0)
        before = mm(lower, down.astype(BF)) + seen_row
        slot = jnp.sum(down * before, 1, keepdims=True).astype(jnp.int32)
        column_ref[c * block : (c + 1) * block, :] = column
        dest_column_ref[c * block : (c + 1) * block, :] = jnp.where(
            slot < capacity, place(column) + slot, -1
        )
        before = mm(across.astype(BF), upper) + seen_column
        slot = jnp.sum(across * before, 0, keepdims=True).astype(jnp.int32)
        dest_row_ref[:, c * block : (c + 1) * block] = jnp.where(
            slot < capacity, place(line) + slot, -1
        )
        seen_row = seen_row + jnp.sum(down, 0, keepdims=True)
        seen_column = seen_column + jnp.sum(across, 1, keepdims=True)


def slot_tables(chosen, my_place, experts, local, slots, capacity, after):
    tokens = chosen.shape[1]
    vmem = pl.BlockSpec(memory_space=pltpu.VMEM)
    column = jax.ShapeDtypeStruct((tokens, 1), jnp.int32)
    return pl.pallas_call(
        skipping(
            functools.partial(
                slot_body, experts=experts, local=local, slots=slots, capacity=capacity
            ),
            2,
            1,
        ),
        name="slot_tables",
        in_specs=[
            pl.BlockSpec(memory_space=pltpu.SMEM),
            vmem,
            pl.BlockSpec(memory_space=pl.ANY),
        ],
        out_specs=[vmem] * 3,
        out_shape=[column, column, jax.ShapeDtypeStruct((1, tokens), jnp.int32)],
        cost_estimate=cost(3),
    )(my_place, chosen, after)


def attend_forward_body(
    band_ref,
    below_ref,
    weight_ref,
    qbias_ref,
    vbias_ref,
    scale_ref,
    bias_ref,
    query_zone_ref,
    key_zone_ref,
    heads_ref,
    block_ref,
    own_ref,
    send_ref,
    win_ref,
    qkv_ref,
    inv_ref,
    grid_scr,
    win_scr,
    *,
    band_cols,
    channels,
):
    tokens = band_ref.shape[0]
    half = tokens // 2
    win_area = WINDOW_SIDE * WINDOW_SIDE
    tiles = tiles_of(channels)

    def source(i):
        if i < WINDOW_SIDE // 2:
            return band_ref[half + i * band_cols : half + (i + 1) * band_cols, :]
        at = (i - WINDOW_SIDE // 2) * band_cols
        return below_ref[at : at + band_cols, :]

    to_windows(source, grid_scr, win_scr, band_cols, channels)
    block_ones = block_ref[...]
    chunk = 2 * win_area

    def project(c, carry):
        rows = rows_at(c * chunk, chunk)
        low = jnp.concatenate([win_scr[t, rows, :] for t in range(len(tiles))], 1).astype(BF)
        win_ref[rows, :] = low
        qkv = mm(low, weight_ref[...])
        for lanes in tiles:
            key_lanes = slice(channels + lanes.start, channels + lanes.stop)
            value_lanes = slice(2 * channels + lanes.start, 2 * channels + lanes.stop)
            query = qkv[:, lanes] + qbias_ref[:, lanes]
            inverse = (
                lax.rsqrt(head_sums(query * query, block_ones) + EPS_UNIT) * scale_ref[:, lanes]
            )
            inv_ref[rows, lanes] = inverse
            qkv_ref[rows, lanes] = (query * inverse).astype(BF)
            key = qkv[:, key_lanes]
            inverse = lax.rsqrt(head_sums(key * key, block_ones) + EPS_UNIT)
            inv_ref[rows, key_lanes] = inverse
            qkv_ref[rows, key_lanes] = (key * inverse).astype(BF)
            qkv_ref[rows, value_lanes] = (qkv[:, value_lanes] + vbias_ref[:, lanes]).astype(BF)
        return carry

    lax.fori_loop(0, tokens // chunk, project, 0)

    def attend(n, carry):
        rows = rows_at(n * win_area, win_area)
        query_zone = query_zone_ref[rows, :]
        key_zone = jnp.concatenate([key_zone_ref[rows, :]] * TILE_HEADS, 0)
        for t, lanes in enumerate(tiles):
            query = qkv_ref[rows, lanes]
            key = qkv_ref[rows, channels + lanes.start : channels + lanes.stop]
            value = qkv_ref[rows, 2 * channels + lanes.start : 2 * channels + lanes.stop]
            scores = mm_nt(
                jnp.concatenate([query, query_zone], 1),
                jnp.concatenate([stacked(key, heads_ref), key_zone], 1),
            )
            powers = jnp.exp(scores + bias_ref[t]).astype(BF)
            mixed = mm(powers, jnp.concatenate([stacked(value, heads_ref), heads_ref[...]], 1))
            win_scr[t, rows, :] = mixed[:, :LANES] / mixed[:, LANES:]
        return carry

    lax.fori_loop(0, tokens // win_area, attend, 0, unroll=UNROLL)

    def put(i, value):
        if i < WINDOW_SIDE // 2:
            own_ref[i * band_cols : (i + 1) * band_cols, :] = value.astype(BF)
        else:
            at = (i - WINDOW_SIDE // 2) * band_cols
            send_ref[at : at + band_cols, :] = value.astype(BF)

    from_windows(put, grid_scr, win_scr, band_cols, channels)


def window_body(own_ref, lifted_ref, out_ref, grid_scr, win_scr, *, band_cols, channels):
    def source(i):
        ref = own_ref if i < WINDOW_SIDE // 2 else lifted_ref
        at = (i % (WINDOW_SIDE // 2)) * band_cols
        return ref[at : at + band_cols, :]

    to_windows(source, grid_scr, win_scr, band_cols, channels)
    for t, lanes in enumerate(tiles_of(channels)):
        out_ref[:, lanes] = win_scr[t].astype(BF)


def attend_backward_body(*refs, summed_before):
    (
        back_ref,
        query_ref,
        key_ref,
        value_ref,
        query_inv_ref,
        key_inv_ref,
        scale_ref,
        win_ref,
        bias_ref,
        query_zone_ref,
        key_zone_ref,
        heads_ref,
        block_ref,
        *rest,
    ) = refs
    if summed_before:
        dweight_before_ref, dbias_before_ref, *rest = rest
    dqkv_ref, dweight_ref, dbias_ref, small_ref = rest
    tokens = back_ref.shape[0]
    win_area = WINDOW_SIDE * WINDOW_SIDE
    block_ones = block_ref[...]
    if summed_before:
        dbias_ref[...] = dbias_before_ref[...]
    else:
        dbias_ref[...] = jnp.zeros_like(dbias_ref)
    small_ref[...] = jnp.zeros_like(small_ref)

    def attend(n, carry):
        rows = rows_at(n * win_area, win_area)
        query = query_ref[rows, :]
        key = key_ref[rows, :]
        queries = stacked(query, heads_ref)
        backs = stacked(back_ref[rows, :], heads_ref)
        query_zone = jnp.concatenate([query_zone_ref[rows, :]] * TILE_HEADS, 0)
        scores = mm_nt(
            jnp.concatenate([key, key_zone_ref[rows, :]], 1),
            jnp.concatenate([queries, query_zone], 1),
        )
        powers = jnp.exp(scores + bias_ref[0])
        probs = powers * (1.0 / jnp.sum(powers, 0, keepdims=True))
        weighted = probs * mm_nt(value_ref[rows, :], backs)
        dscores = weighted - probs * jnp.sum(weighted, 0, keepdims=True)
        dbias_ref[...] += dscores
        dlow = dscores.astype(BF)
        dvalue = mm(probs.astype(BF), backs)
        dkey = mm(dlow, queries)
        dquery = mm_tn(dlow, key) * heads_ref[...].astype(FL)
        dquery = sum(dquery[k * win_area : (k + 1) * win_area] for k in range(TILE_HEADS))
        scale = scale_ref[...]
        unit = query.astype(FL)
        along = head_sums(unit * dquery, block_ones)
        dquery = query_inv_ref[rows, :] * (dquery - unit * along / (scale * scale))
        unit = key.astype(FL)
        dkey = key_inv_ref[rows, :] * (dkey - unit * head_sums(unit * dkey, block_ones))
        for part, grad in enumerate((dquery, dkey, dvalue)):
            dqkv_ref[rows, part * LANES : (part + 1) * LANES] = grad.astype(BF)
        small_ref[0:1, :] += jnp.sum(dquery, 0, keepdims=True)
        small_ref[1:2, :] += jnp.sum(dvalue, 0, keepdims=True)
        small_ref[2:3, :] += jnp.sum(along, 0, keepdims=True)
        return carry

    lax.fori_loop(0, tokens // win_area, attend, 0, unroll=UNROLL)
    dweight = mm_tn(win_ref[...], dqkv_ref[...])
    if summed_before:
        dweight = dweight + dweight_before_ref[...]
    dweight_ref[...] = dweight.astype(dweight_ref.dtype)


def input_grad_body(
    first_ref,
    second_ref,
    third_ref,
    weight_ref,
    own_ref,
    send_ref,
    grid_scr,
    win_scr,
    *,
    band_cols,
    channels,
):
    tokens = first_ref.shape[0]
    tiles = tiles_of(channels)
    chunk = 2 * WINDOW_SIDE * WINDOW_SIDE

    def project(c, carry):
        rows = rows_at(c * chunk, chunk)
        parts = [ref[rows, :] for ref in (first_ref, second_ref, third_ref)]
        wide = jnp.concatenate([p[:, lanes] for lanes in tiles for p in parts], 1)
        back = mm_nt(wide, weight_ref[...])
        for t, lanes in enumerate(tiles):
            win_scr[t, rows, :] = back[:, lanes]
        return carry

    lax.fori_loop(0, tokens // chunk, project, 0)

    def put(i, value):
        if i < WINDOW_SIDE // 2:
            own_ref[i * band_cols : (i + 1) * band_cols, :] = value
        else:
            at = (i - WINDOW_SIDE // 2) * band_cols
            send_ref[at : at + band_cols, :] = value.astype(BF)

    from_windows(put, grid_scr, win_scr, band_cols, channels)


def lane_mean(values):
    return jnp.sum(values, -1, keepdims=True) * (1.0 / values.shape[-1])


def normalised(values):
    centred = values - lane_mean(values)
    inverse = lax.rsqrt(lane_mean(centred * centred) + EPS_NORM)
    return centred * inverse, inverse


def normalised_back(back, gain, unit, inverse):
    back = back * gain
    return inverse * (back - lane_mean(back) - unit * lane_mean(back * unit))


CHUNK = 576


def pack_rows(dest_row_ref, rows_ref, out_refs):
    tokens = rows_ref.shape[0]
    start = 0
    for ref in out_refs:
        place = lax.broadcasted_iota(jnp.int32, (ref.shape[0], tokens), 0) + start
        chosen = jnp.where(place == dest_row_ref[...], 1.0, 0.0).astype(BF)
        ref[...] = mm(chosen, rows_ref[...]).astype(BF)
        start += ref.shape[0]


def unpack_rows(dest_col, buffer):
    place = lax.broadcasted_iota(jnp.int32, (dest_col.shape[0], buffer.shape[0]), 1)
    chosen = jnp.where(place == dest_col, 1.0, 0.0).astype(BF)
    return mm(chosen, buffer)


def route_body(
    arrived_ref,
    own_ref,
    band_ref,
    weight_ref,
    small_ref,
    router_ref,
    expert_ref,
    dest_row_ref,
    resid_ref,
    unit_ref,
    aux_ref,
    low_ref,
    *sent_refs,
    experts,
):
    half = arrived_ref.shape[0]
    lane = lax.broadcasted_iota(jnp.int32, (CHUNK, LANES), 1)
    for part, ref in enumerate((arrived_ref, own_ref)):

        def step(c, carry, part=part, ref=ref):
            rows = rows_at(part * half + c * CHUNK, CHUNK)
            projected = mm(ref[rows_at(c * CHUNK, CHUNK), :], weight_ref[...]) + small_ref[0:1, :]
            unit, inverse = normalised(projected)
            unit_ref[rows, :] = unit.astype(BF)
            resid = band_ref[rows, :].astype(FL) + unit * small_ref[1:2, :] + small_ref[2:3, :]
            resid_ref[rows, :] = resid
            low = resid.astype(BF)
            low_ref[rows, :] = low
            logits = jnp.where(lane < experts, mm(low, router_ref[...]), -1e30)
            powers = jnp.exp(logits - jnp.max(logits, -1, keepdims=True))
            probs = powers / jnp.sum(powers, -1, keepdims=True)
            gate = jnp.sum(
                jnp.where(lane == expert_ref[rows, :], probs, 0.0), -1, keepdims=True
            )
            aux_ref[rows, :] = jnp.where(
                lane == LANES - 1, gate, jnp.where(lane == LANES - 2, inverse, probs)
            )
            return carry

        lax.fori_loop(0, half // CHUNK, step, 0)
    pack_rows(dest_row_ref, low_ref, sent_refs)


def merge_body(*refs, experts, band_cols, members):
    returned_refs, refs = refs[:members], refs[members:]
    (
        dest_col_ref,
        dest_row_ref,
        expert_ref,
        aux_ref,
        resid_ref,
        small_ref,
        weight_ref,
        wide_ref,
        cotangent_ref,
        final_ref,
        merged_ref,
        dreduced_ref,
        dresid_ref,
        dlogits_ref,
        sums_ref,
    ) = refs[:15]
    sent_refs = refs[15 : 15 + members]
    unit_scr, picked_scr, inverse_scr, token_scr, back_scr = refs[15 + members :]
    returned = jnp.concatenate([ref[...] for ref in returned_refs], 0)
    tokens, channels = resid_ref.shape
    tiles = tiles_of(channels)
    lane = lax.broadcasted_iota(jnp.int32, (CHUNK, LANES), 1)

    def combine(c, carry):
        rows = rows_at(c * CHUNK, CHUNK)
        picked = unpack_rows(dest_col_ref[rows, :], returned)
        picked_scr[rows, :] = picked
        gate = aux_ref[rows, :][:, LANES - 1 : LANES]
        unit, inverse = normalised(gate * picked)
        unit_scr[rows, :] = unit
        inverse_scr[rows, :] = jnp.broadcast_to(inverse, (CHUNK, LANES))
        resid = resid_ref[rows, :] + unit * small_ref[0:1, :] + small_ref[1:2, :]
        for t, lanes in enumerate(tiles):
            token_scr[t, rows, :] = resid[:, lanes]
        return carry

    lax.fori_loop(0, tokens // CHUNK, combine, 0)
    pairs = band_cols // 2
    for i in range(WINDOW_SIDE // 2):
        for k in range(4):
            start = (2 * i + k % 2) * band_cols + k // 2
            for t in range(len(tiles)):
                at = k * channels + t * LANES
                merged_ref[i * pairs : (i + 1) * pairs, at : at + LANES] = token_scr[
                    t, pl.ds(start, pairs, stride=2), :
                ].astype(BF)
    unit, inverse = normalised(mm(merged_ref[...], weight_ref[...]))
    final_ref[...] = (unit * wide_ref[0:1, :] + wide_ref[1:2, :]).astype(BF)
    back = cotangent_ref[...].astype(FL)
    sums_ref[...] = jnp.zeros_like(sums_ref)
    sums_ref[0:1, :] = jnp.sum(back * unit, 0, keepdims=True)
    sums_ref[1:2, :] = jnp.sum(back, 0, keepdims=True)
    dreduced = normalised_back(back, wide_ref[0:1, :], unit, inverse).astype(BF)
    dreduced_ref[...] = dreduced
    for k in range(4):
        part = mm_nt(dreduced, weight_ref[k * channels : (k + 1) * channels, :])
        for i in range(WINDOW_SIDE // 2):
            start = (2 * i + k % 2) * band_cols + k // 2
            for t, lanes in enumerate(tiles):
                token_scr[t, pl.ds(start, pairs, stride=2), :] = part[
                    i * pairs : (i + 1) * pairs, lanes
                ]

    def spread(c, carry):
        rows = rows_at(c * CHUNK, CHUNK)
        back = jnp.concatenate([token_scr[t, rows, :] for t in range(len(tiles))], 1)
        dresid_ref[rows, :] = back
        unit = unit_scr[rows, :]
        sums_ref[2:3, 0:channels] += jnp.sum(back * unit, 0, keepdims=True)
        sums_ref[3:4, 0:channels] += jnp.sum(back, 0, keepdims=True)
        back = normalised_back(back, small_ref[0:1, :], unit, inverse_scr[rows, :][:, 0:1])
        aux = aux_ref[rows, :]
        gate = aux[:, LANES - 1 : LANES]
        dgate = jnp.sum(back * picked_scr[rows, :], -1, keepdims=True)
        back_scr[rows, :] = (back * gate).astype(BF)
        probs = jnp.where(lane < experts, aux, 0.0)
        chosen = jnp.where(lane == expert_ref[rows, :], 1.0, 0.0)
        dlogits_ref[rows, :] = (probs * (chosen - gate) * dgate).astype(BF)
        return carry

    lax.fori_loop(0, tokens // CHUNK, spread, 0)
    pack_rows(dest_row_ref, back_scr, sent_refs)


def settle_body(*refs, members):
    sent_refs, refs = refs[:members], refs[members:]
    (
        dest_col_ref,
        dresid_ref,
        dlogits_ref,
        router_ref,
        unit_ref,
        aux_ref,
        small_ref,
        weight_ref,
        done_ref,
        low_ref,
        rows_ref,
        sums_ref,
    ) = refs
    sent = jnp.concatenate([ref[...] for ref in sent_refs], 0)
    tokens, channels = dresid_ref.shape
    sums_ref[...] = jnp.zeros_like(sums_ref)

    def step(c, carry):
        rows = rows_at(c * CHUNK, CHUNK)
        back = dresid_ref[rows, :] + unpack_rows(dest_col_ref[rows, :], sent)
        back = back + mm_nt(dlogits_ref[rows, :], router_ref[...])
        done_ref[rows, :] = back
        unit = unit_ref[rows, :].astype(FL)
        sums_ref[1:2, :] += jnp.sum(back * unit, 0, keepdims=True)
        sums_ref[2:3, :] += jnp.sum(back, 0, keepdims=True)
        inverse = aux_ref[rows, :][:, LANES - 2 : LANES - 1]
        back = normalised_back(back, small_ref[1:2, :], unit, inverse)
        sums_ref[0:1, :] += jnp.sum(back, 0, keepdims=True)
        low = back.astype(BF)
        low_ref[rows, :] = low
        rows_ref[rows, :] = mm_nt(low, weight_ref[...]).astype(BF)
        return carry

    lax.fori_loop(0, tokens // CHUNK, step, 0)


def dense_body(*refs):
    (*ins, proj_ref, router_ref) = refs
    arrived, own, low, resid, dlogits = (ins[i::5] for i in range(5))
    half = arrived[0].shape[0]
    proj = router = None
    for a, o, b, r, d in zip(arrived, own, low, resid, dlogits):
        now = mm_tn(a[...], b[0:half, :]) + mm_tn(o[...], b[half:, :])
        then = mm_tn(r[...], d[...])
        proj = now if proj is None else proj + now
        router = then if router is None else router + then
    proj_ref[...] = proj.astype(BF)
    router_ref[...] = router.astype(BF)


def merge_weight_body(*refs):
    (*ins, out_ref) = refs
    total = None
    for left, right in zip(ins[0::2], ins[1::2]):
        now = mm_tn(left[...], right[...])
        total = now if total is None else total + now
    out_ref[...] = total.astype(BF)


def merge_weight_grad(merged, dreduced, channels, after):
    args, specs = [], []
    for left, right in zip(merged, dreduced):
        args += [left, right]
        specs += [
            pl.BlockSpec((left.shape[0], channels), lambda k: (0, k)),
            pl.BlockSpec(right.shape, lambda k: (0, 0)),
        ]
    return pl.pallas_call(
        skipping(merge_weight_body, len(args), len(after)),
        name="merge_weight_grad",
        grid=(4,),
        out_shape=jax.ShapeDtypeStruct((merged[0].shape[1], dreduced[0].shape[1]), BF),
        in_specs=specs + [pl.BlockSpec(memory_space=pl.ANY)] * len(after),
        out_specs=pl.BlockSpec((channels, dreduced[0].shape[1]), lambda k: (k, 0)),
        compiler_params=pltpu.CompilerParams(vmem_limit_bytes=VMEM_BYTES),
        cost_estimate=cost(5),
    )(*args, *after)


PIECE = 384


def spot_of(member, me, bits):
    apart = member ^ me
    spot = 0
    for k in range(bits):
        spot = spot | (((apart >> k) & 1) << (bits - 1 - k))
    return spot


def piece_home(expert, chunk, row_size, chunks):
    piece = expert * chunks + chunk
    return piece % row_size, piece // row_size


def take_weights(own_ref, other_refs, out_scr, expert, local, me, first):
    row_size = len(other_refs)
    chunks = out_scr.shape[1 if first else 0] // PIECE

    @pl.when(expert < local)
    def _():
        out_scr[...] = own_ref[0]

    for chunk in range(chunks):
        member, _ = piece_home(jnp.maximum(expert - local, 0), chunk, row_size, chunks)
        spot = spot_of(member, me, row_size.bit_length() - 1)
        span = slice(chunk * PIECE, (chunk + 1) * PIECE)
        for k, ref in enumerate(other_refs):

            @pl.when((expert >= local) & (spot == k))
            def _(ref=ref, span=span):
                if first:
                    out_scr[:, span] = ref[0]
                else:
                    out_scr[span, :] = ref[0]


def taken(refs, *counts):
    lists = []
    for count in counts:
        lists.append(refs[:count])
        refs = refs[count:]
    return lists + [refs]


def joined(refs):
    return jnp.concatenate([ref[...] for ref in refs], 0)


def put_parts(refs, value):
    start = 0
    for ref in refs:
        ref[...] = value[start : start + ref.shape[0]].astype(BF)
        start += ref.shape[0]


def expert_forward_body(me_ref, *refs, local, members, row_size):
    row_refs, (in_ref, in_bias_ref, out_ref, out_bias_ref), in_others, out_others, refs = taken(
        refs, members, 4, row_size, row_size
    )
    result_refs, (hidden_ref, slope_ref, pre_scr, in_scr, out_scr) = taken(refs, members)
    expert = pl.program_id(0)
    take_weights(in_ref, in_others, in_scr, expert, local, me_ref[0], True)
    take_weights(out_ref, out_others, out_scr, expert, local, me_ref[0], False)
    pre_scr[...] = mm(joined(row_refs), in_scr[...]) + in_bias_ref[0]
    for chunk in range(in_scr.shape[1] // PIECE):
        lanes = slice(chunk * PIECE, (chunk + 1) * PIECE)
        pre = pre_scr[:, lanes]
        cdf = 0.5 * (1.0 + lax.erf(pre * 0.7071067811865476))
        hidden_ref[0, :, lanes] = (pre * cdf).astype(BF)
        slope_ref[0, :, lanes] = (
            cdf + pre * (0.3989422804014327 * jnp.exp(-0.5 * pre * pre))
        ).astype(BF)
    put_parts(result_refs, mm(hidden_ref[0], out_scr[...]) + out_bias_ref[0])


def expert_specs(members, slots, channels, hidden, local, row_size):
    chunks = hidden // PIECE

    def other_at(k, me):
        return (jnp.maximum(k - local, 0) * chunks // row_size, 0, 0)

    def own_at(k, me):
        return (jnp.minimum(k, local - 1), 0, 0)

    return dict(
        tokens=pl.BlockSpec((slots, channels), lambda k, me: (k, 0)),
        wide=pl.BlockSpec((1, members * slots, hidden), lambda k, me: (k, 0, 0)),
        first=pl.BlockSpec((1, channels, hidden), own_at),
        second=pl.BlockSpec((1, hidden, channels), own_at),
        other=pl.BlockSpec((1, PIECE, PIECE), other_at),
        bias=pl.BlockSpec((1, 1, hidden), lambda k, me: (k, 0, 0)),
        low_bias=pl.BlockSpec((1, 1, channels), lambda k, me: (k, 0, 0)),
    )


def call_expert(
    body, name, me, steps, in_specs, out_specs, outs, scratch, args, micros, after=()
):
    return pl.pallas_call(
        skipping(body, 1 + len(args), len(after)),
        name=name,
        grid_spec=pltpu.PrefetchScalarGridSpec(
            num_scalar_prefetch=1,
            grid=(steps,),
            in_specs=in_specs + [pl.BlockSpec(memory_space=pl.ANY)] * len(after),
            out_specs=out_specs,
            scratch_shapes=scratch,
        ),
        out_shape=outs,
        compiler_params=pltpu.CompilerParams(vmem_limit_bytes=VMEM_BYTES),
        cost_estimate=cost(micros),
    )(me, *args, *after)


def expert_forward(
    me, rows, first, second, first_other, second_other, first_bias, second_bias, after
):
    members, row_size = len(rows), len(first_other)
    local, channels, hidden = first.shape
    slots = rows[0].shape[0] // (2 * local)
    count = members * slots
    spec = expert_specs(members, slots, channels, hidden, local, row_size)
    wide = jax.ShapeDtypeStruct((2 * local, count, hidden), BF)
    outs = call_expert(
        functools.partial(
            expert_forward_body, local=local, members=members, row_size=row_size
        ),
        "expert_forward",
        me,
        2 * local,
        [spec["tokens"]] * members
        + [spec["first"], spec["bias"], spec["second"], spec["low_bias"]]
        + [spec["other"]] * (2 * row_size),
        [spec["tokens"]] * members + [spec["wide"], spec["wide"]],
        [jax.ShapeDtypeStruct(rows[0].shape, BF)] * members + [wide, wide],
        [
            pltpu.VMEM((count, hidden), FL),
            pltpu.VMEM((channels, hidden), BF),
            pltpu.VMEM((hidden, channels), BF),
        ],
        [*rows, first, first_bias, second, second_bias, *first_other, *second_other],
        19,
        after,
    )
    return outs[:members], outs[members], outs[members + 1]


def expert_backward_body(me_ref, *refs, local, members, row_size):
    row_refs, (in_ref, out_ref, slope_ref), in_others, out_others, refs = taken(
        refs, members, 3, row_size, row_size
    )
    result_refs, (dpre_ref, dbias_ref, dhidden_scr, in_scr, out_scr) = taken(refs, members)
    expert = pl.program_id(0)
    take_weights(in_ref, in_others, in_scr, expert, local, me_ref[0], True)
    take_weights(out_ref, out_others, out_scr, expert, local, me_ref[0], False)
    dhidden_scr[...] = mm_nt(joined(row_refs), out_scr[...])
    for chunk in range(in_scr.shape[1] // PIECE):
        lanes = slice(chunk * PIECE, (chunk + 1) * PIECE)
        dpre = dhidden_scr[:, lanes] * slope_ref[0, :, lanes].astype(FL)
        dbias_ref[0, :, lanes] = jnp.sum(dpre, 0, keepdims=True)
        dpre_ref[0, :, lanes] = dpre.astype(BF)
    put_parts(result_refs, mm_nt(dpre_ref[0], in_scr[...]))


def expert_backward(me, rows, first, second, first_other, second_other, slope, after):
    members, row_size = len(rows), len(first_other)
    local, channels, hidden = first.shape
    slots = rows[0].shape[0] // (2 * local)
    count = members * slots
    spec = expert_specs(members, slots, channels, hidden, local, row_size)
    outs = call_expert(
        functools.partial(
            expert_backward_body, local=local, members=members, row_size=row_size
        ),
        "expert_backward",
        me,
        2 * local,
        [spec["tokens"]] * members
        + [spec["first"], spec["second"], spec["wide"]]
        + [spec["other"]] * (2 * row_size),
        [spec["tokens"]] * members + [spec["wide"], spec["bias"]],
        [jax.ShapeDtypeStruct(rows[0].shape, BF)] * members
        + [
            jax.ShapeDtypeStruct((2 * local, count, hidden), BF),
            jax.ShapeDtypeStruct((2 * local, 1, hidden), FL),
        ],
        [
            pltpu.VMEM((count, hidden), FL),
            pltpu.VMEM((channels, hidden), BF),
            pltpu.VMEM((hidden, channels), BF),
        ],
        [*rows, first, second, slope, *first_other, *second_other],
        12,
        after,
    )
    return outs[:members], outs[members], outs[members + 1]


def expert_weight_body(me_ref, *refs, local, members, micros, tokens_left):
    token_refs, wide_refs, (keep_ref, send_ref, dbias_ref) = taken(
        refs, members * micros, micros
    )
    expert = pl.program_id(0)
    half = keep_ref.shape[1]
    row_size = 2 * half
    chunks = wide_refs[0].shape[2] // PIECE
    rows = [joined(token_refs[m * members : (m + 1) * members]) for m in range(micros)]
    dbias_ref[0] = sum(jnp.sum(part.astype(FL), 0, keepdims=True) for part in rows)
    total = None
    for part, ref in zip(rows, wide_refs):
        now = mm_tn(part, ref[0]) if tokens_left else mm_tn(ref[0], part)
        total = now if total is None else total + now
    low = total.astype(BF)
    for chunk in range(chunks):
        span = slice(chunk * PIECE, (chunk + 1) * PIECE)
        piece = low[:, span] if tokens_left else low[span, :]
        member, _ = piece_home(expert % local, chunk, row_size, chunks)
        spot = spot_of(member, me_ref[0], row_size.bit_length() - 1)

        @pl.when(spot < half)
        def _(piece=piece, spot=spot):
            keep_ref[0, spot, 0] = piece

        @pl.when(spot >= half)
        def _(piece=piece, spot=spot):
            send_ref[0, spot - half, 0] = piece


def expert_weight_grads(me, tokens, wide, local, row_size, tokens_left, after):
    members, micros = len(tokens[0]), len(tokens)
    together, channels = tokens[0][0].shape
    slots = together // (2 * local)
    width = wide[0].shape[-1]
    chunks = width // PIECE
    subs = local * chunks // row_size
    spec = expert_specs(members, slots, channels, width, local, row_size)
    half_shape = (2, row_size // 2, subs, PIECE, PIECE)
    half_spec = pl.BlockSpec(
        (1, row_size // 2, 1, PIECE, PIECE),
        lambda k, me: (k // local, 0, (k % local) * chunks // row_size, 0, 0),
    )
    half_out = jax.ShapeDtypeStruct(half_shape, BF)
    return call_expert(
        functools.partial(
            expert_weight_body,
            local=local,
            members=members,
            micros=micros,
            tokens_left=tokens_left,
        ),
        "expert_weight_grads",
        me,
        2 * local,
        [spec["tokens"]] * (members * micros) + [spec["wide"]] * micros,
        [half_spec] * 2 + [spec["low_bias"]],
        [half_out] * 2 + [jax.ShapeDtypeStruct((2 * local, 1, channels), FL)],
        [],
        [part for parts in tokens for part in parts] + list(wide),
        13,
        after,
    )


def add_pieces_body(keep_ref, got_ref, *out_refs):
    half = keep_ref.shape[1] // 2
    for group in range(2):
        if half:
            for k in range(half):
                out_refs[0][group, k] = plus(keep_ref[group, k], got_ref[group, k]).astype(BF)
                at = half + k
                out_refs[1][group, k] = plus(keep_ref[group, at], got_ref[group, at]).astype(BF)
        else:
            total = plus(keep_ref[group, 0], got_ref[group, 0])
            out_refs[group][...] = total.astype(out_refs[group].dtype)


def add_pieces(keep, got, after):
    groups, count = keep.shape[:2]
    if count > 1:
        shape = (groups, count // 2) + keep.shape[2:]
        outs = [(shape, BF), (shape, BF)]
    else:
        outs = [(keep.shape[2:], FL), (keep.shape[2:], BF)]
    return call_kernel(add_pieces_body, "add_pieces", outs, [keep, got], micros=3, after=after)


def add_halves_body(own_ref, got_ref, out_ref):
    out_ref[...] = plus(own_ref[...], got_ref[...]).astype(out_ref.dtype)


def add_halves(own, got, after, dtype=BF, micros=2):
    (total,) = call_kernel(
        add_halves_body, "add_halves", [(own.shape, dtype)], [own, got], micros=micros, after=after
    )
    return total


def add_blocks_body(*refs):
    (*block_refs, mine_ref, other_ref) = refs
    for half, ref in enumerate((mine_ref, other_ref)):
        ref[...] = sum(block[half].astype(FL) for block in block_refs).astype(ref.dtype)


def add_blocks(blocks, after):
    shape = blocks[0].shape[1:]
    return call_kernel(
        add_blocks_body,
        "add_blocks",
        [(shape, FL), (shape, BF)],
        blocks,
        micros=0.2,
        after=after,
    )


def place_body(me_ref, *refs, chunks, first):
    (*piece_refs, full_ref) = refs
    row_size = len(piece_refs)
    for c in range(chunks):
        member, _ = piece_home(pl.program_id(0), c, row_size, chunks)
        spot = spot_of(member, me_ref[0], row_size.bit_length() - 1)
        span = slice(c * PIECE, (c + 1) * PIECE)
        value = piece_refs[0][0]
        for k in range(1, row_size):
            value = jnp.where(spot == k, piece_refs[k][0], value)
        if first:
            full_ref[0, :, span] = value.astype(FL)
        else:
            full_ref[0, span, :] = value.astype(FL)


def place_pieces(me, pieces, local, hidden, first, after):
    row_size = len(pieces)
    chunks = hidden // PIECE
    shape = (local, PIECE, hidden) if first else (local, hidden, PIECE)
    return call_expert(
        functools.partial(place_body, chunks=chunks, first=first),
        "place_pieces",
        me,
        local,
        [pl.BlockSpec((1, PIECE, PIECE), lambda e, me: (e * chunks // row_size, 0, 0))]
        * row_size,
        [pl.BlockSpec((1,) + shape[1:], lambda e, me: (e, 0, 0))],
        [jax.ShapeDtypeStruct(shape, FL)],
        [],
        list(pieces),
        4,
        after,
    )[0]


def swapped(rows):
    return lax.all_to_all(rows, "dp", split_axis=0, concat_axis=0, tiled=True)


def exchanged(blocks):
    return [blocks[0]] + [crossed(block, "dp", k) for k, block in enumerate(blocks) if k]


def bits_of(axis):
    return [1 << k for k in reversed(range(lax.axis_size(axis).bit_length() - 1))]


def spread_over_row(piece):
    held = [piece]
    for bit in bits_of("row"):
        held = held + [crossed(part, "row", bit) for part in held]
    return held


def join_body(me_ref, *refs, count):
    part_refs, out_refs = taken(refs, count)
    width = part_refs[0].shape[1]
    for c in range(count):
        spot = spot_of(c, me_ref[0], count.bit_length() - 1)
        value = part_refs[0][...]
        for k in range(1, count):
            value = jnp.where(spot == k, part_refs[k][...], value)
        start = 0
        for ref in out_refs:
            low, high = max(start, c * width), min(start + ref.shape[1], (c + 1) * width)
            if low < high:
                ref[:, low - start : high - start] = value[:, low - c * width : high - c * width]
            start += ref.shape[1]


def join_columns(me, parts, widths):
    rows = parts[0].shape[0]
    vmem = pl.BlockSpec(memory_space=pltpu.VMEM)
    return pl.pallas_call(
        functools.partial(join_body, count=len(parts)),
        name="join_columns",
        in_specs=[pl.BlockSpec(memory_space=pltpu.SMEM)] + [vmem] * len(parts),
        out_specs=[vmem] * len(widths),
        out_shape=[jax.ShapeDtypeStruct((rows, width), BF) for width in widths],
        cost_estimate=cost(2),
    )(me, *parts)


def gathered(shard):
    count = lax.axis_size("dp")
    copies = jnp.broadcast_to(shard[None], (count,) + shard.shape)
    return swapped(copies).reshape(count * shard.shape[0], shard.shape[1])


def side_by_side_body(*refs):
    (*ins, out_ref) = refs
    start = 0
    for ref in ins:
        out_ref[:, start : start + ref.shape[1]] = ref[...]
        start += ref.shape[1]


def copy_body(in_ref, out_ref):
    out_ref[...] = in_ref[...]


def held_back(array, after):
    (copy,) = call_kernel(
        copy_body, "hold", [(array.shape, array.dtype)], [array], micros=1, after=after
    )
    return copy


def crossed(array, axis, bit):
    count = lax.axis_size(axis)
    return lax.ppermute(array, axis, [(i, i ^ bit) for i in range(count)])


def summed(array, axes):
    for axis in axes:
        bit = 1
        while bit < lax.axis_size(axis):
            array = array + crossed(array, axis, bit)
            bit *= 2
    return array


def dense_blocks(grad):
    count = lax.axis_size("dp")
    half = count // 2
    place = lax.axis_index("dp")
    rows = grad.shape[0] // count
    grad = grad.reshape(2, half, rows, grad.shape[1])
    mine, other = place // half, 1 - place // half
    blocks = [
        jnp.concatenate(
            [
                lax.dynamic_slice(
                    grad, (h, (place % half) ^ k, 0, 0), (1, 1, rows, grad.shape[3])
                )[0]
                for h in (mine, other)
            ]
        )
        for k in range(half)
    ]
    return exchanged(blocks)


def dense_spread(part):
    held = spread_over_row(part)
    sums = held
    while len(sums) > 1:
        sums = [plus(left, right) for left, right in zip(sums[::2], sums[1::2])]
    return sums[0].astype(FL), held


def on_device(
    patches,
    unpadded_patch_size,
    patch_expert_index,
    cotangent,
    query_key_value_weight,
    query_projection_bias,
    value_projection_bias,
    log_cosine_scale,
    bias_network_first_weight,
    bias_network_first_bias,
    bias_network_second_weight,
    output_projection_weight,
    output_projection_bias,
    attention_norm_gain,
    attention_norm_bias,
    routing_weight,
    expert_first_weight,
    expert_first_bias,
    expert_second_weight,
    expert_second_bias,
    expert_norm_gain,
    expert_norm_bias,
    patch_merging_weight,
    merging_norm_gain,
    merging_norm_bias,
):
    micro_count, _, band_rows, band_cols, channels = patches.shape
    micros = range(micro_count)
    half_rows = band_rows // 2
    win_count = band_cols // WINDOW_SIDE
    win_area = WINDOW_SIDE * WINDOW_SIDE
    tokens = band_rows * band_cols
    half = tokens // 2
    experts = routing_weight.shape[1]
    dp_size = lax.axis_size("dp")
    local = experts // dp_size
    capacity = (5 * tokens + 4 * experts - 1) // (4 * experts)
    slots = -(-capacity // 16) * 16
    block_rows = 2 * local * slots
    members = dp_size // 2
    row_size = lax.axis_size("row")
    me = lax.axis_index("row").astype(jnp.int32)[None]
    my_place = lax.axis_index("dp").astype(jnp.int32)
    my_place = jnp.stack([my_place // members, my_place % members])
    total_rows = band_rows * lax.axis_size("row")
    row_start = band_rows * lax.axis_index("row")

    wide = 4 * channels + LANES
    shard = jnp.concatenate(
        [query_key_value_weight, output_projection_weight, routing_weight], 1
    )
    parts = -(-wide // (8 * LANES)) * 8 * LANES
    shard = jnp.pad(shard, ((0, 0), (0, parts - shard.shape[1])))
    parts //= row_size
    shard = lax.dynamic_slice(shard, (0, me[0] * parts), (shard.shape[0], parts))
    columns = gathered(shard)
    held = spread_over_row(columns)
    weight_qkv, weight_proj, weight_router = join_columns(
        me, held, [3 * channels, channels, LANES]
    )

    bands = patches.reshape(micro_count, tokens, channels)
    below = passed_along(bands[:, :half], "row", -1)

    zones = [
        mask_operands(
            row_start,
            total_rows,
            band_cols,
            unpadded_patch_size[m, 0, 0],
            unpadded_patch_size[m, 0, 1],
        )
        for m in micros
    ]

    dest_cols, dest_rows, chosen_cols = [], [], []
    for m in micros:
        chosen = patch_expert_index[m].reshape(1, tokens)
        column, dest_col, dest_row = slot_tables(
            chosen, my_place, experts, local, slots, capacity, columns
        )
        chosen_cols.append(column)
        dest_cols.append(dest_col)
        dest_rows.append(dest_row)

    network_first = jnp.concatenate(
        [bias_network_first_weight, bias_network_first_bias[None]], 0
    )
    tile_count = channels // LANES
    bias_shape = ((tile_count, win_area, TILE_HEADS * win_area), FL)
    bias_rows, bias_keys = call_kernel(
        spread_body, "spread_bias", [bias_shape, bias_shape], [network_first, bias_network_second_weight], after=[held[1], dest_rows[-1]]
    )
    hidden = expert_first_weight.shape[-1]
    chunks = hidden // PIECE
    subs = local * chunks // row_size
    first_piece, second_piece = [], []
    for sub in range(subs):
        piece = sub * row_size + me[0]
        at, start = piece // chunks, (piece % chunks) * PIECE
        first_piece.append(
            lax.dynamic_slice(expert_first_weight, (at, 0, start), (1, channels, PIECE))
        )
        second_piece.append(
            lax.dynamic_slice(expert_second_weight, (at, start, 0), (1, PIECE, channels))
        )
    first_got = crossed(held_back(jnp.concatenate(first_piece), [columns]), "dp", members)
    second_got = crossed(held_back(jnp.concatenate(second_piece), [first_got]), "dp", members)
    first_other = spread_over_row(first_got)
    second_other = spread_over_row(second_got)
    expert_bias = jnp.concatenate([expert_first_bias, expert_second_bias], 1)
    expert_bias = jnp.concatenate([expert_bias, crossed(expert_bias, "dp", members)], 0)

    lane = jnp.arange(LANES)
    head_marks = jnp.repeat(
        (lane // HEAD_DIM)[None, :] == jnp.arange(TILE_HEADS)[:, None], win_area, 0
    ).astype(BF)
    block_ones = (
        ((jnp.arange(2 * LANES) % LANES) // HEAD_DIM)[:, None] == (lane // HEAD_DIM)[None, :]
    ).astype(BF)
    scale_lanes = jnp.repeat(jnp.exp(log_cosine_scale), HEAD_DIM)[None, :]
    qbias = query_projection_bias[None, :]
    vbias = value_projection_bias[None, :]
    attn_small = jnp.stack([output_projection_bias, attention_norm_gain, attention_norm_bias])
    moe_small = jnp.stack([expert_norm_gain, expert_norm_bias])
    merge_small = jnp.stack([merging_norm_gain, merging_norm_bias])
    first_bias = expert_bias[:, None, :hidden]
    second_bias = expert_bias[:, None, hidden:]

    grid_scratch = ((channels // LANES, band_rows * (band_cols + 8), LANES), FL)
    win_scratch = ((channels // LANES, tokens, LANES), FL)

    none = [None] * micro_count
    attended, arrived, routed, received = list(none), list(none), list(none), list(none)
    expert_out, returned, merged, back_res = list(none), list(none), list(none), list(none)
    expert_back, back_sent, settled, finished = list(none), list(none), list(none), list(none)
    outputs, input_grads, input_parts = list(none), list(none), list(none)

    forward_after = [[first_got, *dest_rows], []]
    route_after = [[second_got, first_other[1]], []]
    for m in micros:
        attended[m] = call_kernel(
            functools.partial(attend_forward_body, band_cols=band_cols, channels=channels),
            "attend_forward",
            [
                ((half, channels), BF),
                ((half, channels), BF),
                ((tokens, channels), BF),
                ((tokens, 3 * channels), BF),
                ((tokens, 2 * channels), FL),
            ],
            [
                bands[m],
                below[m],
                weight_qkv,
                qbias,
                vbias,
                scale_lanes,
                bias_rows,
                *zones[m],
                head_marks,
                block_ones,
            ],
            [grid_scratch, win_scratch],
            micros=16,
            after=(forward_after[m] if m < 2 else []) + [a[0] for a in attended[:m][-1:]],
        )
        arrived[m] = passed_along(attended[m][1], "row", 1)
    for m in micros:
        routed[m] = call_kernel(
            functools.partial(route_body, experts=experts),
            "route",
            [
                ((tokens, channels), FL),
                ((tokens, channels), BF),
                ((tokens, LANES), FL),
                ((tokens, channels), BF),
            ]
            + [((block_rows, channels), BF)] * members,
            [
                arrived[m],
                attended[m][0],
                bands[m],
                weight_proj,
                attn_small,
                weight_router,
                chosen_cols[m],
                dest_rows[m],
            ],
            micros=12,
            after=[attended[-1][0] if m == 0 else routed[m - 1][2]]
            + (route_after[m] if m < 2 else [])
            + (received[m - 1][1:] if m else []),
        )
        if m == 0:
            shard = held_back(patch_merging_weight, [routed[m][2]])
            weight_merge = lax.all_gather(shard, "dp", axis=0, tiled=True)
        received[m] = exchanged(routed[m][4:])
    for m in micros:
        expert_out[m] = expert_forward(
            me,
            received[m],
            expert_first_weight,
            expert_second_weight,
            first_other,
            second_other,
            first_bias,
            second_bias,
            [routed[-1][2] if m == 0 else expert_out[m - 1][0][0]],
        )
        returned[m] = exchanged(expert_out[m][0])
    for m in micros:
        merged[m] = call_kernel(
            functools.partial(
                merge_body, experts=experts, band_cols=band_cols, members=members
            ),
            "merge",
            [
                ((tokens // 4, 2 * channels), BF),
                ((tokens // 4, 4 * channels), BF),
                ((tokens // 4, 2 * channels), BF),
                ((tokens, channels), FL),
                ((tokens, LANES), BF),
                ((8, 2 * channels), FL),
            ]
            + [((block_rows, channels), BF)] * members,
            [
                *returned[m],
                dest_cols[m],
                dest_rows[m],
                chosen_cols[m],
                routed[m][2],
                routed[m][0],
                moe_small,
                weight_merge,
                merge_small,
                cotangent[m, 0].reshape(tokens // 4, 2 * channels),
            ],
            [
                ((tokens, channels), FL),
                ((tokens, channels), FL),
                ((tokens, LANES), FL),
                ((channels // LANES, tokens, LANES), FL),
                ((tokens, channels), BF),
            ],
            micros=14,
            after=[expert_out[-1][0][0] if m == 0 else merged[m - 1][0]],
        )
        outputs[m] = merged[m][0].reshape(band_rows // 2, band_cols // 2, 2 * channels)
        back_res[m] = exchanged(merged[m][6:])
    for m in micros:
        expert_back[m] = expert_backward(
            me,
            back_res[m],
            expert_first_weight,
            expert_second_weight,
            first_other,
            second_other,
            expert_out[m][2],
            [merged[-1][0] if m == 0 else expert_back[m - 1][2]],
        )
        back_sent[m] = exchanged(expert_back[m][0])

    def settle(m, after):
        return call_kernel(
            functools.partial(settle_body, members=members),
            "settle",
            [
                ((tokens, channels), FL),
                ((tokens, channels), BF),
                ((tokens, channels), BF),
                ((8, channels), FL),
            ],
            [
                *back_sent[m],
                dest_cols[m],
                merged[m][3],
                merged[m][4],
                weight_router,
                routed[m][1],
                routed[m][2],
                attn_small,
                weight_proj,
            ],
            micros=7,
            after=after,
        )

    settled[0] = settle(0, [expert_back[-1][2]])
    in_keep, in_send, _ = expert_weight_grads(
        me, received, [b[1] for b in expert_back], local, row_size, True, [settled[0][3]]
    )
    for m in micros[1:]:
        settled[m] = settle(m, [in_keep])
    grad_merge = merge_weight_grad(
        [b[1] for b in merged], [b[2] for b in merged], channels, [settled[-1][3]]
    )
    out_keep, out_send, grad_eout_bias = expert_weight_grads(
        me, back_res, [b[1] for b in expert_out], local, row_size, False, [grad_merge]
    )

    merge_blocks = dense_blocks(grad_merge)

    state = dict(
        first=dict(keep=in_keep, send=in_send), second=dict(keep=out_keep, send=out_send)
    )
    row_bits = list(reversed(bits_of("row")))
    latest = out_keep

    def transfer(kind):
        at = state[kind]
        step = at.setdefault("step", 0)
        if step < len(row_bits):
            at["got"] = crossed(at["send"], "row", row_bits[step])
        else:
            at["got"] = crossed(at["send"], "dp", members)

    def advance(kind):
        nonlocal latest
        at = state[kind]
        if at["step"] < len(row_bits):
            at["keep"], at["send"] = add_pieces(at["keep"], at["got"], [latest])
            latest = at["send"]
        else:
            at["held"] = spread_over_row(add_halves(at["keep"], at["got"], [latest]))
            latest = at["held"][0]
            return
        at["step"] += 1
        transfer(kind)

    transfer("first")
    transfer("second")
    plan = {
        "start": ["first"],
        (0, 1): ["first", "second"],
        (1, 0): ["first", "second"],
    }
    for _ in range(len(row_bits) - 2):
        plan[(0, 1)] = plan[(0, 1)] + ["first", "second"]

    def advance_at(place):
        nonlocal latest, merge_sums, sum_merge
        if place == (0, 0):
            merge_sums = add_blocks(merge_blocks, [latest])
            latest = merge_sums[0]
        elif place == (0, tile_count - 1):
            mine, other = merge_sums
            latest = add_halves(mine, crossed(other, "dp", members), [latest])
            sum_merge, _ = dense_spread(latest)
        for kind in plan.get(place, ()):
            advance(kind)

    merge_sums = sum_merge = None

    advance_at("start")
    dense_args = []
    for m in micros:
        dense_args += [arrived[m], attended[m][0], settled[m][1], routed[m][3], merged[m][4]]
    grad_proj, grad_router = call_kernel(
        dense_body,
        "dense_weight_grads",
        [((channels, channels), BF), ((channels, LANES), BF)],
        dense_args,
        micros=4,
        after=[latest],
    )
    latest = grad_router

    tile_sums = [None] * tile_count
    tile_smalls = []
    weight_grads = [grad_proj, grad_router]
    for m in micros:
        lifted = passed_along(settled[m][2][:half], "row", -1)
        (back_windows,) = call_kernel(
            functools.partial(window_body, band_cols=band_cols, channels=channels),
            "window_grads",
            [((tokens, channels), BF)],
            [settled[m][2][half:], lifted],
            [grid_scratch, win_scratch],
            micros=3,
            after=[latest],
        )
        latest = back_windows
        win, qkv, inverse = attended[m][2:]
        last = m == micro_count - 1
        grads = []
        for t in range(tile_count):

            def part(array, rows, at):
                return (array, pl.BlockSpec((rows, LANES), lambda i, at=at: (0, at)))

            args = [
                part(back_windows, tokens, t),
                part(qkv, tokens, t),
                part(qkv, tokens, tile_count + t),
                part(qkv, tokens, 2 * tile_count + t),
                part(inverse, tokens, t),
                part(inverse, tokens, tile_count + t),
                part(scale_lanes, 1, t),
                win,
                (
                    bias_keys,
                    pl.BlockSpec((1,) + bias_shape[0][1:], lambda i, t=t: (t, 0, 0)),
                ),
                *zones[m],
                head_marks,
                block_ones,
            ]
            if m:
                args += tile_sums[t]
            dqkv, dweight, dbias, small = call_kernel(
                functools.partial(attend_backward_body, summed_before=m > 0),
                "attend_backward",
                [
                    ((tokens, 3 * LANES), BF),
                    ((channels, 3 * LANES), BF if last else FL),
                    (bias_shape[0][1:], FL),
                    ((8, LANES), FL),
                ],
                args,
                micros=0.5 if last and t else 10,
                after=[latest],
            )
            latest = small
            tile_sums[t] = [dweight, dbias]
            tile_smalls.append(small)
            grads.append(dqkv)
            if last:
                weight_grads.append(dweight)
            advance_at((m, t))
        if last:
            tall = SUM_ROWS + 2 * local * (hidden // channels + 1)
            (sums,) = call_kernel(
                functools.partial(
                    fold_body, tile_count=tile_count, micro_count=micro_count
                ),
                "fold_bias",
                [((-(-tall // 8) * 8, channels), FL)],
                [sums[1] for sums in tile_sums]
                + tile_smalls
                + [part[3] for part in settled]
                + [part[5] for part in merged]
                + [part[2] for part in expert_back]
                + [grad_eout_bias],
                micros=3,
                after=[latest, state["second"]["got"]],
            )
            latest = sums
            advance("second")
            (joined_grads,) = call_kernel(
                side_by_side_body,
                "join_grads",
                [((channels, sum(w.shape[1] for w in weight_grads)), BF)],
                weight_grads,
                micros=2,
                after=[latest],
            )
            latest = joined_grads
            dense = dense_blocks(joined_grads)
        input_parts[m] = call_kernel(
            functools.partial(input_grad_body, band_cols=band_cols, channels=channels),
            "input_grad",
            [((half, channels), FL), ((half, channels), BF)],
            grads + [weight_qkv],
            [grid_scratch, win_scratch],
            micros=5,
            after=[latest],
        )
        latest = input_parts[m][1]
        passed = passed_along(input_parts[m][1], "row", 1).astype(FL)
        input_grads[m] = (
            (settled[m][0] + jnp.concatenate([passed, input_parts[m][0]], 0))
            .astype(BF)
            .reshape(band_rows, band_cols, channels)
        )
    steps = [("row", 1 << k) for k in range(row_size.bit_length() - 1)]
    steps += [("dp", 1 << k) for k in range(dp_size.bit_length() - 1)]
    tail = ["blocks", "first", "part"]
    for k, (axis, bit) in enumerate(steps):
        if axis == "dp" and steps[k - 1][0] == "row":
            sums, biases = sums[:SUM_ROWS], sums[SUM_ROWS:tall]
        sums = latest = add_halves(sums, crossed(sums, axis, bit), [latest], FL, 0.2)
        job = tail.pop(0) if tail else None
        if job == "blocks":
            mine, other = add_blocks(dense, [latest])
            latest = mine
        elif job == "first":
            latest = sum_ein = place_pieces(
                me, state["first"]["held"], local, hidden, True, [latest]
            )
        elif job == "part":
            latest = part = add_halves(mine, crossed(other, "dp", members), [latest], BF, 0.2)
    sum_dense, held = dense_spread(part)
    sum_eout = place_pieces(me, state["second"]["held"], local, hidden, False, [latest])
    sum_proj = sum_dense[:, :channels]
    sum_router = sum_dense[:, channels : channels + experts]
    sum_qkv = sum_dense[:, channels + LANES :].reshape(-1, tile_count, 3, LANES)
    sum_qkv = sum_qkv.swapaxes(1, 2).reshape(-1, 3 * channels)
    in_bias = biases[: 2 * local * chunks].reshape(2 * local, hidden)
    out_bias = biases[2 * local * chunks :]
    other_bias = crossed(
        jnp.concatenate([in_bias[local:], out_bias[local:]], 1), "dp", members
    )
    sum_ein_bias = in_bias[:local] + other_bias[:, :hidden]
    sum_eout_bias = out_bias[:local] + other_bias[:, hidden:]
    grad_first, grad_second = call_kernel(
        bias_network_back_body,
        "bias_network_back",
        [(network_first.shape, FL), (bias_network_second_weight.shape, FL)],
        [sums, network_first, bias_network_second_weight],
        micros=0.2,
    )
    grad_first, grad_first_bias = grad_first[:2], grad_first[2]
    sum_qbias, sum_vbias, sum_scale = (
        sums[ATTN_AT],
        sums[ATTN_AT + 1],
        sums[ATTN_AT + 2, ::HEAD_DIM],
    )
    sum_proj_bias, sum_again, sum_ashift = (sums[SETTLE_AT + k] for k in range(3))
    sum_rgain = sums[MERGE_AT : MERGE_AT + 2].reshape(2 * channels)
    sum_rshift = sums[MERGE_AT + 2 : MERGE_AT + 4].reshape(2 * channels)
    sum_mgain, sum_mshift = sums[MERGE_AT + 4], sums[MERGE_AT + 5]
    return (
        jnp.stack(outputs)[:, None],
        jnp.stack(input_grads)[:, None],
        sum_qkv,
        sum_qbias,
        sum_vbias,
        sum_scale,
        grad_first,
        grad_first_bias,
        grad_second,
        sum_proj,
        sum_proj_bias,
        sum_again,
        sum_ashift,
        sum_router,
        sum_ein,
        sum_ein_bias,
        sum_eout,
        sum_eout_bias,
        sum_mgain,
        sum_mshift,
        sum_merge,
        sum_rgain,
        sum_rshift,
    )


def solution(mesh):
    return jax.shard_map(
        on_device,
        mesh=mesh,
        in_specs=(
            P(None, "dp", "row", None, None),
            P(None, "dp", None),
            P(None, "dp", "row", None, None),
            P(None, "dp", "row", None, None),
            P("dp", None),
            P(),
            P(),
            P(),
            P(),
            P(),
            P(),
            P("dp", None),
            P(),
            P(),
            P(),
            P("dp", None),
            P("dp", None, None),
            P("dp", None),
            P("dp", None, None),
            P("dp", None),
            P(),
            P(),
            P("dp", None),
            P(),
            P(),
        ),
        out_specs=(
            P(None, "dp", "row", None, None),
            P(None, "dp", "row", None, None),
            P("dp", None),
            P(),
            P(),
            P(),
            P(),
            P(),
            P(),
            P("dp", None),
            P(),
            P(),
            P(),
            P("dp", None),
            P("dp", None, None),
            P("dp", None),
            P("dp", None, None),
            P("dp", None),
            P(),
            P(),
            P("dp", None),
            P(),
            P(),
        ),
        check_vma=False,
    )
```

```python
import functools

import jax
import jax.numpy as jnp
from jax import lax
from jax.experimental import pallas as pl
from jax.experimental.pallas import tpu as pltpu
from jax.sharding import PartitionSpec as P

HEAD_COUNT = 12
HEAD_DIM = 32
WINDOW_SIDE = 12
LANES = 128
SHEAR = 384
ZONES = 16
UNROLL = 8
COST_SCALE = 0.4
TILE_HEADS = LANES // HEAD_DIM


PRECISION_HIGH = lax.Precision.HIGHEST
EPS_NORM = 1e-05
EPS_UNIT = 1e-06
MASK_FILL = -100.0
BF = jnp.bfloat16
FL = jnp.float32
VMEM_BYTES = 52 * 2**20


def cost(micros):
    return pl.CostEstimate(
        flops=int(micros * COST_SCALE * 1.1e9), bytes_accessed=10**5, transcendentals=0
    )


def passed_along(array, axis, by):
    count = lax.axis_size(axis)
    return lax.ppermute(array, axis, [(i, (i + by) % count) for i in range(count)])


def exact_error_gelu(values):
    return jax.nn.gelu(values, approximate=False)


SPANS = 2 * WINDOW_SIDE - 1
AREA = WINDOW_SIDE * WINDOW_SIDE


def span_coordinate(steps):
    size = jnp.abs(steps) * (8.0 / (WINDOW_SIDE - 1))
    value = jnp.log2(size + 1.0) / 3.0
    return jnp.where(steps < 0, -value, value)


def bias_network(first_ref, second_ref):
    shape = (2 * SHEAR, 1)
    row = lax.broadcasted_iota(jnp.int32, shape, 0)
    below = row >= SHEAR
    place = jnp.where(below, row - SHEAR + 1, row - (WINDOW_SIDE - 1))
    held = jnp.clip(place, 0, SPANS * WINDOW_SIDE - 1)
    column = held % WINDOW_SIDE
    valid = (held == place) & (jnp.logical_not(below) | (column > 0))
    rows_apart = (held // WINDOW_SIDE - (WINDOW_SIDE - 1)).astype(FL)
    columns_apart = jnp.where(below, column - WINDOW_SIDE, column).astype(FL)
    down, across = span_coordinate(rows_apart), span_coordinate(columns_apart)
    pre = down * first_ref[0:1, :] + across * first_ref[1:2, :] + first_ref[2:3, :]
    cdf = 0.5 * (1.0 + lax.erf(pre * 0.7071067811865476))
    hidden = pre * cdf
    slope = cdf + pre * (0.3989422804014327 * jnp.exp(-0.5 * pre * pre))
    level = jax.nn.sigmoid(
        lax.dot_general(
            hidden,
            second_ref[...],
            (((1,), (0,)), ((), ())),
            precision=PRECISION_HIGH,
            preferred_element_type=FL,
        )
    )
    return down, across, valid, hidden, slope, level


def mask_operands(row_start, total_rows, total_cols, valid_rows, valid_cols):
    half_win = WINDOW_SIDE // 2
    rows_at = row_start + jnp.arange(WINDOW_SIDE)
    cols_at = jnp.arange(total_cols)
    row_zone = (rows_at >= total_rows - WINDOW_SIDE).astype(jnp.int32) + (
        rows_at >= total_rows - half_win
    ).astype(jnp.int32)
    col_zone = (cols_at >= total_cols - WINDOW_SIDE).astype(jnp.int32) + (
        cols_at >= total_cols - half_win
    ).astype(jnp.int32)
    zone_ids = 3 * row_zone[:, None] + col_zone[None, :]
    outside = ((rows_at + half_win) % total_rows >= valid_rows)[:, None] | (
        (cols_at + half_win) % total_cols >= valid_cols
    )[None, :]
    codes = zone_ids + jnp.where(outside, ZONES, 0)
    win_count = total_cols // WINDOW_SIDE
    codes = (
        codes.reshape(WINDOW_SIDE, win_count, WINDOW_SIDE)
        .transpose(1, 0, 2)
        .reshape(win_count, WINDOW_SIDE * WINDOW_SIDE)
    )
    zones, out = codes % ZONES, codes // ZONES
    mask = jnp.where(zones[:, :, None] != zones[:, None, :], MASK_FILL, 0.0) + jnp.where(
        out[:, None, :] > 0, MASK_FILL, 0.0
    )
    peak = jnp.max(mask, -1)[:, :, None]
    lane = jnp.arange(LANES)
    same = zones[:, :, None] == lane
    query = jnp.where(
        lane < ZONES,
        jnp.where(same, -MASK_FILL, 0.0),
        jnp.where(lane == ZONES, MASK_FILL, jnp.where(lane == ZONES + 1, MASK_FILL - peak, 0.0)),
    )
    key = jnp.where(
        lane < ZONES,
        jnp.where(same, 1.0, 0.0),
        jnp.where(lane == ZONES, out[:, :, None], jnp.where(lane == ZONES + 1, 1.0, 0.0)),
    )
    return (
        query.astype(BF).reshape(-1, LANES),
        key.astype(BF).reshape(-1, LANES),
    )


def plus(left, right):
    return left.astype(FL) + right.astype(FL)


def mm(left, right):
    return jnp.dot(left, right, preferred_element_type=FL)


def mm_nt(left, right):
    return lax.dot_general(left, right, (((1,), (1,)), ((), ())), preferred_element_type=FL)


def mm_tn(left, right):
    return lax.dot_general(left, right, (((0,), (0,)), ((), ())), preferred_element_type=FL)


def skipping(body, count, extra):
    def run(*refs):
        return body(*refs[:count], *refs[count + extra :])

    return run


def call_kernel(body, name, outs, args, scratch=(), micros=5, after=()):
    specs, arrays = [], []
    for arg in args:
        array, spec = arg if isinstance(arg, tuple) else (arg, None)
        if spec is None:
            spec = pl.BlockSpec(array.shape, lambda i, rank=array.ndim: (0,) * rank)
        specs.append(spec)
        arrays.append(array)
    return pl.pallas_call(
        skipping(body, len(args), len(after)),
        name=name,
        grid=(1,),
        out_shape=[jax.ShapeDtypeStruct(s, d) for s, d in outs],
        in_specs=specs + [pl.BlockSpec(memory_space=pl.ANY)] * len(after),
        out_specs=[pl.BlockSpec(s, lambda i, rank=len(s): (0,) * rank) for s, _ in outs],
        scratch_shapes=[pltpu.VMEM(s, d) for s, d in scratch],
        compiler_params=pltpu.CompilerParams(vmem_limit_bytes=VMEM_BYTES),
        cost_estimate=cost(micros),
    )(*arrays, *after)


def rows_at(start, size):
    return pl.ds(pl.multiple_of(start, 16), size)


def head_sums(values, block_ones):
    high = values.astype(BF)
    rest = (values - high.astype(FL)).astype(BF)
    return mm(jnp.concatenate([high, rest], 1), block_ones)


def tiles_of(channels):
    return [slice(LANES * t, LANES * (t + 1)) for t in range(channels // LANES)]


def to_windows(sources, grid_ref, win_ref, band_cols, channels):
    half_win = WINDOW_SIDE // 2
    pitch = band_cols + 8
    win_area = WINDOW_SIDE * WINDOW_SIDE
    for i in range(WINDOW_SIDE):
        value = sources(i).astype(FL)
        for t, lanes in enumerate(tiles_of(channels)):
            grid_ref[t, i * pitch : i * pitch + band_cols, :] = value[:, lanes]
            grid_ref[t, i * pitch + band_cols : (i + 1) * pitch, :] = value[0:8, lanes]
    for t in range(channels // LANES):
        for n in range(band_cols // WINDOW_SIDE):
            for i in range(WINDOW_SIDE):
                at = i * pitch + n * WINDOW_SIDE + half_win
                to = n * win_area + i * WINDOW_SIDE
                win_ref[t, to : to + WINDOW_SIDE, :] = grid_ref[t, at : at + WINDOW_SIDE, :]


def from_windows(put, grid_ref, win_ref, band_cols, channels):
    half_win = WINDOW_SIDE // 2
    pitch = band_cols + 8
    win_area = WINDOW_SIDE * WINDOW_SIDE
    for t in range(channels // LANES):
        for n in range(band_cols // WINDOW_SIDE):
            for i in range(WINDOW_SIDE):
                to = i * pitch + n * WINDOW_SIDE + half_win
                at = n * win_area + i * WINDOW_SIDE
                grid_ref[t, to : to + WINDOW_SIDE, :] = win_ref[t, at : at + WINDOW_SIDE, :]
        for i in range(WINDOW_SIDE):
            grid_ref[t, i * pitch : i * pitch + half_win, :] = grid_ref[
                t, i * pitch + band_cols : i * pitch + band_cols + half_win, :
            ]
    for i in range(WINDOW_SIDE):
        put(
            i,
            jnp.concatenate(
                [
                    grid_ref[t, i * pitch : i * pitch + band_cols, :]
                    for t in range(channels // LANES)
                ],
                1,
            ),
        )


def stacked(tile, heads_ref):
    return jnp.concatenate([tile] * TILE_HEADS, 0) * heads_ref[...]


def spread_body(first_ref, second_ref, rows_ref, keys_ref):
    row = lax.broadcasted_iota(jnp.int32, (AREA, AREA), 0) % WINDOW_SIDE
    lane = lax.broadcasted_iota(jnp.int32, (AREA, AREA), 1) % WINDOW_SIDE
    *_, level = bias_network(first_ref, second_ref)
    wide = jnp.concatenate([16.0 * level, jnp.zeros((2 * SHEAR, LANES - HEAD_COUNT), FL)], 1)
    lines = wide.T

    def shear(line):
        wide = pltpu.roll(jnp.broadcast_to(line, (AREA, SHEAR)), SHEAR - (AREA - 1), 1)
        return pltpu.roll(wide, 0, 1, stride=1, stride_axis=0)[:, 0:AREA]

    for t in range(rows_ref.shape[0]):
        rows, keys = [], []
        for k in range(TILE_HEADS):
            line = lines[t * TILE_HEADS + k : t * TILE_HEADS + k + 1]
            key = jnp.where(lane >= row, shear(line[:, :SHEAR]), shear(line[:, SHEAR:]))
            keys.append(key)
            rows.append(key.T)
        rows_ref[t] = jnp.concatenate(rows, 1)
        keys_ref[t] = jnp.concatenate(keys, 1)


LINE_ROWS = 2 * HEAD_COUNT
ATTN_AT = LINE_ROWS
SETTLE_AT = ATTN_AT + 3
MERGE_AT = SETTLE_AT + 3
SUM_ROWS = 40


def fold_body(*refs, tile_count, micro_count):
    dbias_refs, attn_refs, settle_refs, merge_refs, dpre_refs, (dout_ref, out_ref) = taken(
        refs, tile_count, tile_count * micro_count, micro_count, micro_count, micro_count
    )
    row = lax.broadcasted_iota(jnp.int32, (AREA, AREA), 0)
    lane = lax.broadcasted_iota(jnp.int32, (AREA, AREA), 1)
    turn = jnp.where(row + lane == AREA - 1, 1.0, 0.0).astype(BF)
    later = lane % WINDOW_SIDE >= (AREA - 1 - row) % WINDOW_SIDE
    blank = jnp.zeros((AREA, SHEAR - AREA), FL)

    def fold(values):
        wide = jnp.concatenate([values, blank], 1)
        return jnp.sum(pltpu.roll(wide, 0, 1, stride=1, stride_axis=0), 0, keepdims=True)

    channels = out_ref.shape[1]
    out_ref[...] = jnp.zeros_like(out_ref)
    for t, ref in enumerate(dbias_refs):
        values = ref[...]
        for k in range(TILE_HEADS):
            value = values[:, k * AREA : (k + 1) * AREA]
            total = None
            for _ in range(3):
                part = value.astype(BF)
                value = value - part.astype(FL)
                now = mm(turn, part)
                total = now if total is None else total + now
            head = t * TILE_HEADS + k
            out_ref[head : head + 1, :] = fold(jnp.where(later, total, 0.0))
            at = HEAD_COUNT + head
            out_ref[at : at + 1, :] = fold(jnp.where(later, 0.0, total))
        lanes = slice(t * LANES, (t + 1) * LANES)
        out_ref[ATTN_AT : ATTN_AT + 3, lanes] = sum(
            attn_refs[m * tile_count + t][0:3, :] for m in range(micro_count)
        )
    out_ref[SETTLE_AT : SETTLE_AT + 3, :] = sum(ref[0:3, :] for ref in settle_refs)
    merge = sum(ref[0:4, :] for ref in merge_refs)
    for k, (at, half) in enumerate(((0, 0), (0, 1), (1, 0), (1, 1), (2, 0), (3, 0))):
        out_ref[MERGE_AT + k : MERGE_AT + k + 1, :] = merge[
            at : at + 1, half * channels : (half + 1) * channels
        ]
    experts, _, hidden = dpre_refs[0].shape
    chunks = hidden // channels
    for e in range(experts):
        total = sum(ref[e] for ref in dpre_refs)
        for c in range(chunks):
            at = SUM_ROWS + e * chunks + c
            out_ref[at : at + 1, :] = total[:, c * channels : (c + 1) * channels]
        at = SUM_ROWS + experts * chunks + e
        out_ref[at : at + 1, :] = dout_ref[e]


def bias_network_back_body(sums_ref, first_ref, second_ref, dfirst_ref, dsecond_ref):
    down, across, valid, hidden, slope, level = bias_network(first_ref, second_ref)
    lines = jnp.concatenate(
        [sums_ref[0:HEAD_COUNT, :], sums_ref[HEAD_COUNT : 2 * HEAD_COUNT, :]], 1
    )
    lines = jnp.concatenate([lines, jnp.zeros((LANES - HEAD_COUNT, 2 * SHEAR), FL)], 0)
    grad = lines.T[:, 0:HEAD_COUNT]
    grad = jnp.where(valid, grad * 16.0 * level * (1.0 - level), 0.0)
    dsecond_ref[...] = lax.dot_general(
        hidden,
        grad,
        (((0,), (0,)), ((), ())),
        precision=PRECISION_HIGH,
        preferred_element_type=FL,
    )
    dpre = slope * lax.dot_general(
        grad,
        second_ref[...],
        (((1,), (1,)), ((), ())),
        precision=PRECISION_HIGH,
        preferred_element_type=FL,
    )
    dfirst_ref[0:1, :] = jnp.sum(down * dpre, 0, keepdims=True)
    dfirst_ref[1:2, :] = jnp.sum(across * dpre, 0, keepdims=True)
    dfirst_ref[2:3, :] = jnp.sum(dpre, 0, keepdims=True)


def slot_body(
    place_ref,
    experts_ref,
    column_ref,
    dest_column_ref,
    dest_row_ref,
    *,
    experts,
    local,
    slots,
    capacity,
):
    tokens = experts_ref.shape[1]

    def place(expert):
        upper = jnp.where(expert >= experts // 2, 1, 0)
        inner = expert - upper * (experts // 2)
        apart = upper ^ place_ref[0]
        member = (inner // local) ^ place_ref[1]
        return ((2 * member + apart) * local + inner % local) * slots

    block = LANES
    lower = (
        lax.broadcasted_iota(jnp.int32, (block, block), 0)
        > lax.broadcasted_iota(jnp.int32, (block, block), 1)
    ).astype(FL).astype(BF)
    upper = (
        lax.broadcasted_iota(jnp.int32, (block, block), 0)
        < lax.broadcasted_iota(jnp.int32, (block, block), 1)
    ).astype(FL).astype(BF)
    lane = lax.broadcasted_iota(jnp.int32, (block, LANES), 1)
    sublane = lax.broadcasted_iota(jnp.int32, (LANES, block), 0)
    seen_row = jnp.zeros((1, LANES), FL)
    seen_column = jnp.zeros((LANES, 1), FL)
    for c in range(tokens // block):
        line = experts_ref[:, c * block : (c + 1) * block]
        across = jnp.where(sublane == line, 1.0, 0.0)
        column = jnp.broadcast_to(line.astype(FL), (block, block)).T[:, 0:1].astype(jnp.int32)
        down = jnp.where(lane == column, 1.0, 0.0)
        before = mm(lower, down.astype(BF)) + seen_row
        slot = jnp.sum(down * before, 1, keepdims=True).astype(jnp.int32)
        column_ref[c * block : (c + 1) * block, :] = column
        dest_column_ref[c * block : (c + 1) * block, :] = jnp.where(
            slot < capacity, place(column) + slot, -1
        )
        before = mm(across.astype(BF), upper) + seen_column
        slot = jnp.sum(across * before, 0, keepdims=True).astype(jnp.int32)
        dest_row_ref[:, c * block : (c + 1) * block] = jnp.where(
            slot < capacity, place(line) + slot, -1
        )
        seen_row = seen_row + jnp.sum(down, 0, keepdims=True)
        seen_column = seen_column + jnp.sum(across, 1, keepdims=True)


def slot_tables(chosen, my_place, experts, local, slots, capacity, after):
    tokens = chosen.shape[1]
    vmem = pl.BlockSpec(memory_space=pltpu.VMEM)
    column = jax.ShapeDtypeStruct((tokens, 1), jnp.int32)
    return pl.pallas_call(
        skipping(
            functools.partial(
                slot_body, experts=experts, local=local, slots=slots, capacity=capacity
            ),
            2,
            1,
        ),
        name="slot_tables",
        in_specs=[
            pl.BlockSpec(memory_space=pltpu.SMEM),
            vmem,
            pl.BlockSpec(memory_space=pl.ANY),
        ],
        out_specs=[vmem] * 3,
        out_shape=[column, column, jax.ShapeDtypeStruct((1, tokens), jnp.int32)],
        cost_estimate=cost(3),
    )(my_place, chosen, after)


def attend_forward_body(
    band_ref,
    below_ref,
    weight_ref,
    qbias_ref,
    vbias_ref,
    scale_ref,
    bias_ref,
    query_zone_ref,
    key_zone_ref,
    heads_ref,
    block_ref,
    own_ref,
    send_ref,
    win_ref,
    qkv_ref,
    inv_ref,
    grid_scr,
    win_scr,
    *,
    band_cols,
    channels,
):
    tokens = band_ref.shape[0]
    half = tokens // 2
    win_area = WINDOW_SIDE * WINDOW_SIDE
    tiles = tiles_of(channels)

    def source(i):
        if i < WINDOW_SIDE // 2:
            return band_ref[half + i * band_cols : half + (i + 1) * band_cols, :]
        at = (i - WINDOW_SIDE // 2) * band_cols
        return below_ref[at : at + band_cols, :]

    to_windows(source, grid_scr, win_scr, band_cols, channels)
    block_ones = block_ref[...]
    chunk = 2 * win_area

    def project(c, carry):
        rows = rows_at(c * chunk, chunk)
        low = jnp.concatenate([win_scr[t, rows, :] for t in range(len(tiles))], 1).astype(BF)
        win_ref[rows, :] = low
        qkv = mm(low, weight_ref[...])
        for lanes in tiles:
            key_lanes = slice(channels + lanes.start, channels + lanes.stop)
            value_lanes = slice(2 * channels + lanes.start, 2 * channels + lanes.stop)
            query = qkv[:, lanes] + qbias_ref[:, lanes]
            inverse = (
                lax.rsqrt(head_sums(query * query, block_ones) + EPS_UNIT) * scale_ref[:, lanes]
            )
            inv_ref[rows, lanes] = inverse
            qkv_ref[rows, lanes] = (query * inverse).astype(BF)
            key = qkv[:, key_lanes]
            inverse = lax.rsqrt(head_sums(key * key, block_ones) + EPS_UNIT)
            inv_ref[rows, key_lanes] = inverse
            qkv_ref[rows, key_lanes] = (key * inverse).astype(BF)
            qkv_ref[rows, value_lanes] = (qkv[:, value_lanes] + vbias_ref[:, lanes]).astype(BF)
        return carry

    lax.fori_loop(0, tokens // chunk, project, 0)

    def attend(n, carry):
        rows = rows_at(n * win_area, win_area)
        query_zone = query_zone_ref[rows, :]
        key_zone = jnp.concatenate([key_zone_ref[rows, :]] * TILE_HEADS, 0)
        for t, lanes in enumerate(tiles):
            query = qkv_ref[rows, lanes]
            key = qkv_ref[rows, channels + lanes.start : channels + lanes.stop]
            value = qkv_ref[rows, 2 * channels + lanes.start : 2 * channels + lanes.stop]
            scores = mm_nt(
                jnp.concatenate([query, query_zone], 1),
                jnp.concatenate([stacked(key, heads_ref), key_zone], 1),
            )
            powers = jnp.exp(scores + bias_ref[t]).astype(BF)
            mixed = mm(powers, jnp.concatenate([stacked(value, heads_ref), heads_ref[...]], 1))
            win_scr[t, rows, :] = mixed[:, :LANES] / mixed[:, LANES:]
        return carry

    lax.fori_loop(0, tokens // win_area, attend, 0, unroll=UNROLL)

    def put(i, value):
        if i < WINDOW_SIDE // 2:
            own_ref[i * band_cols : (i + 1) * band_cols, :] = value.astype(BF)
        else:
            at = (i - WINDOW_SIDE // 2) * band_cols
            send_ref[at : at + band_cols, :] = value.astype(BF)

    from_windows(put, grid_scr, win_scr, band_cols, channels)


def window_body(own_ref, lifted_ref, out_ref, grid_scr, win_scr, *, band_cols, channels):
    def source(i):
        ref = own_ref if i < WINDOW_SIDE // 2 else lifted_ref
        at = (i % (WINDOW_SIDE // 2)) * band_cols
        return ref[at : at + band_cols, :]

    to_windows(source, grid_scr, win_scr, band_cols, channels)
    for t, lanes in enumerate(tiles_of(channels)):
        out_ref[:, lanes] = win_scr[t].astype(BF)


def attend_backward_body(*refs, summed_before):
    (
        back_ref,
        query_ref,
        key_ref,
        value_ref,
        query_inv_ref,
        key_inv_ref,
        scale_ref,
        win_ref,
        bias_ref,
        query_zone_ref,
        key_zone_ref,
        heads_ref,
        block_ref,
        *rest,
    ) = refs
    if summed_before:
        dweight_before_ref, dbias_before_ref, *rest = rest
    dqkv_ref, dweight_ref, dbias_ref, small_ref = rest
    tokens = back_ref.shape[0]
    win_area = WINDOW_SIDE * WINDOW_SIDE
    block_ones = block_ref[...]
    if summed_before:
        dbias_ref[...] = dbias_before_ref[...]
    else:
        dbias_ref[...] = jnp.zeros_like(dbias_ref)
    small_ref[...] = jnp.zeros_like(small_ref)

    def attend(n, carry):
        rows = rows_at(n * win_area, win_area)
        query = query_ref[rows, :]
        key = key_ref[rows, :]
        queries = stacked(query, heads_ref)
        backs = stacked(back_ref[rows, :], heads_ref)
        query_zone = jnp.concatenate([query_zone_ref[rows, :]] * TILE_HEADS, 0)
        scores = mm_nt(
            jnp.concatenate([key, key_zone_ref[rows, :]], 1),
            jnp.concatenate([queries, query_zone], 1),
        )
        powers = jnp.exp(scores + bias_ref[0])
        probs = powers * (1.0 / jnp.sum(powers, 0, keepdims=True))
        weighted = probs * mm_nt(value_ref[rows, :], backs)
        dscores = weighted - probs * jnp.sum(weighted, 0, keepdims=True)
        dbias_ref[...] += dscores
        dlow = dscores.astype(BF)
        dvalue = mm(probs.astype(BF), backs)
        dkey = mm(dlow, queries)
        dquery = mm_tn(dlow, key) * heads_ref[...].astype(FL)
        dquery = sum(dquery[k * win_area : (k + 1) * win_area] for k in range(TILE_HEADS))
        scale = scale_ref[...]
        unit = query.astype(FL)
        along = head_sums(unit * dquery, block_ones)
        dquery = query_inv_ref[rows, :] * (dquery - unit * along / (scale * scale))
        unit = key.astype(FL)
        dkey = key_inv_ref[rows, :] * (dkey - unit * head_sums(unit * dkey, block_ones))
        for part, grad in enumerate((dquery, dkey, dvalue)):
            dqkv_ref[rows, part * LANES : (part + 1) * LANES] = grad.astype(BF)
        small_ref[0:1, :] += jnp.sum(dquery, 0, keepdims=True)
        small_ref[1:2, :] += jnp.sum(dvalue, 0, keepdims=True)
        small_ref[2:3, :] += jnp.sum(along, 0, keepdims=True)
        return carry

    lax.fori_loop(0, tokens // win_area, attend, 0, unroll=UNROLL)
    dweight = mm_tn(win_ref[...], dqkv_ref[...])
    if summed_before:
        dweight = dweight + dweight_before_ref[...]
    dweight_ref[...] = dweight.astype(dweight_ref.dtype)


def input_grad_body(
    first_ref,
    second_ref,
    third_ref,
    weight_ref,
    own_ref,
    send_ref,
    grid_scr,
    win_scr,
    *,
    band_cols,
    channels,
):
    tokens = first_ref.shape[0]
    tiles = tiles_of(channels)
    chunk = 2 * WINDOW_SIDE * WINDOW_SIDE

    def project(c, carry):
        rows = rows_at(c * chunk, chunk)
        parts = [ref[rows, :] for ref in (first_ref, second_ref, third_ref)]
        wide = jnp.concatenate([p[:, lanes] for lanes in tiles for p in parts], 1)
        back = mm_nt(wide, weight_ref[...])
        for t, lanes in enumerate(tiles):
            win_scr[t, rows, :] = back[:, lanes]
        return carry

    lax.fori_loop(0, tokens // chunk, project, 0)

    def put(i, value):
        if i < WINDOW_SIDE // 2:
            own_ref[i * band_cols : (i + 1) * band_cols, :] = value
        else:
            at = (i - WINDOW_SIDE // 2) * band_cols
            send_ref[at : at + band_cols, :] = value.astype(BF)

    from_windows(put, grid_scr, win_scr, band_cols, channels)


def lane_mean(values):
    return jnp.sum(values, -1, keepdims=True) * (1.0 / values.shape[-1])


def normalised(values):
    centred = values - lane_mean(values)
    inverse = lax.rsqrt(lane_mean(centred * centred) + EPS_NORM)
    return centred * inverse, inverse


def normalised_back(back, gain, unit, inverse):
    back = back * gain
    return inverse * (back - lane_mean(back) - unit * lane_mean(back * unit))


CHUNK = 576
WIDE_CHUNK = 1152


def pack_rows(dest_row_ref, rows_ref, out_refs):
    tokens = rows_ref.shape[0]
    start = 0
    for ref in out_refs:
        place = lax.broadcasted_iota(jnp.int32, (ref.shape[0], tokens), 0) + start
        chosen = jnp.where(place == dest_row_ref[...], 1.0, 0.0).astype(BF)
        ref[...] = mm(chosen, rows_ref[...]).astype(BF)
        start += ref.shape[0]


def unpack_rows(dest_col, buffer):
    place = lax.broadcasted_iota(jnp.int32, (dest_col.shape[0], buffer.shape[0]), 1)
    chosen = jnp.where(place == dest_col, 1.0, 0.0).astype(BF)
    return mm(chosen, buffer)


def route_body(
    arrived_ref,
    own_ref,
    band_ref,
    weight_ref,
    small_ref,
    router_ref,
    expert_ref,
    dest_row_ref,
    resid_ref,
    unit_ref,
    aux_ref,
    low_ref,
    *sent_refs,
    experts,
):
    half = arrived_ref.shape[0]
    lane = lax.broadcasted_iota(jnp.int32, (CHUNK, LANES), 1)
    for part, ref in enumerate((arrived_ref, own_ref)):

        def step(c, carry, part=part, ref=ref):
            rows = rows_at(part * half + c * CHUNK, CHUNK)
            projected = mm(ref[rows_at(c * CHUNK, CHUNK), :], weight_ref[...]) + small_ref[0:1, :]
            unit, inverse = normalised(projected)
            unit_ref[rows, :] = unit.astype(BF)
            resid = band_ref[rows, :].astype(FL) + unit * small_ref[1:2, :] + small_ref[2:3, :]
            resid_ref[rows, :] = resid
            low = resid.astype(BF)
            low_ref[rows, :] = low
            logits = jnp.where(lane < experts, mm(low, router_ref[...]), -1e30)
            powers = jnp.exp(logits - jnp.max(logits, -1, keepdims=True))
            probs = powers / jnp.sum(powers, -1, keepdims=True)
            gate = jnp.sum(
                jnp.where(lane == expert_ref[rows, :], probs, 0.0), -1, keepdims=True
            )
            aux_ref[rows, :] = jnp.where(
                lane == LANES - 1, gate, jnp.where(lane == LANES - 2, inverse, probs)
            )
            return carry

        lax.fori_loop(0, half // CHUNK, step, 0)
    pack_rows(dest_row_ref, low_ref, sent_refs)


def merge_body(*refs, experts, band_cols, members):
    returned_refs, refs = refs[:members], refs[members:]
    (
        dest_col_ref,
        dest_row_ref,
        expert_ref,
        aux_ref,
        resid_ref,
        small_ref,
        weight_ref,
        wide_ref,
        cotangent_ref,
        final_ref,
        merged_ref,
        dreduced_ref,
        dresid_ref,
        dlogits_ref,
        sums_ref,
    ) = refs[:15]
    sent_refs = refs[15 : 15 + members]
    unit_scr, picked_scr, inverse_scr, token_scr, back_scr = refs[15 + members :]
    returned = jnp.concatenate([ref[...] for ref in returned_refs], 0)
    tokens, channels = resid_ref.shape
    tiles = tiles_of(channels)
    lane = lax.broadcasted_iota(jnp.int32, (WIDE_CHUNK, LANES), 1)

    def combine(c, carry):
        rows = rows_at(c * WIDE_CHUNK, WIDE_CHUNK)
        picked = unpack_rows(dest_col_ref[rows, :], returned)
        picked_scr[rows, :] = picked
        gate = aux_ref[rows, :][:, LANES - 1 : LANES]
        unit, inverse = normalised(gate * picked)
        unit_scr[rows, :] = unit
        inverse_scr[rows, :] = jnp.broadcast_to(inverse, (WIDE_CHUNK, LANES))
        resid = resid_ref[rows, :] + unit * small_ref[0:1, :] + small_ref[1:2, :]
        for t, lanes in enumerate(tiles):
            token_scr[t, rows, :] = resid[:, lanes]
        return carry

    lax.fori_loop(0, tokens // WIDE_CHUNK, combine, 0)
    pairs = band_cols // 2
    for i in range(WINDOW_SIDE // 2):
        for k in range(4):
            start = (2 * i + k % 2) * band_cols + k // 2
            for t in range(len(tiles)):
                at = k * channels + t * LANES
                merged_ref[i * pairs : (i + 1) * pairs, at : at + LANES] = token_scr[
                    t, pl.ds(start, pairs, stride=2), :
                ].astype(BF)
    unit, inverse = normalised(mm(merged_ref[...], weight_ref[...]))
    final_ref[...] = (unit * wide_ref[0:1, :] + wide_ref[1:2, :]).astype(BF)
    back = cotangent_ref[...].astype(FL)
    sums_ref[...] = jnp.zeros_like(sums_ref)
    sums_ref[0:1, :] = jnp.sum(back * unit, 0, keepdims=True)
    sums_ref[1:2, :] = jnp.sum(back, 0, keepdims=True)
    dreduced = normalised_back(back, wide_ref[0:1, :], unit, inverse).astype(BF)
    dreduced_ref[...] = dreduced
    for k in range(4):
        part = mm_nt(dreduced, weight_ref[k * channels : (k + 1) * channels, :])
        for i in range(WINDOW_SIDE // 2):
            start = (2 * i + k % 2) * band_cols + k // 2
            for t, lanes in enumerate(tiles):
                token_scr[t, pl.ds(start, pairs, stride=2), :] = part[
                    i * pairs : (i + 1) * pairs, lanes
                ]

    def spread(c, carry):
        rows = rows_at(c * WIDE_CHUNK, WIDE_CHUNK)
        back = jnp.concatenate([token_scr[t, rows, :] for t in range(len(tiles))], 1)
        dresid_ref[rows, :] = back
        unit = unit_scr[rows, :]
        sums_ref[2:3, 0:channels] += jnp.sum(back * unit, 0, keepdims=True)
        sums_ref[3:4, 0:channels] += jnp.sum(back, 0, keepdims=True)
        back = normalised_back(back, small_ref[0:1, :], unit, inverse_scr[rows, :][:, 0:1])
        aux = aux_ref[rows, :]
        gate = aux[:, LANES - 1 : LANES]
        dgate = jnp.sum(back * picked_scr[rows, :], -1, keepdims=True)
        back_scr[rows, :] = (back * gate).astype(BF)
        probs = jnp.where(lane < experts, aux, 0.0)
        chosen = jnp.where(lane == expert_ref[rows, :], 1.0, 0.0)
        dlogits_ref[rows, :] = (probs * (chosen - gate) * dgate).astype(BF)
        return carry

    lax.fori_loop(0, tokens // WIDE_CHUNK, spread, 0)
    pack_rows(dest_row_ref, back_scr, sent_refs)


def settle_body(*refs, members):
    sent_refs, refs = refs[:members], refs[members:]
    (
        dest_col_ref,
        dresid_ref,
        dlogits_ref,
        router_ref,
        unit_ref,
        aux_ref,
        small_ref,
        weight_ref,
        done_ref,
        low_ref,
        rows_ref,
        sums_ref,
    ) = refs
    sent = jnp.concatenate([ref[...] for ref in sent_refs], 0)
    tokens, channels = dresid_ref.shape
    sums_ref[...] = jnp.zeros_like(sums_ref)

    def step(c, carry):
        rows = rows_at(c * WIDE_CHUNK, WIDE_CHUNK)
        back = dresid_ref[rows, :] + unpack_rows(dest_col_ref[rows, :], sent)
        back = back + mm_nt(dlogits_ref[rows, :], router_ref[...])
        done_ref[rows, :] = back
        unit = unit_ref[rows, :].astype(FL)
        sums_ref[1:2, :] += jnp.sum(back * unit, 0, keepdims=True)
        sums_ref[2:3, :] += jnp.sum(back, 0, keepdims=True)
        inverse = aux_ref[rows, :][:, LANES - 2 : LANES - 1]
        back = normalised_back(back, small_ref[1:2, :], unit, inverse)
        sums_ref[0:1, :] += jnp.sum(back, 0, keepdims=True)
        low = back.astype(BF)
        low_ref[rows, :] = low
        rows_ref[rows, :] = mm_nt(low, weight_ref[...]).astype(BF)
        return carry

    lax.fori_loop(0, tokens // WIDE_CHUNK, step, 0)


def dense_body(*refs):
    (*ins, proj_ref, router_ref) = refs
    arrived, own, low, resid, dlogits = (ins[i::5] for i in range(5))
    half = arrived[0].shape[0]
    proj = router = None
    for a, o, b, r, d in zip(arrived, own, low, resid, dlogits):
        now = mm_tn(a[...], b[0:half, :]) + mm_tn(o[...], b[half:, :])
        then = mm_tn(r[...], d[...])
        proj = now if proj is None else proj + now
        router = then if router is None else router + then
    proj_ref[...] = proj.astype(BF)
    router_ref[...] = router.astype(BF)


def merge_weight_body(*refs):
    (*ins, out_ref) = refs
    total = None
    for left, right in zip(ins[0::2], ins[1::2]):
        now = mm_tn(left[...], right[...])
        total = now if total is None else total + now
    out_ref[...] = total.astype(BF)


def merge_weight_grad(merged, dreduced, channels, after):
    args, specs = [], []
    for left, right in zip(merged, dreduced):
        args += [left, right]
        specs += [
            pl.BlockSpec((left.shape[0], channels), lambda k: (0, k)),
            pl.BlockSpec(right.shape, lambda k: (0, 0)),
        ]
    return pl.pallas_call(
        skipping(merge_weight_body, len(args), len(after)),
        name="merge_weight_grad",
        grid=(4,),
        out_shape=jax.ShapeDtypeStruct((merged[0].shape[1], dreduced[0].shape[1]), BF),
        in_specs=specs + [pl.BlockSpec(memory_space=pl.ANY)] * len(after),
        out_specs=pl.BlockSpec((channels, dreduced[0].shape[1]), lambda k: (k, 0)),
        compiler_params=pltpu.CompilerParams(vmem_limit_bytes=VMEM_BYTES),
        cost_estimate=cost(5),
    )(*args, *after)


PIECE = 384


def spot_of(member, me, bits):
    apart = member ^ me
    spot = 0
    for k in range(bits):
        spot = spot | (((apart >> k) & 1) << (bits - 1 - k))
    return spot


def piece_home(expert, chunk, row_size, chunks):
    piece = expert * chunks + chunk
    return piece % row_size, piece // row_size


def take_weights(own_ref, other_refs, out_scr, expert, local, me, first):
    row_size = len(other_refs)
    chunks = out_scr.shape[1 if first else 0] // PIECE

    @pl.when(expert < local)
    def _():
        out_scr[...] = own_ref[0]

    for chunk in range(chunks):
        member, _ = piece_home(jnp.maximum(expert - local, 0), chunk, row_size, chunks)
        spot = spot_of(member, me, row_size.bit_length() - 1)
        span = slice(chunk * PIECE, (chunk + 1) * PIECE)
        for k, ref in enumerate(other_refs):

            @pl.when((expert >= local) & (spot == k))
            def _(ref=ref, span=span):
                if first:
                    out_scr[:, span] = ref[0]
                else:
                    out_scr[span, :] = ref[0]


def taken(refs, *counts):
    lists = []
    for count in counts:
        lists.append(refs[:count])
        refs = refs[count:]
    return lists + [refs]


def joined(refs):
    return jnp.concatenate([ref[...] for ref in refs], 0)


def put_parts(refs, value):
    start = 0
    for ref in refs:
        ref[...] = value[start : start + ref.shape[0]].astype(BF)
        start += ref.shape[0]


def expert_forward_body(me_ref, *refs, local, members, row_size):
    row_refs, (in_ref, in_bias_ref, out_ref, out_bias_ref), in_others, out_others, refs = taken(
        refs, members, 4, row_size, row_size
    )
    result_refs, (hidden_ref, slope_ref, pre_scr, in_scr, out_scr) = taken(refs, members)
    expert = pl.program_id(0)
    take_weights(in_ref, in_others, in_scr, expert, local, me_ref[0], True)
    take_weights(out_ref, out_others, out_scr, expert, local, me_ref[0], False)
    pre_scr[...] = mm(joined(row_refs), in_scr[...]) + in_bias_ref[0]
    for chunk in range(in_scr.shape[1] // PIECE):
        lanes = slice(chunk * PIECE, (chunk + 1) * PIECE)
        pre = pre_scr[:, lanes]
        cdf = 0.5 * (1.0 + lax.erf(pre * 0.7071067811865476))
        hidden_ref[0, :, lanes] = (pre * cdf).astype(BF)
        slope_ref[0, :, lanes] = (
            cdf + pre * (0.3989422804014327 * jnp.exp(-0.5 * pre * pre))
        ).astype(BF)
    put_parts(result_refs, mm(hidden_ref[0], out_scr[...]) + out_bias_ref[0])


def expert_specs(members, slots, channels, hidden, local, row_size):
    chunks = hidden // PIECE

    def other_at(k, me):
        return (jnp.maximum(k - local, 0) * chunks // row_size, 0, 0)

    def own_at(k, me):
        return (jnp.minimum(k, local - 1), 0, 0)

    return dict(
        tokens=pl.BlockSpec((slots, channels), lambda k, me: (k, 0)),
        wide=pl.BlockSpec((1, members * slots, hidden), lambda k, me: (k, 0, 0)),
        first=pl.BlockSpec((1, channels, hidden), own_at),
        second=pl.BlockSpec((1, hidden, channels), own_at),
        other=pl.BlockSpec((1, PIECE, PIECE), other_at),
        bias=pl.BlockSpec((1, 1, hidden), lambda k, me: (k, 0, 0)),
        low_bias=pl.BlockSpec((1, 1, channels), lambda k, me: (k, 0, 0)),
    )


def call_expert(
    body, name, me, steps, in_specs, out_specs, outs, scratch, args, micros, after=()
):
    return pl.pallas_call(
        skipping(body, 1 + len(args), len(after)),
        name=name,
        grid_spec=pltpu.PrefetchScalarGridSpec(
            num_scalar_prefetch=1,
            grid=(steps,),
            in_specs=in_specs + [pl.BlockSpec(memory_space=pl.ANY)] * len(after),
            out_specs=out_specs,
            scratch_shapes=scratch,
        ),
        out_shape=outs,
        compiler_params=pltpu.CompilerParams(vmem_limit_bytes=VMEM_BYTES),
        cost_estimate=cost(micros),
    )(me, *args, *after)


def expert_forward(
    me, rows, first, second, first_other, second_other, first_bias, second_bias, after
):
    members, row_size = len(rows), len(first_other)
    local, channels, hidden = first.shape
    slots = rows[0].shape[0] // (2 * local)
    count = members * slots
    spec = expert_specs(members, slots, channels, hidden, local, row_size)
    wide = jax.ShapeDtypeStruct((2 * local, count, hidden), BF)
    outs = call_expert(
        functools.partial(
            expert_forward_body, local=local, members=members, row_size=row_size
        ),
        "expert_forward",
        me,
        2 * local,
        [spec["tokens"]] * members
        + [spec["first"], spec["bias"], spec["second"], spec["low_bias"]]
        + [spec["other"]] * (2 * row_size),
        [spec["tokens"]] * members + [spec["wide"], spec["wide"]],
        [jax.ShapeDtypeStruct(rows[0].shape, BF)] * members + [wide, wide],
        [
            pltpu.VMEM((count, hidden), FL),
            pltpu.VMEM((channels, hidden), BF),
            pltpu.VMEM((hidden, channels), BF),
        ],
        [*rows, first, first_bias, second, second_bias, *first_other, *second_other],
        19,
        after,
    )
    return outs[:members], outs[members], outs[members + 1]


def expert_backward_body(me_ref, *refs, local, members, row_size):
    row_refs, (in_ref, out_ref, slope_ref), in_others, out_others, refs = taken(
        refs, members, 3, row_size, row_size
    )
    result_refs, (dpre_ref, dbias_ref, dhidden_scr, in_scr, out_scr) = taken(refs, members)
    expert = pl.program_id(0)
    take_weights(in_ref, in_others, in_scr, expert, local, me_ref[0], True)
    take_weights(out_ref, out_others, out_scr, expert, local, me_ref[0], False)
    dhidden_scr[...] = mm_nt(joined(row_refs), out_scr[...])
    for chunk in range(in_scr.shape[1] // PIECE):
        lanes = slice(chunk * PIECE, (chunk + 1) * PIECE)
        dpre = dhidden_scr[:, lanes] * slope_ref[0, :, lanes].astype(FL)
        dbias_ref[0, :, lanes] = jnp.sum(dpre, 0, keepdims=True)
        dpre_ref[0, :, lanes] = dpre.astype(BF)
    put_parts(result_refs, mm_nt(dpre_ref[0], in_scr[...]))


def expert_backward(me, rows, first, second, first_other, second_other, slope, after):
    members, row_size = len(rows), len(first_other)
    local, channels, hidden = first.shape
    slots = rows[0].shape[0] // (2 * local)
    count = members * slots
    spec = expert_specs(members, slots, channels, hidden, local, row_size)
    outs = call_expert(
        functools.partial(
            expert_backward_body, local=local, members=members, row_size=row_size
        ),
        "expert_backward",
        me,
        2 * local,
        [spec["tokens"]] * members
        + [spec["first"], spec["second"], spec["wide"]]
        + [spec["other"]] * (2 * row_size),
        [spec["tokens"]] * members + [spec["wide"], spec["bias"]],
        [jax.ShapeDtypeStruct(rows[0].shape, BF)] * members
        + [
            jax.ShapeDtypeStruct((2 * local, count, hidden), BF),
            jax.ShapeDtypeStruct((2 * local, 1, hidden), FL),
        ],
        [
            pltpu.VMEM((count, hidden), FL),
            pltpu.VMEM((channels, hidden), BF),
            pltpu.VMEM((hidden, channels), BF),
        ],
        [*rows, first, second, slope, *first_other, *second_other],
        12,
        after,
    )
    return outs[:members], outs[members], outs[members + 1]


def expert_weight_body(me_ref, *refs, local, members, micros, tokens_left):
    token_refs, wide_refs, (keep_ref, send_ref, dbias_ref) = taken(
        refs, members * micros, micros
    )
    expert = pl.program_id(0)
    half = keep_ref.shape[1]
    row_size = 2 * half
    chunks = wide_refs[0].shape[2] // PIECE
    rows = [joined(token_refs[m * members : (m + 1) * members]) for m in range(micros)]
    dbias_ref[0] = sum(jnp.sum(part.astype(FL), 0, keepdims=True) for part in rows)
    total = None
    for part, ref in zip(rows, wide_refs):
        now = mm_tn(part, ref[0]) if tokens_left else mm_tn(ref[0], part)
        total = now if total is None else total + now
    low = total.astype(BF)
    for chunk in range(chunks):
        span = slice(chunk * PIECE, (chunk + 1) * PIECE)
        piece = low[:, span] if tokens_left else low[span, :]
        member, _ = piece_home(expert % local, chunk, row_size, chunks)
        spot = spot_of(member, me_ref[0], row_size.bit_length() - 1)

        @pl.when(spot < half)
        def _(piece=piece, spot=spot):
            keep_ref[0, spot, 0] = piece

        @pl.when(spot >= half)
        def _(piece=piece, spot=spot):
            send_ref[0, spot - half, 0] = piece


def expert_weight_grads(me, tokens, wide, local, row_size, tokens_left, after):
    members, micros = len(tokens[0]), len(tokens)
    together, channels = tokens[0][0].shape
    slots = together // (2 * local)
    width = wide[0].shape[-1]
    chunks = width // PIECE
    subs = local * chunks // row_size
    spec = expert_specs(members, slots, channels, width, local, row_size)
    half_shape = (2, row_size // 2, subs, PIECE, PIECE)
    half_spec = pl.BlockSpec(
        (1, row_size // 2, 1, PIECE, PIECE),
        lambda k, me: (k // local, 0, (k % local) * chunks // row_size, 0, 0),
    )
    half_out = jax.ShapeDtypeStruct(half_shape, BF)
    return call_expert(
        functools.partial(
            expert_weight_body,
            local=local,
            members=members,
            micros=micros,
            tokens_left=tokens_left,
        ),
        "expert_weight_grads",
        me,
        2 * local,
        [spec["tokens"]] * (members * micros) + [spec["wide"]] * micros,
        [half_spec] * 2 + [spec["low_bias"]],
        [half_out] * 2 + [jax.ShapeDtypeStruct((2 * local, 1, channels), FL)],
        [],
        [part for parts in tokens for part in parts] + list(wide),
        13,
        after,
    )


def add_pieces_body(keep_ref, got_ref, *out_refs):
    half = keep_ref.shape[1] // 2
    for group in range(2):
        if half:
            for k in range(half):
                out_refs[0][group, k] = plus(keep_ref[group, k], got_ref[group, k]).astype(BF)
                at = half + k
                out_refs[1][group, k] = plus(keep_ref[group, at], got_ref[group, at]).astype(BF)
        else:
            total = plus(keep_ref[group, 0], got_ref[group, 0])
            out_refs[group][...] = total.astype(out_refs[group].dtype)


def add_pieces(keep, got, after):
    groups, count = keep.shape[:2]
    if count > 1:
        shape = (groups, count // 2) + keep.shape[2:]
        outs = [(shape, BF), (shape, BF)]
    else:
        outs = [(keep.shape[2:], FL), (keep.shape[2:], BF)]
    return call_kernel(add_pieces_body, "add_pieces", outs, [keep, got], micros=3, after=after)


def add_halves_body(own_ref, got_ref, out_ref):
    out_ref[...] = plus(own_ref[...], got_ref[...]).astype(out_ref.dtype)


def add_halves(own, got, after, dtype=BF, micros=2):
    (total,) = call_kernel(
        add_halves_body, "add_halves", [(own.shape, dtype)], [own, got], micros=micros, after=after
    )
    return total


def add_blocks_body(*refs):
    (*block_refs, mine_ref, other_ref) = refs
    for half, ref in enumerate((mine_ref, other_ref)):
        ref[...] = sum(block[half].astype(FL) for block in block_refs).astype(ref.dtype)


def add_blocks(blocks, after):
    shape = blocks[0].shape[1:]
    return call_kernel(
        add_blocks_body,
        "add_blocks",
        [(shape, FL), (shape, BF)],
        blocks,
        micros=0.2,
        after=after,
    )


def place_body(me_ref, *refs, chunks, first):
    (*piece_refs, full_ref) = refs
    row_size = len(piece_refs)
    for c in range(chunks):
        member, _ = piece_home(pl.program_id(0), c, row_size, chunks)
        spot = spot_of(member, me_ref[0], row_size.bit_length() - 1)
        span = slice(c * PIECE, (c + 1) * PIECE)
        value = piece_refs[0][0]
        for k in range(1, row_size):
            value = jnp.where(spot == k, piece_refs[k][0], value)
        if first:
            full_ref[0, :, span] = value.astype(FL)
        else:
            full_ref[0, span, :] = value.astype(FL)


def place_pieces(me, pieces, local, hidden, first, after):
    row_size = len(pieces)
    chunks = hidden // PIECE
    shape = (local, PIECE, hidden) if first else (local, hidden, PIECE)
    return call_expert(
        functools.partial(place_body, chunks=chunks, first=first),
        "place_pieces",
        me,
        local,
        [pl.BlockSpec((1, PIECE, PIECE), lambda e, me: (e * chunks // row_size, 0, 0))]
        * row_size,
        [pl.BlockSpec((1,) + shape[1:], lambda e, me: (e, 0, 0))],
        [jax.ShapeDtypeStruct(shape, FL)],
        [],
        list(pieces),
        4,
        after,
    )[0]


def swapped(rows):
    return lax.all_to_all(rows, "dp", split_axis=0, concat_axis=0, tiled=True)


def exchanged(blocks):
    return [blocks[0]] + [crossed(block, "dp", k) for k, block in enumerate(blocks) if k]


def bits_of(axis):
    return [1 << k for k in reversed(range(lax.axis_size(axis).bit_length() - 1))]


def spread_over_row(piece):
    held = [piece]
    for bit in bits_of("row"):
        held = held + [crossed(part, "row", bit) for part in held]
    return held


def join_body(me_ref, *refs, count):
    part_refs, out_refs = taken(refs, count)
    width = part_refs[0].shape[1]
    for c in range(count):
        spot = spot_of(c, me_ref[0], count.bit_length() - 1)
        value = part_refs[0][...]
        for k in range(1, count):
            value = jnp.where(spot == k, part_refs[k][...], value)
        start = 0
        for ref in out_refs:
            low, high = max(start, c * width), min(start + ref.shape[1], (c + 1) * width)
            if low < high:
                ref[:, low - start : high - start] = value[:, low - c * width : high - c * width]
            start += ref.shape[1]


def join_columns(me, parts, widths):
    rows = parts[0].shape[0]
    vmem = pl.BlockSpec(memory_space=pltpu.VMEM)
    return pl.pallas_call(
        functools.partial(join_body, count=len(parts)),
        name="join_columns",
        in_specs=[pl.BlockSpec(memory_space=pltpu.SMEM)] + [vmem] * len(parts),
        out_specs=[vmem] * len(widths),
        out_shape=[jax.ShapeDtypeStruct((rows, width), BF) for width in widths],
        cost_estimate=cost(2),
    )(me, *parts)


def gathered(shard):
    count = lax.axis_size("dp")
    copies = jnp.broadcast_to(shard[None], (count,) + shard.shape)
    return swapped(copies).reshape(count * shard.shape[0], shard.shape[1])


def side_by_side_body(*refs):
    (*ins, out_ref) = refs
    start = 0
    for ref in ins:
        out_ref[:, start : start + ref.shape[1]] = ref[...]
        start += ref.shape[1]


def copy_body(in_ref, out_ref):
    out_ref[...] = in_ref[...]


def held_back(array, after):
    (copy,) = call_kernel(
        copy_body, "hold", [(array.shape, array.dtype)], [array], micros=1, after=after
    )
    return copy


def crossed(array, axis, bit):
    count = lax.axis_size(axis)
    return lax.ppermute(array, axis, [(i, i ^ bit) for i in range(count)])


def summed(array, axes):
    for axis in axes:
        bit = 1
        while bit < lax.axis_size(axis):
            array = array + crossed(array, axis, bit)
            bit *= 2
    return array


def dense_blocks(grad):
    count = lax.axis_size("dp")
    half = count // 2
    place = lax.axis_index("dp")
    rows = grad.shape[0] // count
    grad = grad.reshape(2, half, rows, grad.shape[1])
    mine, other = place // half, 1 - place // half
    blocks = [
        jnp.concatenate(
            [
                lax.dynamic_slice(
                    grad, (h, (place % half) ^ k, 0, 0), (1, 1, rows, grad.shape[3])
                )[0]
                for h in (mine, other)
            ]
        )
        for k in range(half)
    ]
    return exchanged(blocks)


def dense_spread(part):
    held = spread_over_row(part)
    sums = held
    while len(sums) > 1:
        sums = [plus(left, right) for left, right in zip(sums[::2], sums[1::2])]
    return sums[0].astype(FL), held


def on_device(
    patches,
    unpadded_patch_size,
    patch_expert_index,
    cotangent,
    query_key_value_weight,
    query_projection_bias,
    value_projection_bias,
    log_cosine_scale,
    bias_network_first_weight,
    bias_network_first_bias,
    bias_network_second_weight,
    output_projection_weight,
    output_projection_bias,
    attention_norm_gain,
    attention_norm_bias,
    routing_weight,
    expert_first_weight,
    expert_first_bias,
    expert_second_weight,
    expert_second_bias,
    expert_norm_gain,
    expert_norm_bias,
    patch_merging_weight,
    merging_norm_gain,
    merging_norm_bias,
):
    micro_count, _, band_rows, band_cols, channels = patches.shape
    micros = range(micro_count)
    half_rows = band_rows // 2
    win_count = band_cols // WINDOW_SIDE
    win_area = WINDOW_SIDE * WINDOW_SIDE
    tokens = band_rows * band_cols
    half = tokens // 2
    experts = routing_weight.shape[1]
    dp_size = lax.axis_size("dp")
    local = experts // dp_size
    capacity = (5 * tokens + 4 * experts - 1) // (4 * experts)
    slots = -(-capacity // 16) * 16
    block_rows = 2 * local * slots
    members = dp_size // 2
    row_size = lax.axis_size("row")
    me = lax.axis_index("row").astype(jnp.int32)[None]
    my_place = lax.axis_index("dp").astype(jnp.int32)
    my_place = jnp.stack([my_place // members, my_place % members])
    total_rows = band_rows * lax.axis_size("row")
    row_start = band_rows * lax.axis_index("row")

    wide = 4 * channels + LANES
    shard = jnp.concatenate(
        [query_key_value_weight, output_projection_weight, routing_weight], 1
    )
    parts = -(-wide // (8 * LANES)) * 8 * LANES
    shard = jnp.pad(shard, ((0, 0), (0, parts - shard.shape[1])))
    parts //= row_size
    shard = lax.dynamic_slice(shard, (0, me[0] * parts), (shard.shape[0], parts))
    columns = gathered(shard)
    held = spread_over_row(columns)
    weight_qkv, weight_proj, weight_router = join_columns(
        me, held, [3 * channels, channels, LANES]
    )

    bands = patches.reshape(micro_count, tokens, channels)
    below = passed_along(bands[:, :half], "row", -1)

    zones = [
        mask_operands(
            row_start,
            total_rows,
            band_cols,
            unpadded_patch_size[m, 0, 0],
            unpadded_patch_size[m, 0, 1],
        )
        for m in micros
    ]

    dest_cols, dest_rows, chosen_cols = [], [], []
    for m in micros:
        chosen = patch_expert_index[m].reshape(1, tokens)
        column, dest_col, dest_row = slot_tables(
            chosen, my_place, experts, local, slots, capacity, columns
        )
        chosen_cols.append(column)
        dest_cols.append(dest_col)
        dest_rows.append(dest_row)

    network_first = jnp.concatenate(
        [bias_network_first_weight, bias_network_first_bias[None]], 0
    )
    tile_count = channels // LANES
    bias_shape = ((tile_count, win_area, TILE_HEADS * win_area), FL)
    bias_rows, bias_keys = call_kernel(
        spread_body, "spread_bias", [bias_shape, bias_shape], [network_first, bias_network_second_weight], after=[held[1], dest_rows[-1]]
    )
    hidden = expert_first_weight.shape[-1]
    chunks = hidden // PIECE
    subs = local * chunks // row_size
    first_piece, second_piece = [], []
    for sub in range(subs):
        piece = sub * row_size + me[0]
        at, start = piece // chunks, (piece % chunks) * PIECE
        first_piece.append(
            lax.dynamic_slice(expert_first_weight, (at, 0, start), (1, channels, PIECE))
        )
        second_piece.append(
            lax.dynamic_slice(expert_second_weight, (at, start, 0), (1, PIECE, channels))
        )
    first_got = crossed(held_back(jnp.concatenate(first_piece), [columns]), "dp", members)
    second_got = crossed(held_back(jnp.concatenate(second_piece), [first_got]), "dp", members)
    first_other = spread_over_row(first_got)
    second_other = spread_over_row(second_got)
    expert_bias = jnp.concatenate([expert_first_bias, expert_second_bias], 1)
    expert_bias = jnp.concatenate([expert_bias, crossed(expert_bias, "dp", members)], 0)

    lane = jnp.arange(LANES)
    head_marks = jnp.repeat(
        (lane // HEAD_DIM)[None, :] == jnp.arange(TILE_HEADS)[:, None], win_area, 0
    ).astype(BF)
    block_ones = (
        ((jnp.arange(2 * LANES) % LANES) // HEAD_DIM)[:, None] == (lane // HEAD_DIM)[None, :]
    ).astype(BF)
    scale_lanes = jnp.repeat(jnp.exp(log_cosine_scale), HEAD_DIM)[None, :]
    qbias = query_projection_bias[None, :]
    vbias = value_projection_bias[None, :]
    attn_small = jnp.stack([output_projection_bias, attention_norm_gain, attention_norm_bias])
    moe_small = jnp.stack([expert_norm_gain, expert_norm_bias])
    merge_small = jnp.stack([merging_norm_gain, merging_norm_bias])
    first_bias = expert_bias[:, None, :hidden]
    second_bias = expert_bias[:, None, hidden:]

    grid_scratch = ((channels // LANES, band_rows * (band_cols + 8), LANES), FL)
    win_scratch = ((channels // LANES, tokens, LANES), FL)

    none = [None] * micro_count
    attended, arrived, routed, received = list(none), list(none), list(none), list(none)
    expert_out, returned, merged, back_res = list(none), list(none), list(none), list(none)
    expert_back, back_sent, settled, finished = list(none), list(none), list(none), list(none)
    outputs, input_grads, input_parts = list(none), list(none), list(none)

    forward_after = [[first_got, *dest_rows], []]
    route_after = [[second_got, first_other[1]], []]
    for m in micros:
        attended[m] = call_kernel(
            functools.partial(attend_forward_body, band_cols=band_cols, channels=channels),
            "attend_forward",
            [
                ((half, channels), BF),
                ((half, channels), BF),
                ((tokens, channels), BF),
                ((tokens, 3 * channels), BF),
                ((tokens, 2 * channels), FL),
            ],
            [
                bands[m],
                below[m],
                weight_qkv,
                qbias,
                vbias,
                scale_lanes,
                bias_rows,
                *zones[m],
                head_marks,
                block_ones,
            ],
            [grid_scratch, win_scratch],
            micros=16,
            after=(forward_after[m] if m < 2 else []) + [a[0] for a in attended[:m][-1:]],
        )
        arrived[m] = passed_along(attended[m][1], "row", 1)
    for m in micros:
        routed[m] = call_kernel(
            functools.partial(route_body, experts=experts),
            "route",
            [
                ((tokens, channels), FL),
                ((tokens, channels), BF),
                ((tokens, LANES), FL),
                ((tokens, channels), BF),
            ]
            + [((block_rows, channels), BF)] * members,
            [
                arrived[m],
                attended[m][0],
                bands[m],
                weight_proj,
                attn_small,
                weight_router,
                chosen_cols[m],
                dest_rows[m],
            ],
            micros=12,
            after=[attended[-1][0] if m == 0 else routed[m - 1][2]]
            + (route_after[m] if m < 2 else [])
            + (received[m - 1][1:] if m else []),
        )
        if m == 0:
            shard = held_back(patch_merging_weight, [routed[m][2]])
            weight_merge = lax.all_gather(shard, "dp", axis=0, tiled=True)
        received[m] = exchanged(routed[m][4:])
    for m in micros:
        expert_out[m] = expert_forward(
            me,
            received[m],
            expert_first_weight,
            expert_second_weight,
            first_other,
            second_other,
            first_bias,
            second_bias,
            [routed[-1][2] if m == 0 else expert_out[m - 1][0][0]],
        )
        returned[m] = exchanged(expert_out[m][0])
    for m in micros:
        merged[m] = call_kernel(
            functools.partial(
                merge_body, experts=experts, band_cols=band_cols, members=members
            ),
            "merge",
            [
                ((tokens // 4, 2 * channels), BF),
                ((tokens // 4, 4 * channels), BF),
                ((tokens // 4, 2 * channels), BF),
                ((tokens, channels), FL),
                ((tokens, LANES), BF),
                ((8, 2 * channels), FL),
            ]
            + [((block_rows, channels), BF)] * members,
            [
                *returned[m],
                dest_cols[m],
                dest_rows[m],
                chosen_cols[m],
                routed[m][2],
                routed[m][0],
                moe_small,
                weight_merge,
                merge_small,
                cotangent[m, 0].reshape(tokens // 4, 2 * channels),
            ],
            [
                ((tokens, channels), FL),
                ((tokens, channels), FL),
                ((tokens, LANES), FL),
                ((channels // LANES, tokens, LANES), FL),
                ((tokens, channels), BF),
            ],
            micros=14,
            after=[expert_out[-1][0][0] if m == 0 else merged[m - 1][0]],
        )
        outputs[m] = merged[m][0].reshape(band_rows // 2, band_cols // 2, 2 * channels)
        back_res[m] = exchanged(merged[m][6:])
    for m in micros:
        expert_back[m] = expert_backward(
            me,
            back_res[m],
            expert_first_weight,
            expert_second_weight,
            first_other,
            second_other,
            expert_out[m][2],
            [merged[-1][0] if m == 0 else expert_back[m - 1][2]],
        )
        back_sent[m] = exchanged(expert_back[m][0])

    def settle(m, after):
        return call_kernel(
            functools.partial(settle_body, members=members),
            "settle",
            [
                ((tokens, channels), FL),
                ((tokens, channels), BF),
                ((tokens, channels), BF),
                ((8, channels), FL),
            ],
            [
                *back_sent[m],
                dest_cols[m],
                merged[m][3],
                merged[m][4],
                weight_router,
                routed[m][1],
                routed[m][2],
                attn_small,
                weight_proj,
            ],
            micros=7,
            after=after,
        )

    settled[0] = settle(0, [expert_back[-1][2]])
    in_keep, in_send, _ = expert_weight_grads(
        me, received, [b[1] for b in expert_back], local, row_size, True, [settled[0][3]]
    )
    for m in micros[1:]:
        settled[m] = settle(m, [in_keep])
    grad_merge = merge_weight_grad(
        [b[1] for b in merged], [b[2] for b in merged], channels, [settled[-1][3]]
    )
    out_keep, out_send, grad_eout_bias = expert_weight_grads(
        me, back_res, [b[1] for b in expert_out], local, row_size, False, [grad_merge]
    )

    merge_blocks = dense_blocks(grad_merge)

    state = dict(
        first=dict(keep=in_keep, send=in_send), second=dict(keep=out_keep, send=out_send)
    )
    row_bits = list(reversed(bits_of("row")))
    latest = out_keep

    def transfer(kind):
        at = state[kind]
        step = at.setdefault("step", 0)
        if step < len(row_bits):
            at["got"] = crossed(at["send"], "row", row_bits[step])
        else:
            at["got"] = crossed(at["send"], "dp", members)

    def advance(kind):
        nonlocal latest
        at = state[kind]
        if at["step"] < len(row_bits):
            at["keep"], at["send"] = add_pieces(at["keep"], at["got"], [latest])
            latest = at["send"]
        else:
            at["held"] = spread_over_row(add_halves(at["keep"], at["got"], [latest]))
            latest = at["held"][0]
            return
        at["step"] += 1
        transfer(kind)

    transfer("first")
    transfer("second")
    plan = {
        "start": ["first"],
        (0, 1): ["first", "second"],
        (1, 0): ["first", "second"],
    }
    for _ in range(len(row_bits) - 2):
        plan[(0, 1)] = plan[(0, 1)] + ["first", "second"]

    def advance_at(place):
        nonlocal latest, merge_sums, sum_merge
        if place == (0, 0):
            merge_sums = add_blocks(merge_blocks, [latest])
            latest = merge_sums[0]
        elif place == (0, tile_count - 1):
            mine, other = merge_sums
            latest = add_halves(mine, crossed(other, "dp", members), [latest])
            sum_merge, _ = dense_spread(latest)
        for kind in plan.get(place, ()):
            advance(kind)

    merge_sums = sum_merge = None

    advance_at("start")
    dense_args = []
    for m in micros:
        dense_args += [arrived[m], attended[m][0], settled[m][1], routed[m][3], merged[m][4]]
    grad_proj, grad_router = call_kernel(
        dense_body,
        "dense_weight_grads",
        [((channels, channels), BF), ((channels, LANES), BF)],
        dense_args,
        micros=4,
        after=[latest],
    )
    latest = grad_router

    tile_sums = [None] * tile_count
    tile_smalls = []
    weight_grads = [grad_proj, grad_router]
    for m in micros:
        lifted = passed_along(settled[m][2][:half], "row", -1)
        (back_windows,) = call_kernel(
            functools.partial(window_body, band_cols=band_cols, channels=channels),
            "window_grads",
            [((tokens, channels), BF)],
            [settled[m][2][half:], lifted],
            [grid_scratch, win_scratch],
            micros=3,
            after=[latest],
        )
        latest = back_windows
        win, qkv, inverse = attended[m][2:]
        last = m == micro_count - 1
        grads = []
        for t in range(tile_count):

            def part(array, rows, at):
                return (array, pl.BlockSpec((rows, LANES), lambda i, at=at: (0, at)))

            args = [
                part(back_windows, tokens, t),
                part(qkv, tokens, t),
                part(qkv, tokens, tile_count + t),
                part(qkv, tokens, 2 * tile_count + t),
                part(inverse, tokens, t),
                part(inverse, tokens, tile_count + t),
                part(scale_lanes, 1, t),
                win,
                (
                    bias_keys,
                    pl.BlockSpec((1,) + bias_shape[0][1:], lambda i, t=t: (t, 0, 0)),
                ),
                *zones[m],
                head_marks,
                block_ones,
            ]
            if m:
                args += tile_sums[t]
            dqkv, dweight, dbias, small = call_kernel(
                functools.partial(attend_backward_body, summed_before=m > 0),
                "attend_backward",
                [
                    ((tokens, 3 * LANES), BF),
                    ((channels, 3 * LANES), BF if last else FL),
                    (bias_shape[0][1:], FL),
                    ((8, LANES), FL),
                ],
                args,
                micros=0.5 if last and t else 10,
                after=[latest],
            )
            latest = small
            tile_sums[t] = [dweight, dbias]
            tile_smalls.append(small)
            grads.append(dqkv)
            if last:
                weight_grads.append(dweight)
            advance_at((m, t))
        if last:
            tall = SUM_ROWS + 2 * local * (hidden // channels + 1)
            (sums,) = call_kernel(
                functools.partial(
                    fold_body, tile_count=tile_count, micro_count=micro_count
                ),
                "fold_bias",
                [((-(-tall // 8) * 8, channels), FL)],
                [sums[1] for sums in tile_sums]
                + tile_smalls
                + [part[3] for part in settled]
                + [part[5] for part in merged]
                + [part[2] for part in expert_back]
                + [grad_eout_bias],
                micros=3,
                after=[latest, state["second"]["got"]],
            )
            latest = sums
            advance("second")
            (joined_grads,) = call_kernel(
                side_by_side_body,
                "join_grads",
                [((channels, sum(w.shape[1] for w in weight_grads)), BF)],
                weight_grads,
                micros=2,
                after=[latest],
            )
            latest = joined_grads
            dense = dense_blocks(joined_grads)
        input_parts[m] = call_kernel(
            functools.partial(input_grad_body, band_cols=band_cols, channels=channels),
            "input_grad",
            [((half, channels), FL), ((half, channels), BF)],
            grads + [weight_qkv],
            [grid_scratch, win_scratch],
            micros=5,
            after=[latest],
        )
        latest = input_parts[m][1]
        passed = passed_along(input_parts[m][1], "row", 1).astype(FL)
        input_grads[m] = (
            (settled[m][0] + jnp.concatenate([passed, input_parts[m][0]], 0))
            .astype(BF)
            .reshape(band_rows, band_cols, channels)
        )
    steps = [("row", 1 << k) for k in range(row_size.bit_length() - 1)]
    steps += [("dp", 1 << k) for k in range(dp_size.bit_length() - 1)]
    tail = ["blocks", "first", "part"]
    for k, (axis, bit) in enumerate(steps):
        if axis == "dp" and steps[k - 1][0] == "row":
            sums, biases = sums[:SUM_ROWS], sums[SUM_ROWS:tall]
        sums = latest = add_halves(sums, crossed(sums, axis, bit), [latest], FL, 0.2)
        job = tail.pop(0) if tail else None
        if job == "blocks":
            mine, other = add_blocks(dense, [latest])
            latest = mine
        elif job == "first":
            latest = sum_ein = place_pieces(
                me, state["first"]["held"], local, hidden, True, [latest]
            )
        elif job == "part":
            latest = part = add_halves(mine, crossed(other, "dp", members), [latest], BF, 0.2)
    sum_dense, held = dense_spread(part)
    sum_eout = place_pieces(me, state["second"]["held"], local, hidden, False, [latest])
    sum_proj = sum_dense[:, :channels]
    sum_router = sum_dense[:, channels : channels + experts]
    sum_qkv = sum_dense[:, channels + LANES :].reshape(-1, tile_count, 3, LANES)
    sum_qkv = sum_qkv.swapaxes(1, 2).reshape(-1, 3 * channels)
    in_bias = biases[: 2 * local * chunks].reshape(2 * local, hidden)
    out_bias = biases[2 * local * chunks :]
    other_bias = crossed(
        jnp.concatenate([in_bias[local:], out_bias[local:]], 1), "dp", members
    )
    sum_ein_bias = in_bias[:local] + other_bias[:, :hidden]
    sum_eout_bias = out_bias[:local] + other_bias[:, hidden:]
    grad_first, grad_second = call_kernel(
        bias_network_back_body,
        "bias_network_back",
        [(network_first.shape, FL), (bias_network_second_weight.shape, FL)],
        [sums, network_first, bias_network_second_weight],
        micros=0.2,
    )
    grad_first, grad_first_bias = grad_first[:2], grad_first[2]
    sum_qbias, sum_vbias, sum_scale = (
        sums[ATTN_AT],
        sums[ATTN_AT + 1],
        sums[ATTN_AT + 2, ::HEAD_DIM],
    )
    sum_proj_bias, sum_again, sum_ashift = (sums[SETTLE_AT + k] for k in range(3))
    sum_rgain = sums[MERGE_AT : MERGE_AT + 2].reshape(2 * channels)
    sum_rshift = sums[MERGE_AT + 2 : MERGE_AT + 4].reshape(2 * channels)
    sum_mgain, sum_mshift = sums[MERGE_AT + 4], sums[MERGE_AT + 5]
    return (
        jnp.stack(outputs)[:, None],
        jnp.stack(input_grads)[:, None],
        sum_qkv,
        sum_qbias,
        sum_vbias,
        sum_scale,
        grad_first,
        grad_first_bias,
        grad_second,
        sum_proj,
        sum_proj_bias,
        sum_again,
        sum_ashift,
        sum_router,
        sum_ein,
        sum_ein_bias,
        sum_eout,
        sum_eout_bias,
        sum_mgain,
        sum_mshift,
        sum_merge,
        sum_rgain,
        sum_rshift,
    )


def solution(mesh):
    return jax.shard_map(
        on_device,
        mesh=mesh,
        in_specs=(
            P(None, "dp", "row", None, None),
            P(None, "dp", None),
            P(None, "dp", "row", None, None),
            P(None, "dp", "row", None, None),
            P("dp", None),
            P(),
            P(),
            P(),
            P(),
            P(),
            P(),
            P("dp", None),
            P(),
            P(),
            P(),
            P("dp", None),
            P("dp", None, None),
            P("dp", None),
            P("dp", None, None),
            P("dp", None),
            P(),
            P(),
            P("dp", None),
            P(),
            P(),
        ),
        out_specs=(
            P(None, "dp", "row", None, None),
            P(None, "dp", "row", None, None),
            P("dp", None),
            P(),
            P(),
            P(),
            P(),
            P(),
            P(),
            P("dp", None),
            P(),
            P(),
            P(),
            P("dp", None),
            P("dp", None, None),
            P("dp", None),
            P("dp", None, None),
            P("dp", None),
            P(),
            P(),
            P("dp", None),
            P(),
            P(),
        ),
        check_vma=False,
    )
```
